128 devices in a mesh: dp: 32 (over x, y, z_hi), tensor: 4 (over z_lo, core).
Axes of the slice: x: 4, y: 4, z: 4 (z_hi: 2, z_lo: 2; z = z_hi * 2 + z_lo), core: 2. Of those that a mesh axis runs over, the one named last changes fastest.
Arguments:
- tokens: bfloat16 [16384, 2048], P(('dp', 'tensor')), may hold values from -6 to 6
- attn_gain: bfloat16 [2048], replicated, may hold values from 0.5 to 1.5
- query_weight: bfloat16 [2048, 2048], P(None, 'tensor'), may hold values from -0.125 to 0.125
- key_weight: bfloat16 [2048, 256], P(None, 'tensor'), may hold values from -0.125 to 0.125
- value_weight: bfloat16 [2048, 256], P(None, 'tensor'), may hold values from -0.125 to 0.125
- out_weight: bfloat16 [2048, 2048], P('tensor'), may hold values from -0.5 to 0.5
- mlp_gain: bfloat16 [2048], replicated, may hold values from 0.5 to 1.5
- gate_weight: bfloat16 [2048, 5632], P(None, 'tensor'), may hold values from -0.125 to 0.125
- up_weight: bfloat16 [2048, 5632], P(None, 'tensor'), may hold values from -0.125 to 0.125
- down_weight: bfloat16 [5632, 2048], P('tensor'), may hold values from -0.109375 to 0.109375
- cotangent: bfloat16 [16384, 2048], P(('dp', 'tensor')), may hold values from -24 to 24
- doc_lengths: int32 [128], P('dp'), may hold values from 0 to 512, as said below
Outputs:
- result: bfloat16 [16384, 2048], P(('dp', 'tensor'))
- grad_tokens: bfloat16 [16384, 2048], P(('dp', 'tensor'))
- grad_attn_gain: float32 [2048], replicated
- grad_query: float32 [2048, 2048], P('dp', 'tensor')
- grad_key: float32 [2048, 256], P('dp', 'tensor')
- grad_value: float32 [2048, 256], P('dp', 'tensor')
- grad_out_weight: float32 [2048, 2048], P('tensor', 'dp')
- grad_mlp_gain: float32 [2048], replicated
- grad_gate: float32 [2048, 5632], P('dp', 'tensor')
- grad_up: float32 [2048, 5632], P('dp', 'tensor')
- grad_down: float32 [5632, 2048], P('tensor', 'dp')
The draws below stay inside these ranges and needn't reach their ends.
Inputs may be any that keep to these rules, and one draw needn't show every extreme that they name: `doc_lengths`: each pack's 4 entries sum to 512; entries may be 0. In each pack one document starts within its first 128 tokens and ends after its first 384. In every draw some pack holds a single document.
All inputs are finite; a program needn't handle non-finite values.
Results may differ from the reference program's by a relative error of at most 0.028.
Values may be sent and summed in bfloat16 or wider, within the bound.
No kernel may reach another device: no remote copies, remote signals or barrier semaphores. Data moves between devices by JAX's collectives and lax.ppermute only.
A program may use at most 192 MiB of HBM per device.

```python
import jax
import jax.numpy as jnp
from jax import lax

D = 2048
H = 32
KV = 4
HD = 64
FF = 5632
TOK_DEV = 128
DOCS = 4
GROUP = 512
TOKENS = 16384
NDOCS = 128
N_DP = 32


def draw_doc_lengths(key, part):
    key = jax.random.fold_in(key, 11)
    keys = jax.random.split(key, 4)
    packs = NDOCS // DOCS
    leading = jax.random.randint(keys[0], (packs,), 0, TOK_DEV)
    closing = jax.random.randint(keys[1], (packs,), GROUP - TOK_DEV + 1, GROUP + 1)
    chosen = jax.random.randint(keys[2], (), 0, packs)
    single = jnp.arange(packs) == chosen
    leading = jnp.where(single, 0, leading)
    closing = jnp.where(single, GROUP, closing)
    remain = GROUP - closing
    third = jax.random.randint(keys[3], (packs,), 0, remain + 1)
    table = jnp.stack((leading, closing - leading, third, remain - third), axis=1)
    return table.astype(jnp.int32).reshape(NDOCS)


def with_spikes(drawn, stream_key, source, target, parts, factor):
    def block_of(dim):
        return (jnp.arange(drawn.shape[dim]) // (drawn.shape[dim] // parts)).reshape((-1,) + (1,) * (drawn.ndim - 1 - dim))

    first = jax.random.permutation(stream_key, parts)[block_of(target)]
    second = (block_of(target) + parts // 2) % parts
    return jnp.where((block_of(source) == first) | (block_of(source) == second), factor * drawn, drawn)


def shard_levels(stream_key, dims, shards, low, high):
    level, own = 1.0, jax.random.fold_in(stream_key, 6)
    for dim, blocks in shards:
        steps = jnp.exp(jax.random.uniform(jax.random.fold_in(own, dim), (blocks,), jnp.float32, low / len(shards), high / len(shards)))
        level = level * jnp.repeat(steps, dims[dim] // blocks).reshape([-1 if axis == dim else 1 for axis in range(len(dims))])
    return level


def gaussian(rng, shape, spread, bound, shards=(), kind=jnp.bfloat16):
    level = shard_levels(rng, shape, shards, -0.22, 0.18) if shards else 1.0
    result = jax.random.normal(rng, shape, jnp.float32) * spread * level
    return jnp.minimum(jnp.maximum(result, -bound), bound).astype(kind)


def noise_with(stream_key, dims, width, reach, cuts, heavy, kind=jnp.bfloat16):
    array = width * jax.random.normal(stream_key, dims, jnp.float32)
    if cuts:
        array = array * shard_levels(stream_key, dims, cuts, -0.22, 0.18)
    return jnp.clip(with_spikes(array, jax.random.fold_in(stream_key, 3), *heavy), -reach, reach).astype(kind)


def setup_inputs(seed: int = 0) -> dict:
    splits = jax.random.split(jax.random.key(seed), 13)
    tokens = gaussian(splits[0], (TOKENS, D), 1.0, 6.0, ((0, 128),))
    attn_gain = jnp.clip(1.0 + 0.1 * jax.random.normal(splits[1], (D,), jnp.float32), 0.5, 1.5).astype(jnp.bfloat16)
    query_weight = gaussian(splits[2], (D, H * HD), D ** -0.5, 0.125, ((1, 4),))
    key_weight = gaussian(splits[3], (D, KV * HD), D ** -0.5, 0.125, ((1, 4),))
    value_weight = gaussian(splits[4], (D, KV * HD), D ** -0.5, 0.125, ((1, 4),))
    out_weight = gaussian(splits[5], (H * HD, D), (H * HD // 16) ** -0.5, 0.5, ((0, 4),))
    mlp_gain = jnp.clip(1.0 + 0.1 * jax.random.normal(splits[6], (D,), jnp.float32), 0.5, 1.5).astype(jnp.bfloat16)
    gate_weight = gaussian(splits[7], (D, FF), D ** -0.5, 0.125, ((1, 4),))
    up_weight = gaussian(splits[8], (D, FF), D ** -0.5, 0.125, ((1, 4),))
    down_weight = gaussian(splits[9], (FF, D), (FF // 2) ** -0.5, 0.109375, ((0, 4),))
    cotangent = noise_with(splits[10], (TOKENS, D), 1.0, 24.0, ((0, 128),), (0, 1, 128, 5.5))
    doc_lengths = draw_doc_lengths(jax.random.fold_in(splits[12], 71), 0)
    return dict(tokens=tokens, attn_gain=attn_gain, query_weight=query_weight, key_weight=key_weight, value_weight=value_weight, out_weight=out_weight, mlp_gain=mlp_gain, gate_weight=gate_weight, up_weight=up_weight, down_weight=down_weight, cotangent=cotangent, doc_lengths=doc_lengths)


EPSILON = 1e-05
THETA = 10000.0
MASKED = -1000000000.0

@jax.custom_vjp
def low(v):
    return lax.optimization_barrier(v.astype(jnp.bfloat16)).astype(jnp.float32)

@jax.custom_vjp
def low_back(v):
    return v

def low_keep(v):
    return (low(v), None)

def low_pass(kept, grad):
    return (grad,)

def back_keep(v):
    return (v, None)

def back_low(kept, grad):
    return (low(grad),)
low.defvjp(low_keep, low_pass)
low_back.defvjp(back_keep, back_low)

def highest_dot(left, right):
    return jnp.dot(left, right, precision=lax.Precision.HIGHEST)

def doc_layout(lengths, length_all):
    finish = jnp.cumsum(lengths.astype(jnp.int32)).astype(jnp.int32)
    places = jnp.arange(length_all, dtype=jnp.int32)
    passed = places[:, None] >= finish[None, :]
    segment = lax.optimization_barrier(jnp.sum(passed.astype(jnp.int32), axis=1)).astype(jnp.int32)
    opening = lax.optimization_barrier(jnp.max(jnp.where(passed, finish[None, :], 0), axis=1)).astype(jnp.int32)
    return (segment, (places - opening).astype(jnp.int32))

def rotary_tables(offset, head_size):
    half_size = head_size // 2
    freqs = THETA ** (-(jnp.arange(half_size, dtype=jnp.float32) * 2.0 / head_size))
    angles = offset.astype(jnp.float32)[:, None] * freqs[None, :]
    return (jnp.cos(angles), jnp.sin(angles))

def rotate(values, cosine, sine):
    half_size = values.shape[-1] // 2
    first_half = values[..., :half_size]
    second_half = values[..., half_size:]
    return jnp.concatenate((first_half * cosine - second_half * sine, second_half * cosine + first_half * sine), axis=-1)

def rms_norm(values, gain):
    return values * lax.rsqrt(lax.optimization_barrier(jnp.mean(values * values, axis=-1, keepdims=True)) + EPSILON) * gain

def layer(resid_in, attn_gain, query_weight, key_weight, value_weight, out_weight, mlp_gain, gate_weight, up_weight, down_weight, segment, offset):
    cosine, sine = rotary_tables(offset, HD)
    places = jnp.arange(GROUP, dtype=jnp.int32)
    allowed = (segment[:, None] == segment[None, :]) & (places[:, None] >= places[None, :])
    scale = 1.0 / HD ** 0.5
    seen_one = low(rms_norm(resid_in, attn_gain))
    queries = low(rotate(low_back(highest_dot(seen_one, query_weight)).reshape(GROUP, H, HD).transpose(1, 0, 2), cosine, sine))
    keys_all = low(rotate(low_back(highest_dot(seen_one, key_weight)).reshape(GROUP, KV, HD).transpose(1, 0, 2), cosine, sine))
    values_all = low(low_back(highest_dot(seen_one, value_weight))).reshape(GROUP, KV, HD).transpose(1, 0, 2)
    grouped = queries.reshape(KV, H // KV, GROUP, HD)

    def one_group(items):
        query_group, key_group, value_group = items
        scores = jnp.einsum('hqd,kd->hqk', query_group, key_group, precision=lax.Precision.HIGHEST) * scale
        scores = low_back(jnp.where(allowed, scores, MASKED))
        chances = jax.nn.softmax(scores, axis=-1)
        return jnp.einsum('hqk,kd->hqd', low(chances), value_group, precision=lax.Precision.HIGHEST)
    mixed = lax.map(jax.checkpoint(one_group), (grouped, keys_all, values_all))
    mixed = mixed.reshape(H, GROUP, HD).transpose(1, 0, 2).reshape(GROUP, H * HD)
    mixed = low(low_back(mixed))
    resid_mid = resid_in + low_back(highest_dot(mixed, out_weight))
    seen_two = low(rms_norm(resid_mid, mlp_gain))
    gate_val = low_back(highest_dot(seen_two, gate_weight))
    up_val = low_back(highest_dot(seen_two, up_weight))
    hidden = low(jax.nn.silu(gate_val) * up_val)
    return resid_mid + low_back(highest_dot(hidden, down_weight))

def reference(tokens, attn_gain, query_weight, key_weight, value_weight, out_weight, mlp_gain, gate_weight, up_weight, down_weight, cotangent, doc_lengths):
    weights = tuple((w.astype(jnp.float32) for w in (attn_gain, query_weight, key_weight, value_weight, out_weight, mlp_gain, gate_weight, up_weight, down_weight)))
    packs_in = tokens.astype(jnp.float32).reshape(N_DP, GROUP, D)
    packs_ct = cotangent.astype(jnp.float32).reshape(N_DP, GROUP, D)
    packs_len = doc_lengths.reshape(N_DP, DOCS)

    def step(totals, items):
        pack_in, pack_ct, pack_len = items
        segment, offset = doc_layout(pack_len, GROUP)

        def run(resid_in, *params):
            return layer(resid_in, *params, segment, offset)
        output, pull = jax.vjp(run, pack_in, *weights)
        grads = pull(pack_ct)
        totals = tuple((a + b for a, b in zip(totals, grads[1:])))
        return (totals, (output.astype(jnp.bfloat16), grads[0].astype(jnp.bfloat16)))
    start_totals = tuple((jnp.zeros_like(w) for w in weights))
    totals, (outputs, grad_ins) = lax.scan(step, start_totals, (packs_in, packs_ct, packs_len))
    return (outputs.reshape(TOKENS, D), grad_ins.reshape(TOKENS, D), totals[0], totals[1], totals[2], totals[3], totals[4], totals[5], totals[6], totals[7], totals[8])
```

```python
import math

import jax
import jax.numpy as jnp
from jax import lax
from jax.sharding import PartitionSpec as P

HD = 64
EPSILON = 1e-05
THETA = 10000.0
MASKED = -1000000000.0
BF = jnp.bfloat16
F32 = jnp.float32


def dp_perm(xor_x, xor_y, xor_z):
    return [(d, d ^ (xor_x * 8 + xor_y * 2 + xor_z)) for d in range(32)]


def tensor_perm(xor):
    return [(t, t ^ xor) for t in range(4)]


def over_core(values):
    return lax.ppermute(values, "tensor", tensor_perm(1))


def over_z(values):
    return lax.ppermute(values, "tensor", tensor_perm(2))


def over_x(values, xor):
    return lax.ppermute(values, "dp", dp_perm(xor, 0, 0))


def over_y(values, xor):
    return lax.ppermute(values, "dp", dp_perm(0, xor, 0))


def over_z_hi(values):
    return lax.ppermute(values, "dp", dp_perm(0, 0, 1))


def gather_rows(block):
    pair = jnp.concatenate((block, over_z(block)), axis=0)
    return jnp.concatenate((pair, over_core(pair)), axis=0)


def chip_sum(part):
    half = part.shape[0] // 2
    return part[:half].astype(F32) + over_core(part[half:].astype(BF)).astype(F32)


def scatter_rows(part):
    chip = chip_sum(part)
    quarter = chip.shape[0] // 2
    return chip[:quarter] + over_z(chip[quarter:].astype(BF)).astype(F32)


def sum_rows(part):
    chip = chip_sum(part)
    quarter = chip.shape[0] // 2
    low = chip.astype(BF)
    return chip + over_z(jnp.concatenate((low[quarter:], low[:quarter]), axis=0)).astype(F32)


def relative_columns(values, place_x, place_y):
    pieces = []
    for jx in range(4):
        for jy in range(4):
            start = ((place_x ^ jx) * 4 + (place_y ^ jy)) * 128
            pieces.append(lax.dynamic_slice_in_dim(values, start, 128, axis=1))
    return jnp.concatenate(pieces, axis=1)


def add_low(left, right):
    return (left.astype(F32) + right.astype(F32)).astype(BF)


def reduce_axis(part, axis, mirror, send):
    def pick(values, *js):
        return jnp.concatenate([lax.slice_in_dim(values, j, j + 1, axis=axis) for j in js], axis=axis)

    first, second = (1, 3) if mirror == 0 else (3, 1)
    kept = add_low(pick(part, 0, second), send(pick(part, first, 2), first))
    return add_low(pick(kept, 0)if False else lax.slice_in_dim(kept, 0, 1, axis=axis), send(lax.slice_in_dim(kept, 1, 2, axis=axis), second))


def reduce_dp(grad, place_z):
    width = grad.shape[1]
    cube = grad.reshape(4, 4, 4, 32, width)
    done = []
    for number in range(4):
        part = cube[:, :, number]
        mirror = number % 2
        if number < 2:
            part = reduce_axis(part, 0, mirror, over_x)
            part = reduce_axis(part, 1, mirror, over_y)
        else:
            part = reduce_axis(part, 1, mirror, over_y)
            part = reduce_axis(part, 0, mirror, over_x)
        done.append(part.reshape(32, width))
    whole = jnp.concatenate(done, axis=0)
    give = lax.dynamic_slice_in_dim(whole, (1 - place_z) * 64, 64, axis=0)
    keep = lax.dynamic_slice_in_dim(whole, place_z * 64, 64, axis=0)
    return keep.astype(F32) + over_z_hi(give).astype(F32)


def sum_all(values):
    for xor in (1, 3):
        values = values + over_x(values, xor)
    for xor in (1, 3):
        values = values + over_y(values, xor)
    values = values + over_z_hi(values)
    values = values + over_z(values)
    return values + over_core(values)


def rotary_tables(offset, head_size):
    half_size = head_size // 2
    freqs = THETA ** (-(jnp.arange(half_size, dtype=F32) * 2.0 / head_size))
    angles = offset.astype(F32)[:, None] * freqs[None, :]
    return (jnp.cos(angles), jnp.sin(angles))


def rotate(values, cosine, sine):
    half_size = values.shape[-1] // 2
    first_half = values[..., :half_size]
    second_half = values[..., half_size:]
    return jnp.concatenate(
        (first_half * cosine - second_half * sine, second_half * cosine + first_half * sine),
        axis=-1,
    )


def dot(left, right):
    return jnp.dot(left, right, preferred_element_type=F32)


def dot_t(left, right):
    return lax.dot_general(left, right, (((0,), (0,)), ((), ())), preferred_element_type=F32)


def dot_rt(left, right):
    return lax.dot_general(left, right, (((1,), (1,)), ((), ())), preferred_element_type=F32)


def per_device(
    tokens,
    attn_gain,
    query_weight,
    key_weight,
    value_weight,
    out_weight,
    mlp_gain,
    gate_weight,
    up_weight,
    down_weight,
    cotangent,
    doc_lengths,
):
    rows = tokens.shape[0]
    place_dp = lax.axis_index("dp")
    place_t = lax.axis_index("tensor")
    place_x, place_y, place_z = place_dp // 8, (place_dp // 2) % 4, place_dp % 2
    heads = query_weight.shape[1] // HD
    q_width = heads * HD
    scale = 1.0 / math.sqrt(HD)
    places = jnp.concatenate(
        [(place_t ^ j) * rows + jnp.arange(rows, dtype=jnp.int32) for j in (0, 2, 1, 3)]
    )
    finish = jnp.cumsum(doc_lengths)
    passed = places[:, None] >= finish[None, :]
    segment = jnp.sum(passed.astype(jnp.int32), axis=1)
    offset = places - jnp.max(jnp.where(passed, finish[None, :], 0), axis=1)
    allowed = (segment[:, None] == segment[None, :]) & (places[:, None] >= places[None, :])
    cosine, sine = rotary_tables(offset, HD)
    gain_one = attn_gain.astype(F32)
    gain_two = mlp_gain.astype(F32)

    seen = gather_rows(tokens).astype(F32)
    cot_all = gather_rows(cotangent)
    inverse_one = lax.rsqrt(jnp.mean(seen * seen, axis=-1, keepdims=True) + EPSILON)
    normed_one = seen * inverse_one
    h1 = (normed_one * gain_one).astype(BF)
    joined = jnp.concatenate((query_weight, key_weight, value_weight), axis=1)
    project = dot(h1, joined)

    def split_heads(values):
        return values.reshape(values.shape[0], -1, HD).transpose(1, 0, 2)

    def join_heads(values):
        return values.transpose(1, 0, 2).reshape(values.shape[1], -1)

    queries = rotate(split_heads(project[:, :q_width]), cosine, sine).astype(BF)
    keys = rotate(project[:, q_width : q_width + HD], cosine, sine).astype(BF)
    vals = project[:, q_width + HD :].astype(BF)

    scores = jnp.where(
        allowed, jnp.einsum("hqd,kd->hqk", queries, keys, preferred_element_type=F32) * scale, MASKED
    )
    highest = jnp.max(scores, axis=-1, keepdims=True)
    raised = jnp.exp(scores - highest)
    totals = jnp.sum(raised, axis=-1, keepdims=True)
    log_totals = highest + jnp.log(totals)
    chances = (raised / totals).astype(BF)
    mixed = jnp.einsum("hqk,kd->hqd", chances, vals, preferred_element_type=F32)
    heads_out = join_heads(mixed).astype(BF)

    mid = seen[: 2 * rows] + sum_rows(dot(heads_out, out_weight))
    inverse_two = lax.rsqrt(jnp.mean(mid * mid, axis=-1, keepdims=True) + EPSILON)
    normed_two = mid * inverse_two
    h2_half = (normed_two * gain_two).astype(BF)
    h2 = jnp.concatenate((h2_half, over_core(h2_half)), axis=0)

    gate = dot(h2, gate_weight)
    up = dot(h2, up_weight)
    sig = jax.nn.sigmoid(gate)
    active = gate * sig
    hidden = (active * up).astype(BF)
    grad_hidden = dot_rt(cot_all, down_weight)
    grad_gate_val = (grad_hidden * up * sig * (1.0 + gate * (1.0 - sig))).astype(BF)
    grad_up_val = (grad_hidden * active).astype(BF)
    grad_both = jnp.concatenate((grad_gate_val, grad_up_val), axis=1)

    grad_h2 = sum_rows(dot_rt(grad_gate_val, gate_weight) + dot_rt(grad_up_val, up_weight))

    cot_rel = relative_columns(cot_all, place_x, place_y)
    h2_rel = relative_columns(h2, place_x, place_y)
    h1_rel = relative_columns(h1, place_x, place_y)
    out_down = reduce_dp(dot_t(cot_rel, hidden).astype(BF), place_z)
    out_both = reduce_dp(dot_t(h2_rel, grad_both).astype(BF), place_z)

    result = (mid[:rows] + scatter_rows(dot(hidden, down_weight))).astype(BF)

    scaled = grad_h2 * gain_two
    grad_mid = cot_all[: 2 * rows].astype(F32) + inverse_two * (
        scaled - normed_two * jnp.mean(scaled * normed_two, axis=-1, keepdims=True)
    )
    grad_gain_two = jnp.sum(grad_h2[:rows] * normed_two[:rows], axis=0)
    grad_mid_low = grad_mid.astype(BF)
    grad_mid_all = jnp.concatenate((grad_mid_low, over_core(grad_mid_low)), axis=0)

    mid_rel = relative_columns(grad_mid_all, place_x, place_y)
    grad_out = dot_t(mid_rel, heads_out).astype(BF)
    grad_heads = split_heads(dot_rt(grad_mid_all, out_weight).astype(BF))

    chances = jnp.exp(scores - log_totals)
    grad_chances = jnp.einsum("hqd,kd->hqk", grad_heads, vals, preferred_element_type=F32)
    centre = jnp.sum(chances * grad_chances, axis=-1, keepdims=True)
    grad_scores = (chances * (grad_chances - centre)).astype(BF)
    grad_queries = jnp.einsum("hqk,kd->hqd", grad_scores, keys, preferred_element_type=F32) * scale
    grad_keys = jnp.einsum("hqk,hqd->kd", grad_scores, queries, preferred_element_type=F32) * scale
    grad_vals = jnp.einsum("hqk,hqd->kd", chances.astype(BF), grad_heads, preferred_element_type=F32)
    grad_project = jnp.concatenate(
        (
            join_heads(rotate(grad_queries, cosine, -sine)).astype(BF),
            rotate(grad_keys, cosine, -sine).astype(BF),
            grad_vals.astype(BF),
        ),
        axis=1,
    )
    grad_h1_part = dot_rt(grad_project, joined)
    grad_joined = dot_t(h1_rel, grad_project).astype(BF)
    out_attn = reduce_dp(jnp.concatenate((grad_joined, grad_out), axis=1), place_z)
    grad_gain_one = jnp.sum(grad_h1_part * normed_one, axis=0)
    grad_gains = sum_all(
        jnp.stack((grad_gain_one, grad_gain_two))
    )
    grad_h1 = scatter_rows(grad_h1_part)
    own_norm, own_inverse = normed_one[:rows], inverse_one[:rows]
    scaled = grad_h1 * gain_one
    grad_tokens = grad_mid[:rows] + own_inverse * (
        scaled - own_norm * jnp.mean(scaled * own_norm, axis=-1, keepdims=True)
    )
    ff = gate_weight.shape[1]
    return (
        result,
        grad_tokens.astype(BF),
        grad_gains[0],
        out_attn[:, :q_width],
        out_attn[:, q_width : q_width + HD],
        out_attn[:, q_width + HD : q_width + 2 * HD],
        out_attn[:, q_width + 2 * HD :].T,
        grad_gains[1],
        out_both[:, :ff],
        out_both[:, ff:],
        out_down.T,
    )


def solution(mesh):
    in_specs = (
        P(("dp", "tensor"), None),
        P(),
        P(None, "tensor"),
        P(None, "tensor"),
        P(None, "tensor"),
        P("tensor", None),
        P(),
        P(None, "tensor"),
        P(None, "tensor"),
        P("tensor", None),
        P(("dp", "tensor"), None),
        P("dp"),
    )
    out_specs = (
        P(("dp", "tensor"), None),
        P(("dp", "tensor"), None),
        P(),
        P("dp", "tensor"),
        P("dp", "tensor"),
        P("dp", "tensor"),
        P("tensor", "dp"),
        P(),
        P("dp", "tensor"),
        P("dp", "tensor"),
        P("tensor", "dp"),
    )
    return jax.shard_map(
        per_device, mesh=mesh, in_specs=in_specs, out_specs=out_specs, check_vma=False
    )
```

```python
import functools
import math

import jax
import jax.numpy as jnp
from jax import lax
from jax.experimental import pallas as pl
from jax.experimental.pallas import tpu as pltpu
from jax.sharding import PartitionSpec as P

HD = 64
EPSILON = 1e-05
THETA = 10000.0
MASKED = -1000000000.0
BF = jnp.bfloat16
F32 = jnp.float32
VMEM_LIMIT = 56 * 1024 * 1024


def dot(left, right):
    return jnp.dot(left, right, preferred_element_type=F32)


def dot_t(left, right):
    return lax.dot_general(left, right, (((0,), (0,)), ((), ())), preferred_element_type=F32)


def dot_rt(left, right):
    return lax.dot_general(left, right, (((1,), (1,)), ((), ())), preferred_element_type=F32)


def vmem():
    return pl.BlockSpec(memory_space=pltpu.VMEM)


def smem():
    return pl.BlockSpec(memory_space=pltpu.SMEM)


def hbm():
    return pl.BlockSpec(memory_space=pl.ANY)


def params(**more):
    return pltpu.CompilerParams(vmem_limit_bytes=VMEM_LIMIT, **more)


def swap_halves(values):
    width = values.shape[1]
    lane = lax.broadcasted_iota(jnp.int32, values.shape, 1)
    return jnp.where(
        lane % HD < HD // 2,
        pltpu.roll(values, width - HD // 2, 1),
        pltpu.roll(values, HD // 2, 1),
    )


def wide(table, width):
    return jnp.concatenate([table] * (width // table.shape[1]), axis=1) if width > table.shape[1] else table[:, :width]


def places_of(place_t, ends, rows, shape, axis):
    index = lax.broadcasted_iota(jnp.int32, shape, axis)
    block = index // rows
    order = jnp.where(block == 0, 0, jnp.where(block == 1, 2, jnp.where(block == 2, 1, 3)))
    places = (place_t ^ order) * rows + index % rows
    opening = jnp.zeros(shape, jnp.int32)
    for end in ends:
        opening = jnp.maximum(opening, jnp.where(places >= end, end, 0))
    return places, opening


def doc_ends(place_ref, count):
    ends, total = [], jnp.int32(0)
    for i in range(count):
        total = total + place_ref[1 + i]
        ends.append(total)
    return ends


def attention_kernel(
    docs, place_ref, own, zpart, cpart, diag, gain, wq, wk, wv, wo, cos, sin,
    h1_ref, qkv_ref, o_ref, lse_ref, high_ref, low_ref, bias_ref,
):
    rows = own.shape[0]
    every = 4 * rows
    half = 2 * rows
    q_width = wq.shape[1]
    heads = q_width // HD
    gain_row = gain[...].astype(F32)
    for number, block in enumerate((own, zpart, cpart, diag)):
        values = block[...].astype(F32)
        inverse = lax.rsqrt(jnp.mean(values * values, axis=-1, keepdims=True) + EPSILON)
        h1_ref[number * rows : (number + 1) * rows, :] = (values * inverse * gain_row).astype(BF)
    h1 = h1_ref[...]
    joined = jnp.concatenate((wk[...], wv[...]), axis=1)
    table_c, table_s = cos[...], sin[...]

    def rope(values):
        width = values.shape[1]
        return values * wide(table_c, width) + swap_halves(values) * wide(table_s, width)

    scale = 1.0 / math.sqrt(HD)
    kv = dot(h1, joined)
    lane = lax.broadcasted_iota(jnp.int32, kv.shape, 1)
    qkv_ref[:, q_width:] = jnp.where(lane < HD, rope(kv), kv).astype(BF)
    qkv_ref[:, :q_width] = rope(dot(h1, wq[...])).astype(BF)

    ends = doc_ends(place_ref, docs)
    places_q, opening_q = places_of(place_ref[0], ends, rows, (every, 1), 0)
    places_k, _ = places_of(place_ref[0], ends, rows, (1, every), 1)
    bias_ref[...] = jnp.where((places_k <= places_q) & (places_k >= opening_q), 0.0, MASKED)

    keys = qkv_ref[:, q_width : q_width + HD]
    kv_low = qkv_ref[:, q_width:]
    lane = lax.broadcasted_iota(jnp.int32, kv_low.shape, 1)
    ones_vals = jnp.where(lane < HD, jnp.ones_like(kv_low), kv_low)
    lse_lane = lax.broadcasted_iota(jnp.int32, (every, 128), 1)
    lse = jnp.zeros((every, 128), F32)
    for head in range(heads):
        query = qkv_ref[:, head * HD : (head + 1) * HD]
        scores = dot_rt(query, keys) * scale + bias_ref[...]
        highest = jnp.max(scores, axis=-1, keepdims=True)
        raised = jnp.exp(scores - highest)
        mixed = dot(raised.astype(BF), ones_vals)
        totals = mixed[:, :1]
        o_ref[:, head * HD : (head + 1) * HD] = (mixed[:, HD:] / totals).astype(BF)
        lse = jnp.where(lse_lane == head, highest + jnp.log(totals), lse)
    lse_ref[...] = lse.T[:heads, :]
    high_ref[...] = dot(o_ref[:half, :], wo[...])
    low_ref[...] = dot(o_ref[half:, :], wo[...]).astype(BF)


def attention(place_docs, blocks, gain, wq, wk, wv, wo, cos, sin):
    rows, width = blocks[0].shape
    every = rows * 4
    q_width = wq.shape[1]
    heads = q_width // HD
    shapes = (
        jax.ShapeDtypeStruct((every, width), BF),
        jax.ShapeDtypeStruct((every, q_width + 2 * HD), BF),
        jax.ShapeDtypeStruct((every, q_width), BF),
        jax.ShapeDtypeStruct((heads, every), F32),
        jax.ShapeDtypeStruct((2 * rows, width), F32),
        jax.ShapeDtypeStruct((2 * rows, width), BF),
    )
    return pl.pallas_call(
        functools.partial(attention_kernel, place_docs.shape[0] - 1),
        out_shape=shapes,
        in_specs=[smem()] + [vmem()] * 11,
        out_specs=[vmem()] * 6,
        scratch_shapes=[pltpu.VMEM((every, every), F32)],
        compiler_params=params(),
        name="attention",
        cost_estimate=pl.CostEstimate(flops=3 * 10**9, bytes_accessed=16 * 10**6, transcendentals=2**21),
    )(place_docs, *blocks, gain.reshape(1, -1), wq, wk, wv, wo, cos, sin)


def mlp_kernel(tile, h2_a, h2_b, dh_ref, wg_hbm, wu_hbm, hid_ref, dgate_ref, dup_ref, wg, wu, h2, sems):
    half = h2_a.shape[0]
    units = wg.shape[1]
    spans = [(s, min(tile, units - s)) for s in range(0, units, tile)]

    def copies(i):
        s, n = spans[i]
        return (
            pltpu.make_async_copy(wg_hbm.at[:, pl.ds(s, n)], wg.at[:, pl.ds(s, n)], sems.at[0, i]),
            pltpu.make_async_copy(wu_hbm.at[:, pl.ds(s, n)], wu.at[:, pl.ds(s, n)], sems.at[1, i]),
        )

    for i in range(len(spans)):
        for copy in copies(i):
            copy.start()
    h2[:half, :] = h2_a[...]
    h2[half:, :] = h2_b[...]
    for i, (s, n) in enumerate(spans):
        for copy in copies(i):
            copy.wait()
        gate = dot(h2[...], wg[:, s : s + n])
        up = dot(h2[...], wu[:, s : s + n])
        dh = dh_ref[:, s : s + n]
        sig = jax.nn.sigmoid(gate)
        active = gate * sig
        hid_ref[:, s : s + n] = (active * up).astype(BF)
        dgate_ref[:, s : s + n] = (dh * up * (sig + active * (1.0 - sig))).astype(BF)
        dup_ref[:, s : s + n] = (dh * active).astype(BF)


def mlp(h2_halves, dh, wg, wu, tile=256):
    half, width = h2_halves[0].shape
    every = 2 * half
    units = wg.shape[1]
    count = -(-units // tile)
    return pl.pallas_call(
        functools.partial(mlp_kernel, tile),
        out_shape=[jax.ShapeDtypeStruct((every, units), BF)] * 3,
        in_specs=[vmem()] * 3 + [hbm()] * 2,
        out_specs=[vmem()] * 3,
        scratch_shapes=[
            pltpu.VMEM((width, units), BF),
            pltpu.VMEM((width, units), BF),
            pltpu.VMEM((every, width), BF),
            pltpu.SemaphoreType.DMA((2, count)),
        ],
        compiler_params=params(),
        name="mlp",
        cost_estimate=pl.CostEstimate(flops=6 * 10**9, bytes_accessed=20 * 10**6, transcendentals=2**20),
    )(*h2_halves, dh, wg, wu)


def mlp_back_kernel(dgate, dup, wg, wu, h2_a, h2_b, high_ref, low_ref, gain_ref):
    half = h2_a.shape[0]
    part = dot_rt(dgate[...], wg[...]) + dot_rt(dup[...], wu[...])
    high_ref[...] = part[:half]
    low_ref[...] = part[half:].astype(BF)
    gain_ref[...] = jnp.sum(part[:half] * h2_a[...].astype(F32), axis=0, keepdims=True) + jnp.sum(
        part[half:] * h2_b[...].astype(F32), axis=0, keepdims=True
    )


def mlp_back(dgate, dup, wg, wu, h2_halves, step=256):
    half, width = h2_halves[0].shape
    units = wg.shape[1]
    every = 2 * half
    whole = pl.BlockSpec((every, units), lambda i: (0, 0))
    weight = pl.BlockSpec((step, units), lambda i: (i, 0))
    side = pl.BlockSpec((half, step), lambda i: (0, i))
    return pl.pallas_call(
        mlp_back_kernel,
        out_shape=(
            jax.ShapeDtypeStruct((half, width), F32),
            jax.ShapeDtypeStruct((half, width), BF),
            jax.ShapeDtypeStruct((1, width), F32),
        ),
        grid=(width // step,),
        in_specs=[whole, whole, weight, weight, side, side],
        out_specs=(side, side, pl.BlockSpec((1, step), lambda i: (0, i))),
        compiler_params=params(),
        name="mlp_back",
        cost_estimate=pl.CostEstimate(flops=6 * 10**9, bytes_accessed=20 * 10**6, transcendentals=0),
    )(dgate, dup, wg, wu, *h2_halves)


SEND = ((1, 2), (3, 2))
KEEP = ((0, 3), (0, 1))
ORDER = (1, 2, 3, 0)


def gradient_kernel(counts, tile, place_ref, *refs):
    outs = refs[sum(counts) + len(counts) :]
    jx = (pl.program_id(0) + 1) % 4
    place_x, place_y = place_ref[0], place_ref[1]
    sends = [(jx == SEND[part][0]) | (jx == SEND[part][1]) for part in range(2)]
    first = at = 0
    for count in counts:
        lefts, right = refs[first : first + count], refs[first + count]
        first += count + 1
        columns = []
        for jy in range(4):
            start = pl.multiple_of(((place_x ^ jx) * 4 + (place_y ^ jy)) * 128, 128)
            columns.append(jnp.concatenate([left[:, pl.ds(start, 128)] for left in lefts], axis=0))
        left = jnp.concatenate(columns, axis=1)
        width = right.shape[1]
        for s in range(0, width, tile):
            n = min(tile, width - s)
            cube = dot_t(left, right[:, s : s + n]).astype(BF).reshape(4, 4, 32, n)
            for b in range(n // 128):
                block = at + s // 128 + b
                piece = cube[:, :, :, b * 128 : (b + 1) * 128]
                for part in range(2):
                    @pl.when(sends[part])
                    def _():
                        outs[2 * part][0, :, block] = piece[:, part]

                    @pl.when(jnp.logical_not(sends[part]))
                    def _():
                        outs[2 * part + 1][0, :, block] = piece[:, part]

                    for slot in range(2):
                        outs[4 + 2 * part][slot, 0, block] = piece[SEND[part][slot], 2 + part]
                        outs[5 + 2 * part][slot, 0, block] = piece[KEEP[part][slot], 2 + part]
        at += width // 128


def gradient(place_xy, groups, tile=512):
    width = sum(right.shape[1] for _, right in groups)
    every = groups[0][1].shape[0]
    operands = [ref for lefts, right in groups for ref in (*lefts, right)]
    blocks = width // 128
    out = jax.ShapeDtypeStruct((2, 4, blocks, 32, 128), BF)

    def slots(seq):
        def index(step, place):
            value = jnp.where(step == 0, seq[0], jnp.where(step == 1, seq[1], jnp.where(step == 2, seq[2], seq[3])))
            return (value, 0, 0, 0, 0)

        return pl.BlockSpec((1, 4, blocks, 32, 128), index)

    along = pl.BlockSpec((2, 1, blocks, 32, 128), lambda step, place: (0, (step + 1) % 4, 0, 0, 0))
    grid_spec = pltpu.PrefetchScalarGridSpec(
        num_scalar_prefetch=1,
        grid=(4,),
        in_specs=[pl.BlockSpec(operand.shape, lambda step, place: (0, 0)) for operand in operands],
        out_specs=[
            slots((0, 1, 1, 1)),
            slots((1, 1, 1, 0)),
            slots((1, 1, 0, 0)),
            slots((1, 1, 1, 0)),
            along, along, along, along,
        ],
    )
    return pl.pallas_call(
        functools.partial(gradient_kernel, [len(lefts) for lefts, _ in groups], tile),
        out_shape=[out] * 8,
        grid_spec=grid_spec,
        compiler_params=params(),
        name="gradient",
        cost_estimate=pl.CostEstimate(
            flops=2 * every * 2048 * width,
            bytes_accessed=sum(2 * operand.size for operand in operands) + 4096 * width,
            transcendentals=0,
        ),
    )(place_xy, *operands)


def attention_back_kernel(
    docs, place_ref, mid_a, mid_b, qkv, lse_ref, h1, wq, wk, wv, wo, cos, sin,
    dqkv_ref, high_ref, low_ref, gain_ref, bias_ref, do_ref, kv_t_ref,
):
    half = mid_a.shape[0]
    rows, every = half // 2, 2 * half
    q_width = wq.shape[1]
    heads = q_width // HD
    width = wq.shape[0]
    scale = 1.0 / math.sqrt(HD)
    mid = jnp.concatenate((mid_a[...], mid_b[...]), axis=0)
    do_ref[...] = dot_rt(mid, wo[...]).astype(BF)
    ends = doc_ends(place_ref, docs)
    places_q, opening_q = places_of(place_ref[0], ends, rows, (1, every), 1)
    places_k, _ = places_of(place_ref[0], ends, rows, (every, 1), 0)
    bias_ref[...] = jnp.where((places_k <= places_q) & (places_k >= opening_q), 0.0, MASKED)
    keys = qkv[:, q_width : q_width + HD]
    vals = qkv[:, q_width + HD : q_width + 2 * HD]
    dk = jnp.zeros((every, HD), F32)
    dv = jnp.zeros((every, HD), F32)
    table_c, table_s = cos[...], sin[...]

    def unrope(values):
        wide_now = values.shape[1]
        return values * wide(table_c, wide_now) - swap_halves(values) * wide(table_s, wide_now)

    for pair in range(heads // 2):
        dqs = []
        for head in (2 * pair, 2 * pair + 1):
            cut = slice(head * HD, (head + 1) * HD)
            query = qkv[:, cut]
            grad_o = do_ref[:, cut]
            scores = dot_rt(keys, query) * scale + bias_ref[...]
            chances = jnp.exp(scores - lse_ref[head : head + 1, :])
            grad_chances = dot_rt(vals, grad_o)
            centre = jnp.sum(chances * grad_chances, axis=0, keepdims=True)
            grad_scores = (chances * (grad_chances - centre)).astype(BF)
            dv = dv + dot(chances.astype(BF), grad_o)
            dk = dk + dot(grad_scores, query)
            dqs.append(dot_t(grad_scores, keys))
        dq = jnp.concatenate(dqs, axis=1) * scale
        dqkv_ref[:, pair * 2 * HD : (pair + 1) * 2 * HD] = unrope(dq).astype(BF)
    both = jnp.concatenate((dk * scale, dv), axis=1)
    lane = lax.broadcasted_iota(jnp.int32, both.shape, 1)
    dqkv_ref[:, q_width:] = jnp.where(lane < HD, unrope(both), both).astype(BF)
    kv_t_ref[:, :HD] = wk[...]
    kv_t_ref[:, HD:] = wv[...]
    step = 512
    for s in range(0, width, step):
        part = dot_rt(dqkv_ref[:, :q_width], wq[s : s + step, :]) + dot_rt(dqkv_ref[:, q_width:], kv_t_ref[s : s + step, :])
        high_ref[:, s : s + step] = part[:half]
        low_ref[:, s : s + step] = part[half:].astype(BF)
        gain_ref[:, s : s + step] = jnp.sum(part * h1[:, s : s + step].astype(F32), axis=0, keepdims=True)


def attention_back(place_docs, mids, qkv, lse, h1, wq, wk, wv, wo, cos, sin):
    half, width = mids[0].shape
    every = 2 * half
    q_width = wq.shape[1]
    shapes = (
        jax.ShapeDtypeStruct((every, q_width + 2 * HD), BF),
        jax.ShapeDtypeStruct((half, width), F32),
        jax.ShapeDtypeStruct((half, width), BF),
        jax.ShapeDtypeStruct((1, width), F32),
    )
    return pl.pallas_call(
        functools.partial(attention_back_kernel, place_docs.shape[0] - 1),
        out_shape=shapes,
        in_specs=[smem()] + [vmem()] * 11,
        out_specs=[vmem()] * 4,
        scratch_shapes=[
            pltpu.VMEM((every, every), F32),
            pltpu.VMEM((every, q_width), BF),
            pltpu.VMEM((width, 2 * HD), BF),
        ],
        compiler_params=params(),
        name="attention_back",
        cost_estimate=pl.CostEstimate(flops=5 * 10**9, bytes_accessed=16 * 10**6, transcendentals=2**21),
    )(place_docs, *mids, qkv, lse, h1, wq, wk, wv, wo, cos, sin)


def rotary_tables(offset):
    half_size = HD // 2
    freqs = THETA ** (-(jnp.arange(half_size, dtype=F32) * 2.0 / HD))
    angles = offset.astype(F32)[:, None] * freqs[None, :]
    cosine, sine = jnp.cos(angles), jnp.sin(angles)
    return jnp.concatenate((cosine,) * 4, axis=1), jnp.concatenate((-sine, sine) * 2, axis=1)


def over_core(values):
    return lax.ppermute(values, "tensor", [(t, t ^ 1) for t in range(4)])


def over_z(values):
    return lax.ppermute(values, "tensor", [(t, t ^ 2) for t in range(4)])


def over_x(values, xor):
    return lax.ppermute(values, "dp", [(d, d ^ (xor * 8)) for d in range(32)])


def over_y(values, xor):
    return lax.ppermute(values, "dp", [(d, d ^ (xor * 2)) for d in range(32)])


def over_z_hi(values):
    return lax.ppermute(values, "dp", [(d, d ^ 1) for d in range(32)])


def after(value, *others):
    return lax.optimization_barrier((value, *others))[0] if others else value


def add(*terms):
    total = terms[0].astype(F32)
    for term in terms[1:]:
        total = total + term.astype(F32)
    return total


def norm(values):
    inverse = lax.rsqrt(jnp.mean(values * values, axis=-1, keepdims=True) + EPSILON)
    return values * inverse, inverse


def norm_back(normed, inverse, gain, grads):
    scaled = grads * gain
    return inverse * (scaled - normed * jnp.mean(scaled * normed, axis=-1, keepdims=True))


def swapped(chip):
    rows = chip.shape[0] // 2
    low = chip.astype(BF)
    return jnp.concatenate((low[rows:], low[:rows]), axis=0)


LINKS = ((over_x, 1), (over_x, 3), (over_y, 1), (over_y, 3))
ROUTES = ((0, 1, 2, 3), (1, 0, 3, 2), (2, 3, 0, 1), (3, 2, 1, 0))


class Reduction:
    def __init__(self, arrays):
        self.blocks = arrays[0].shape[2]
        self.kept = [arrays[2 * part + 1] for part in range(4)]
        self.next = [arrays[2 * part].reshape(-1, 32, 128) for part in range(4)]
        self.got = [None] * 4
        self.done = [None] * 4

    def take(self, part, step, got):
        first, second = ((1, 3), (3, 1))[part % 2]
        kept = self.kept[part]
        if step == 0:
            got = got.reshape(2, 4, self.blocks, 32, 128)
            self.got[part] = got
            self.next[part] = add(kept[1], got[1]).astype(BF).reshape(-1, 32, 128)
        elif step == 1:
            got = got.reshape(4, self.blocks, 32, 128)
            chunk = add(kept[0], self.got[part][0], got).astype(BF)
            self.kept[part] = chunk
            low = min(first, 2)
            self.next[part] = chunk[low : low + 2].reshape(-1, 32, 128)
        elif step == 2:
            got = got.reshape(2, self.blocks, 32, 128)
            near, far = (got[0], got[1]) if first == 1 else (got[1], got[0])
            self.got[part] = near
            self.next[part] = add(kept[second], far).astype(BF)
        else:
            self.done[part] = add(kept[0], self.got[part], got).astype(BF)

    def ends(self, place_z):
        low = jnp.stack(self.done[:2])
        high = jnp.stack(self.done[2:])
        return jnp.where(place_z == 0, high, low), jnp.where(place_z == 0, low, high)


def stage(jobs, before=()):
    arrived = []
    for number, (hop, xor) in enumerate(LINKS):
        takers = [(r, part, step) for r, step in jobs for part in range(4) if ROUTES[part][step] == number]
        pieces = [r.next[part] for r, part, _ in takers]
        operand = jnp.concatenate(pieces, axis=0) if len(pieces) > 1 else pieces[0]
        got = hop(after(operand, *([before[number]] if before else [])), xor)
        arrived.append(got)
        at = 0
        for (r, part, step), piece in zip(takers, pieces):
            r.take(part, step, got[at : at + piece.shape[0]])
            at += piece.shape[0]
    return arrived


def finish(reductions, place_z, before=()):
    ends = [r.ends(place_z) for r in reductions]
    gives = jnp.concatenate([give.reshape(-1, 32, 128) for give, _ in ends], axis=0)
    got = over_z_hi(after(gives, *before))
    at, rows = 0, []
    for r, (_, keep) in zip(reductions, ends):
        total = add(keep, got[at : at + 2 * r.blocks].reshape(keep.shape))
        at += 2 * r.blocks
        rows.append(total.transpose(0, 2, 1, 3).reshape(64, r.blocks * 128))
    return rows


def sum_all(values, before):
    values = after(values, *before)
    for xor in (1, 3):
        values = values + over_x(values, xor)
    for xor in (1, 3):
        values = values + over_y(values, xor)
    values = values + over_z_hi(values)
    values = values + over_z(values)
    return values + over_core(values)


def per_device(
    tokens,
    attn_gain,
    query_weight,
    key_weight,
    value_weight,
    out_weight,
    mlp_gain,
    gate_weight,
    up_weight,
    down_weight,
    cotangent,
    doc_lengths,
):
    rows = tokens.shape[0]
    place_dp = lax.axis_index("dp")
    place_t = lax.axis_index("tensor")
    place_z = place_dp % 2
    place_xy = jnp.stack((place_dp // 8, (place_dp // 2) % 4))
    q_width = query_weight.shape[1]
    gain_one, gain_two = attn_gain.astype(F32), mlp_gain.astype(F32)

    across = over_z(tokens)
    token_blocks = (tokens, across, over_core(tokens), over_core(across))
    places = jnp.concatenate(
        [(place_t ^ j) * rows + jnp.arange(rows, dtype=jnp.int32) for j in (0, 2, 1, 3)]
    )
    opening, ending = jnp.zeros_like(places), jnp.int32(0)
    for number in range(doc_lengths.shape[0]):
        ending = ending + doc_lengths[number]
        opening = jnp.maximum(opening, jnp.where(places >= ending, ending, 0))
    cos, sin = rotary_tables(places - opening)
    place_docs = jnp.concatenate((place_t[None], doc_lengths))

    cot_across = over_z(after(cotangent, across))
    h1, qkv, heads_out, lse, high, low = attention(
        place_docs, token_blocks, attn_gain, query_weight, key_weight, value_weight, out_weight, cos, sin
    )
    cot_pair = jnp.concatenate((cotangent, after(cot_across, low)), axis=0)
    received = over_core(low)
    chip = add(high, received)
    z_sums = over_z(swapped(chip))
    cot_halves = (cot_pair, over_core(after(cot_pair, received)))
    grad_hidden = dot_rt(after(cot_halves[0], chip), down_weight), dot_rt(after(cot_halves[1], chip), down_weight)
    grad_hidden = jnp.concatenate(grad_hidden, axis=0)
    z_sums = after(z_sums, grad_hidden)
    mid = jnp.concatenate((tokens, across), axis=0).astype(F32) + add(chip, z_sums)
    normed_two, inverse_two = norm(mid)
    h2 = (normed_two * gain_two).astype(BF)
    h2 = (h2, over_core(h2))
    hidden, grad_gate_val, grad_up_val = mlp(h2, grad_hidden, gate_weight, up_weight)

    down = gradient(place_xy, [(cot_halves, hidden)])
    links = stage([(down_sum := Reduction(down), 0)])
    high, low, gain_two_part = mlp_back(
        after(grad_gate_val, down[0]), grad_up_val, gate_weight, up_weight, h2
    )
    received = over_core(low)
    both = gradient(place_xy, [(h2, after(grad_gate_val, low)), (h2, grad_up_val)])
    chip = add(high, after(received, both[0]))
    z_sums = over_z(swapped(chip))
    links = stage([(both_sum := Reduction(both), 0)], links)

    mlp_part = dot(after(hidden, chip), down_weight).astype(BF)
    z_sums = after(z_sums, mlp_part)
    grad_mid = cot_pair.astype(F32) + norm_back(normed_two, inverse_two, gain_two, add(chip, z_sums))
    mid_low = grad_mid.astype(BF)
    mid_low = (mid_low, over_core(mid_low))

    jobs = [down_sum, both_sum]
    links = stage([(r, 1) for r in jobs], links)
    grad_project, high, low, gain_one_part = attention_back(
        place_docs, mid_low, qkv, lse, h1, query_weight, key_weight, value_weight, out_weight, cos, sin
    )
    received = over_core(low)
    attn = gradient(place_xy, [((h1,), after(grad_project, low)), (mid_low, heads_out)])
    attn_sum = Reduction(attn)
    chip = add(high, after(received, attn[0]))
    grad_h1 = chip[:rows] + over_z(chip[rows:].astype(BF)).astype(F32)

    links = stage([(r, 2) for r in jobs], links)
    links = stage([(r, 3) for r in jobs] + [(attn_sum, 0)], links)
    links = stage([(attn_sum, 1)], links)
    out_down, out_both = finish(jobs, place_z, [grad_h1])
    links = stage([(attn_sum, 2)], links)
    links = stage([(attn_sum, 3)], links)
    (out_attn,) = finish([attn_sum], place_z, [out_down])

    received = over_core(after(mlp_part[2 * rows :], grad_h1))
    chip = add(mlp_part[: 2 * rows], received)
    result = (mid[:rows] + chip[:rows] + over_z(after(chip[rows:].astype(BF), out_down)).astype(F32)).astype(BF)

    grad_gains = sum_all(jnp.concatenate((gain_one_part, gain_two_part), axis=0), [received])
    normed, inverse = norm(tokens.astype(F32))
    grad_tokens = grad_mid[:rows] + norm_back(normed, inverse, gain_one, grad_h1)
    ff = gate_weight.shape[1]
    return (
        result,
        grad_tokens.astype(BF),
        grad_gains[0] / gain_one,
        out_attn[:, :q_width],
        out_attn[:, q_width : q_width + HD],
        out_attn[:, q_width + HD : q_width + 2 * HD],
        out_attn[:, q_width + 2 * HD :].T,
        grad_gains[1] / gain_two,
        out_both[:, :ff],
        out_both[:, ff:],
        out_down.T,
    )


def solution(mesh):
    in_specs = (
        P(("dp", "tensor"), None),
        P(),
        P(None, "tensor"),
        P(None, "tensor"),
        P(None, "tensor"),
        P("tensor", None),
        P(),
        P(None, "tensor"),
        P(None, "tensor"),
        P("tensor", None),
        P(("dp", "tensor"), None),
        P("dp"),
    )
    out_specs = (
        P(("dp", "tensor"), None),
        P(("dp", "tensor"), None),
        P(),
        P("dp", "tensor"),
        P("dp", "tensor"),
        P("dp", "tensor"),
        P("tensor", "dp"),
        P(),
        P("dp", "tensor"),
        P("dp", "tensor"),
        P("tensor", "dp"),
    )
    return jax.shard_map(
        per_device, mesh=mesh, in_specs=in_specs, out_specs=out_specs, check_vma=False
    )
```

```python
import functools
import math

import jax
import jax.numpy as jnp
from jax import lax
from jax.experimental import pallas as pl
from jax.experimental.pallas import tpu as pltpu
from jax.sharding import PartitionSpec as P

HD = 64
EPSILON = 1e-05
THETA = 10000.0
MASKED = -1000000000.0
BF = jnp.bfloat16
F32 = jnp.float32
VMEM_LIMIT = 24 * 1024 * 1024


def cost(time):
    return pl.CostEstimate(flops=int(time * 1e9), bytes_accessed=1024, transcendentals=0)


def dot(left, right):
    return jnp.dot(left, right, preferred_element_type=F32)


def dot_t(left, right):
    return lax.dot_general(left, right, (((0,), (0,)), ((), ())), preferred_element_type=F32)


def dot_rt(left, right):
    return lax.dot_general(left, right, (((1,), (1,)), ((), ())), preferred_element_type=F32)


def vmem():
    return pl.BlockSpec(memory_space=pltpu.VMEM)


def smem():
    return pl.BlockSpec(memory_space=pltpu.SMEM)


def hbm():
    return pl.BlockSpec(memory_space=pl.ANY)


def params(**more):
    return pltpu.CompilerParams(vmem_limit_bytes=VMEM_LIMIT, **more)


def swap_halves(values):
    width = values.shape[1]
    lane = lax.broadcasted_iota(jnp.int32, values.shape, 1)
    return jnp.where(
        lane % HD < HD // 2,
        pltpu.roll(values, width - HD // 2, 1),
        pltpu.roll(values, HD // 2, 1),
    )


def wide(table, width):
    return jnp.concatenate([table] * (width // table.shape[1]), axis=1) if width > table.shape[1] else table[:, :width]


def places_of(place_t, ends, rows, shape, axis):
    index = lax.broadcasted_iota(jnp.int32, shape, axis)
    block = index // rows
    order = jnp.where(block == 0, 0, jnp.where(block == 1, 2, jnp.where(block == 2, 1, 3)))
    places = (place_t ^ order) * rows + index % rows
    opening = jnp.zeros(shape, jnp.int32)
    for end in ends:
        opening = jnp.maximum(opening, jnp.where(places >= end, end, 0))
    return places, opening


def doc_ends(place_ref, count):
    ends, total = [], jnp.int32(0)
    for i in range(count):
        total = total + place_ref[1 + i]
        ends.append(total)
    return ends


def attention_kernel(
    docs, place_ref, own, zpart, cpart, diag, gain, wq, wk, wv, wo, cos, sin,
    h1_ref, qkv_ref, o_ref, lse_ref, high_ref, low_ref, bias_ref,
):
    rows = own.shape[0]
    every = 4 * rows
    half = 2 * rows
    q_width = wq.shape[1]
    heads = q_width // HD
    gain_row = gain[...].astype(F32)
    for number, block in enumerate((own, zpart, cpart, diag)):
        values = block[...].astype(F32)
        inverse = lax.rsqrt(jnp.mean(values * values, axis=-1, keepdims=True) + EPSILON)
        h1_ref[number * rows : (number + 1) * rows, :] = (values * inverse * gain_row).astype(BF)
    h1 = h1_ref[...]
    joined = jnp.concatenate((wk[...], wv[...]), axis=0)
    table_c, table_s = cos[...], sin[...]

    def rope(values):
        width = values.shape[1]
        return values * wide(table_c, width) + swap_halves(values) * wide(table_s, width)

    scale = 1.0 / math.sqrt(HD)
    kv = dot_rt(h1, joined)
    lane = lax.broadcasted_iota(jnp.int32, kv.shape, 1)
    qkv_ref[:, q_width:] = jnp.where(lane < HD, rope(kv), kv).astype(BF)
    qkv_ref[:, :q_width] = rope(dot(h1, wq[...])).astype(BF)

    ends = doc_ends(place_ref, docs)
    places_q, opening_q = places_of(place_ref[0], ends, rows, (every, 1), 0)
    places_k, _ = places_of(place_ref[0], ends, rows, (1, every), 1)
    bias_ref[...] = jnp.where((places_k <= places_q) & (places_k >= opening_q), 0.0, MASKED)

    keys = qkv_ref[:, q_width : q_width + HD]
    kv_low = qkv_ref[:, q_width:]
    lane = lax.broadcasted_iota(jnp.int32, kv_low.shape, 1)
    ones_vals = jnp.where(lane < HD, jnp.ones_like(kv_low), kv_low)
    lse_lane = lax.broadcasted_iota(jnp.int32, (every, 128), 1)
    lse = jnp.zeros((every, 128), F32)
    for head in range(heads):
        query = qkv_ref[:, head * HD : (head + 1) * HD]
        scores = dot_rt(query, keys) * scale + bias_ref[...]
        highest = jnp.max(scores, axis=-1, keepdims=True)
        raised = jnp.exp(scores - highest)
        mixed = dot(raised.astype(BF), ones_vals)
        totals = mixed[:, :1]
        o_ref[:, head * HD : (head + 1) * HD] = (mixed[:, HD:] / totals).astype(BF)
        lse = jnp.where(lse_lane == head, highest + jnp.log(totals), lse)
    lse_ref[...] = lse.T[:heads, :]
    high_ref[...] = dot(o_ref[:half, :], wo[...])
    low_ref[...] = dot(o_ref[half:, :], wo[...]).astype(BF)


def attention(place_docs, blocks, gain, wq, wk, wv, wo, cos, sin):
    rows, width = blocks[0].shape
    every = rows * 4
    q_width = wq.shape[1]
    heads = q_width // HD
    shapes = (
        jax.ShapeDtypeStruct((every, width), BF),
        jax.ShapeDtypeStruct((every, q_width + 2 * HD), BF),
        jax.ShapeDtypeStruct((every, q_width), BF),
        jax.ShapeDtypeStruct((heads, every), F32),
        jax.ShapeDtypeStruct((2 * rows, width), F32),
        jax.ShapeDtypeStruct((2 * rows, width), BF),
    )
    return pl.pallas_call(
        functools.partial(attention_kernel, place_docs.shape[0] - 1),
        out_shape=shapes,
        in_specs=[smem()] + [vmem()] * 11,
        out_specs=[vmem()] * 6,
        scratch_shapes=[pltpu.VMEM((every, every), F32)],
        compiler_params=params(),
        name="attention",
        cost_estimate=cost(11),
    )(place_docs, *blocks, gain, wq, wk.T, wv.T, wo, cos, sin)


SEND = ((1, 2), (3, 2))
KEEP = ((0, 3), (0, 1))


def gradient_body(place_ref, groups, outs, tile=512):
    place_x, place_y = place_ref[0], place_ref[1]
    at = 0
    for lefts, right, begin, width in groups:
        for jx in range(4):
            columns = []
            for jy in range(4):
                start = pl.multiple_of(((place_x ^ jx) * 4 + (place_y ^ jy)) * 128, 128)
                columns.append(jnp.concatenate([left[:, pl.ds(start, 128)] for left in lefts], axis=0))
            left = jnp.concatenate(columns, axis=1)
            for s in range(0, width, tile):
                n = min(tile, width - s)
                cube = dot_t(left, right[:, begin + s : begin + s + n]).astype(BF).reshape(4, 4, 32, n)
                for b in range(n // 128):
                    block = at + s // 128 + b
                    piece = cube[:, :, :, b * 128 : (b + 1) * 128]
                    for part in range(2):
                        for number, slots in enumerate((SEND[part], KEEP[part])):
                            if jx in slots:
                                outs[2 * part + number][slots.index(jx), :, block] = piece[:, part]
                            for slot in range(2):
                                outs[4 + 2 * part + number][slot, jx, block] = piece[slots[slot], 2 + part]
        at += width // 128


def gradient_shapes(width):
    return [jax.ShapeDtypeStruct((2, 4, width // 128, 32, 128), BF)] * 8


def mlp_kernel(tile, split, place_ref, h2_a, h2_b, dh_a, dh_b, wg, wu, cot_a, cot_b, hid_ref, dgate_ref, dup_ref, *outs):
    units = wg.shape[1]
    h2 = jnp.concatenate((h2_a[...], h2_b[...]), axis=0)
    for s in range(0, units, tile):
        cut = slice(s, min(s + tile, units))
        gate = dot(h2, wg[:, cut])
        up = dot(h2, wu[:, cut])
        dh = jnp.concatenate((dh_a[:, cut], dh_b[:, cut]), axis=0)
        sig = jax.nn.sigmoid(gate)
        active = gate * sig
        hid_ref[:, cut] = (active * up).astype(BF)
        dgate_ref[:, cut] = (dh * up * (sig + active * (1.0 - sig))).astype(BF)
        dup_ref[:, cut] = (dh * active).astype(BF)
    gradient_body(place_ref, [((cot_a, cot_b), hid_ref, 0, units), ((h2_a, h2_b), dgate_ref, 0, split)], outs)


def mlp(place_xy, h2_halves, dh, wg, wu, cot_halves, split, tile=512):
    half, width = h2_halves[0].shape
    every = 2 * half
    units = wg.shape[1]
    got = pl.pallas_call(
        functools.partial(mlp_kernel, tile, split),
        out_shape=[jax.ShapeDtypeStruct((every, units), BF)] * 3 + gradient_shapes(units + split),
        in_specs=[smem()] + [vmem()] * 8,
        out_specs=[vmem()] * 11,
        compiler_params=params(),
        name="mlp",
        cost_estimate=cost(18),
    )(place_xy, *h2_halves, *dh, wg, wu, *cot_halves)
    return (*got[:3], got[3:])


def mlp_back_kernel(step, split, place_ref, dgate, dup, wg, wu, h2_a, h2_b, high_ref, low_ref, gain_ref, *outs):
    half, width = h2_a.shape
    for s in range(0, width, step):
        cut = slice(s, s + step)
        part = dot_rt(dgate[...], wg[cut, :]) + dot_rt(dup[...], wu[cut, :])
        high_ref[:, cut] = part[:half]
        low_ref[:, cut] = part[half:].astype(BF)
        gain_ref[:, cut] = jnp.sum(part[:half] * h2_a[:, cut].astype(F32), axis=0, keepdims=True) + jnp.sum(
            part[half:] * h2_b[:, cut].astype(F32), axis=0, keepdims=True
        )
    units = dup.shape[1]
    lefts = (h2_a, h2_b)
    gradient_body(place_ref, [(lefts, dgate, split, units - split), (lefts, dup, 0, units)], outs)


def mlp_back(place_xy, dgate, dup, wg, wu, h2_halves, split, step=512):
    half, width = h2_halves[0].shape
    got = pl.pallas_call(
        functools.partial(mlp_back_kernel, step, split),
        out_shape=[
            jax.ShapeDtypeStruct((half, width), F32),
            jax.ShapeDtypeStruct((half, width), BF),
            jax.ShapeDtypeStruct((1, width), F32),
        ]
        + gradient_shapes(2 * wg.shape[1] - split),
        in_specs=[smem()] + [vmem()] * 6,
        out_specs=[vmem()] * 11,
        compiler_params=params(),
        name="mlp_back",
        cost_estimate=cost(14),
    )(place_xy, dgate, dup, wg, wu, *h2_halves)
    return (*got[:3], got[3:])


def combine_kernel(sums, *refs):
    out = refs[-1]
    at = 0
    for count, terms in sums:
        total = None
        for number, start in terms:
            term = refs[number][start : start + count].astype(F32)
            total = term if total is None else total + term
        out[at : at + count] = total.astype(out.dtype)
        at += count


def combine(sums):
    arrays, plan = [], []
    for terms in sums:
        listed = []
        for array, start, count in terms:
            known = [i for i, a in enumerate(arrays) if a is array]
            if not known:
                arrays.append(array)
            listed.append((known[0] if known else len(arrays) - 1, start))
        plan.append((terms[0][2], listed))
    total = sum(count for count, _ in plan)
    return pl.pallas_call(
        functools.partial(combine_kernel, plan),
        out_shape=jax.ShapeDtypeStruct((total, 32, 128), BF),
        in_specs=[vmem()] * len(arrays),
        out_specs=vmem(),
        compiler_params=params(),
        name="combine",
        cost_estimate=cost(0.5),
    )(*arrays)


def ends_kernel(sums, extra, place_ref, *refs):
    give, keep = refs[-2:]
    at = 0
    if extra:
        total = None
        for number, start in extra:
            term = refs[number][start : start + 1].astype(F32)
            total = term if total is None else total + term
        give[0:1] = total.astype(BF)
        keep[0:1] = total.astype(BF).astype(F32)
        at = 1
    for parts in sums:
        count = parts[0][0]
        totals = []
        for _, terms in parts:
            total = None
            for number, start in terms:
                term = refs[number][start : start + count].astype(F32)
                total = term if total is None else total + term
            totals.append(total)
        for half in range(2):
            cut = slice(at, at + count)
            give[cut] = jnp.where(place_ref[0] == 0, totals[2 + half], totals[half]).astype(BF)
            keep[cut] = jnp.where(place_ref[0] == 0, totals[half], totals[2 + half])
            at += count


def ends(place_z, sums, extra=()):
    arrays, plan = [], []
    for parts in sums:
        planned = []
        for terms in parts:
            listed = []
            for array, start, count in terms:
                known = [i for i, a in enumerate(arrays) if a is array]
                if not known:
                    arrays.append(array)
                listed.append((known[0] if known else len(arrays) - 1, start))
            planned.append((terms[0][2], listed))
        plan.append(planned)
    arrays += [array for array, _, _ in extra]
    more = [(len(arrays) - len(extra) + i, start) for i, (_, start, _) in enumerate(extra)]
    total = sum(2 * parts[0][0] for parts in plan) + bool(extra)
    return pl.pallas_call(
        functools.partial(ends_kernel, plan, more),
        out_shape=(jax.ShapeDtypeStruct((total, 32, 128), BF), jax.ShapeDtypeStruct((total, 32, 128), F32)),
        in_specs=[smem()] + [vmem()] * len(arrays),
        out_specs=[vmem()] * 2,
        compiler_params=params(),
        name="ends",
        cost_estimate=cost(1),
    )(place_z, *arrays)


def attention_back_kernel(
    docs, place_ref, place_xy, mid_a, mid_b, qkv, lse_ref, h1, o_ref, wq, wk, wv, wo, cos, sin, gain_two, *refs
):
    dqkv_ref, high_ref, low_ref, gains, *outs, bias_ref, do_ref = refs
    half = mid_a.shape[0]
    rows, every = half // 2, 2 * half
    q_width = wq.shape[1]
    heads = q_width // HD
    width = wq.shape[0]
    scale = 1.0 / math.sqrt(HD)
    mid = jnp.concatenate((mid_a[...], mid_b[...]), axis=0)
    do_ref[...] = dot_rt(mid, wo[...]).astype(BF)
    ends = doc_ends(place_ref, docs)
    places_q, opening_q = places_of(place_ref[0], ends, rows, (1, every), 1)
    places_k, _ = places_of(place_ref[0], ends, rows, (every, 1), 0)
    bias_ref[...] = jnp.where((places_k <= places_q) & (places_k >= opening_q), 0.0, MASKED)
    keys = qkv[:, q_width : q_width + HD]
    vals = qkv[:, q_width + HD : q_width + 2 * HD]
    dk = jnp.zeros((every, HD), F32)
    dv = jnp.zeros((every, HD), F32)
    table_c, table_s = cos[...], sin[...]

    def unrope(values):
        wide_now = values.shape[1]
        return values * wide(table_c, wide_now) - swap_halves(values) * wide(table_s, wide_now)

    for pair in range(heads // 2):
        dqs = []
        for head in (2 * pair, 2 * pair + 1):
            cut = slice(head * HD, (head + 1) * HD)
            query = qkv[:, cut]
            grad_o = do_ref[:, cut]
            scores = dot_rt(keys, query) * scale + bias_ref[...]
            chances = jnp.exp(scores - lse_ref[head : head + 1, :])
            grad_chances = dot_rt(vals, grad_o)
            centre = jnp.sum(chances * grad_chances, axis=0, keepdims=True)
            grad_scores = (chances * (grad_chances - centre)).astype(BF)
            dv = dv + dot(chances.astype(BF), grad_o)
            dk = dk + dot(grad_scores, query)
            dqs.append(dot_t(grad_scores, keys))
        dq = jnp.concatenate(dqs, axis=1) * scale
        dqkv_ref[:, pair * 2 * HD : (pair + 1) * 2 * HD] = unrope(dq).astype(BF)
    both = jnp.concatenate((dk * scale, dv), axis=1)
    lane = lax.broadcasted_iota(jnp.int32, both.shape, 1)
    dqkv_ref[:, q_width:] = jnp.where(lane < HD, unrope(both), both).astype(BF)
    joined = jnp.concatenate((wk[...], wv[...]), axis=0)
    step = 512
    for s in range(0, width, step):
        part = dot_rt(dqkv_ref[:, :q_width], wq[s : s + step, :]) + dot(dqkv_ref[:, q_width:], joined[:, s : s + step])
        high_ref[:, s : s + step] = part[:half]
        low_ref[:, s : s + step] = part[half:].astype(BF)
        gain_one = jnp.sum(part * h1[:, s : s + step].astype(F32), axis=0, keepdims=True)
        for lane in range(0, step, 128):
            row = (s + lane) // 128
            gains[0, row : row + 1, :] = gain_one[:, lane : lane + 128]
            gains[0, width // 128 + row : width // 128 + row + 1, :] = gain_two[:, s + lane : s + lane + 128]
    gradient_body(place_xy, [((h1,), dqkv_ref, 0, q_width + 2 * HD), ((mid_a, mid_b), o_ref, 0, q_width)], outs)


def attention_back(place_docs, place_xy, mids, qkv, lse, h1, o, wq, wk, wv, wo, cos, sin, gain_two_part):
    half, width = mids[0].shape
    every = 2 * half
    q_width = wq.shape[1]
    got = pl.pallas_call(
        functools.partial(attention_back_kernel, place_docs.shape[0] - 1),
        out_shape=[
            jax.ShapeDtypeStruct((every, q_width + 2 * HD), BF),
            jax.ShapeDtypeStruct((half, width), F32),
            jax.ShapeDtypeStruct((half, width), BF),
            jax.ShapeDtypeStruct((1, width // 64, 128), F32),
        ]
        + gradient_shapes(2 * q_width + 2 * HD),
        in_specs=[smem()] * 2 + [vmem()] * 13,
        out_specs=[vmem()] * 12,
        scratch_shapes=[
            pltpu.VMEM((every, every), F32),
            pltpu.VMEM((every, q_width), BF),
        ],
        compiler_params=params(),
        name="attention_back",
        cost_estimate=cost(19),
    )(place_docs, place_xy, *mids, qkv, lse, h1, o, wq, wk.T, wv.T, wo, cos, sin, gain_two_part)
    return (*got[1:4], got[4:])


def rotary_tables(offset):
    half_size = HD // 2
    freqs = THETA ** (-(jnp.arange(half_size, dtype=F32) * 2.0 / HD))
    angles = offset.astype(F32)[:, None] * freqs[None, :]
    cosine, sine = jnp.cos(angles), jnp.sin(angles)
    return jnp.concatenate((cosine,) * 4, axis=1), jnp.concatenate((-sine, sine) * 2, axis=1)


def over_core(values):
    return lax.ppermute(values, "tensor", [(t, t ^ 1) for t in range(4)])


def over_z(values):
    return lax.ppermute(values, "tensor", [(t, t ^ 2) for t in range(4)])


def over_x(values, xor):
    return lax.ppermute(values, "dp", [(d, d ^ (xor * 8)) for d in range(32)])


def over_y(values, xor):
    return lax.ppermute(values, "dp", [(d, d ^ (xor * 2)) for d in range(32)])


def over_z_hi(values):
    return lax.ppermute(values, "dp", [(d, d ^ 1) for d in range(32)])


def after(value, *others):
    return lax.optimization_barrier((value, *others))[0] if others else value


def add(*terms):
    total = terms[0].astype(F32)
    for term in terms[1:]:
        total = total + term.astype(F32)
    return total


def norm(values):
    inverse = lax.rsqrt(jnp.mean(values * values, axis=-1, keepdims=True) + EPSILON)
    return values * inverse, inverse


def norm_back(normed, inverse, gain, grads):
    scaled = grads * gain
    return inverse * (scaled - normed * jnp.mean(scaled * normed, axis=-1, keepdims=True))


LINKS = ((over_x, 1), (over_x, 3), (over_y, 1), (over_y, 3))
ROUTES = ((0, 1, 2, 3), (1, 0, 3, 2), (2, 3, 0, 1), (3, 2, 1, 0))


class Reduction:
    def __init__(self, arrays):
        self.blocks = arrays[0].shape[2]
        self.sends = [arrays[2 * part].reshape(-1, 32, 128) for part in range(4)]
        kept = [arrays[2 * part + 1].reshape(-1, 32, 128) for part in range(4)]
        self.held = [[(array, 0)] for array in kept]

    def terms(self, part, row, rows=1):
        n = self.blocks
        return [(array, start + row * n, rows * n) for array, start in self.held[part][:3]]

    def sum(self, part, step):
        n = self.blocks
        first, second = ((1, 3), (3, 1))[part % 2]
        held = self.held[part]
        if step == 1:
            return [(array, start + 4 * n, 4 * n) for array, start in held]
        if step == 2:
            return self.terms(part, min(first, 2), 2)
        near, far = (0, 1) if first == 1 else (1, 0)
        array, start = held[3]
        if step == 3:
            return self.terms(part, second) + [(array, start + far * n, n)]
        last, at = held[4]
        return self.terms(part, 0) + [(array, start + near * n, n), (last, at, n)]


class Gains:
    def __init__(self, block):
        self.held = [(block, 0)]

    def terms(self):
        return [(array, start, 1) for array, start in self.held]

    def exchange(self, hop, before):
        sent = sum(array[start : start + 1].astype(F32) for array, start in self.held).astype(BF)
        self.held = [(sent, 0), (hop(after(sent, *before)), 0)]


def takers(jobs, link):
    return [(r, part, step) for r, step in jobs for part in range(4) if ROUTES[part][step] == link]


def prepare(jobs, gains=None, gains_link=None):
    operands = []
    for link in range(4):
        taken = takers(jobs, link)
        if taken[0][2] == 0:
            operands.append(taken[0][0].sends[taken[0][1]])
            continue
        sums = [r.sum(part, step) for r, part, step in taken]
        operands.append(combine(sums + ([gains.terms()] if link == gains_link else [])))
    return operands


def send(jobs, operands, before=None, anchor=None, gains=None, gains_link=None):
    arrived = []
    for link, (operand, (hop, xor)) in enumerate(zip(operands, LINKS)):
        got = hop(after(operand, before[link]) if before else operand, xor)
        arrived.append(got)
        if anchor is not None:
            got = after(got, anchor)
        at = 0
        for r, part, step in takers(jobs, link):
            r.held[part].append((got, at))
            at += r.blocks * (8, 4, 2, 1)[step]
        if link == gains_link:
            gains.held = [(operand, at), (got, at)]
    return arrived


def stage(jobs, before=None, **more):
    return send(jobs, prepare(jobs, **more), before, **more)


def finish(reductions, place_z, before=(), gains=None, anchor=None):
    gives, keeps = ends(
        place_z,
        [[r.sum(part, 4) for part in range(4)] for r in reductions],
        gains.terms() if gains else (),
    )
    got = over_z_hi(after(gives, *before))
    if anchor is not None:
        got = after(got, anchor)
    at, rows = 0, []
    if gains:
        at = 1
        rows.append(add(keeps[0], got[0]))
    for r in reductions:
        cut = slice(at, at + 2 * r.blocks)
        total = add(keeps[cut], got[cut]).reshape(2, r.blocks, 32, 128)
        at += 2 * r.blocks
        rows.append(total.transpose(0, 2, 1, 3).reshape(64, r.blocks * 128))
    return rows


def chip_sums(high, low, *wait):
    rows = low.shape[0] // 2
    got = after(over_core(low), *wait)
    return add(high[:rows], got[:rows]), add(high[rows:], got[rows:])


def per_device(
    tokens,
    attn_gain,
    query_weight,
    key_weight,
    value_weight,
    out_weight,
    mlp_gain,
    gate_weight,
    up_weight,
    down_weight,
    cotangent,
    doc_lengths,
):
    rows = tokens.shape[0]
    place_dp = lax.axis_index("dp")
    place_t = lax.axis_index("tensor")
    place_z = place_dp % 2
    place_xy = jnp.stack((place_dp // 8, (place_dp // 2) % 4))
    q_width = query_weight.shape[1]
    gain_one, gain_two = attn_gain.astype(F32), mlp_gain.astype(F32)

    across = over_z(tokens)
    places = jnp.concatenate(
        [(place_t ^ j) * rows + jnp.arange(rows, dtype=jnp.int32) for j in (0, 2, 1, 3)]
    )
    opening, ending = jnp.zeros_like(places), jnp.int32(0)
    for number in range(doc_lengths.shape[0]):
        ending = ending + doc_lengths[number]
        opening = jnp.maximum(opening, jnp.where(places >= ending, ending, 0))
    cos, sin = rotary_tables(places - opening)
    place_docs = jnp.concatenate((place_t[None], doc_lengths))
    attn_row = attn_gain.reshape(1, -1)
    across, cos, sin, place_docs, place_xy, attn_row = lax.optimization_barrier(
        (across, cos, sin, place_docs, place_xy, attn_row)
    )
    token_blocks = (tokens, across, over_core(tokens), over_core(across))

    cot_across = over_z(after(cotangent, across))
    h1, qkv, heads_out, lse, high, low = attention(
        place_docs, token_blocks, attn_row, query_weight, key_weight, value_weight, out_weight, cos, sin
    )
    cot_pair = jnp.concatenate((cotangent, after(cot_across, low)), axis=0)
    hidden_own = dot_rt(cot_pair, down_weight)
    own, other = chip_sums(high, low, hidden_own)
    z_sums = over_z(jnp.concatenate((other.astype(BF), own.astype(BF)), axis=0))
    cot_halves = (cot_pair, over_core(after(cot_pair, own)))
    hidden_other = dot_rt(after(cot_halves[1], other), down_weight)
    z_sums = after(z_sums, hidden_other)
    mid = jnp.concatenate((add(tokens, own, z_sums[:rows]), add(across, other, z_sums[rows:])), axis=0)
    normed_two, inverse_two = norm(mid)
    h2 = (normed_two * gain_two).astype(BF)
    h2 = (h2, over_core(h2))
    units = gate_weight.shape[1]
    split = units // 2 // 128 * 128 + 128
    hidden, grad_gate_val, grad_up_val, first = mlp(
        place_xy, h2, (hidden_own, hidden_other), gate_weight, up_weight, cot_halves, split
    )
    first_sum = Reduction(first)
    first_links = stage([(first_sum, 0)])
    high, low, gain_two_part, second = mlp_back(
        place_xy, after(grad_gate_val, first[0]), grad_up_val, gate_weight, up_weight, h2, split
    )
    own, other = chip_sums(high, low, *first_links)
    second_sum = Reduction(second)
    links = stage([(second_sum, 0)], first_links)
    z_sums = over_z(jnp.concatenate((other.astype(BF), own.astype(BF)), axis=0))
    mlp_part = dot(after(hidden, other, *first_links), down_weight).astype(BF)
    z_sums = after(z_sums, mlp_part)
    grad_h2 = jnp.concatenate((add(own, z_sums[:rows]), add(other, z_sums[rows:])), axis=0)
    grad_mid = cot_pair.astype(F32) + norm_back(normed_two, inverse_two, gain_two, grad_h2)
    mid_low = grad_mid.astype(BF)
    cut = rows + rows // 2
    mid_low = (mid_low, jnp.concatenate((over_core(mid_low[:cut]), over_core(mid_low[cut:])), axis=0))

    jobs = [(first_sum, 1), (second_sum, 1)]
    operands = prepare(jobs)
    result_got = over_core(after(mlp_part[2 * rows :], mid_low[1]))
    high, low, gains, attn = attention_back(
        place_docs, place_xy, mid_low, after(qkv, *operands), lse, h1, heads_out,
        query_weight, key_weight, value_weight, out_weight, cos, sin, gain_two_part,
    )
    links = send(jobs, operands, links, low)
    attn_sum = Reduction(attn)
    gains = Gains(gains)
    own, other = chip_sums(high, low)
    links = stage([(first_sum, 2), (second_sum, 2)], links, gains=gains, gains_link=0)
    grad_h1 = own + over_z(other.astype(BF)).astype(F32)
    result_chip = add(mlp_part[: 2 * rows], after(result_got, other))
    gains.exchange(over_z, [grad_h1])
    links = stage([(attn_sum, 0)], links)
    result_z = over_z(after(result_chip[rows:].astype(BF), grad_h1))
    result = (mid[:rows] + result_chip[:rows] + result_z.astype(F32)).astype(BF)
    links = stage([(first_sum, 3), (second_sum, 3), (attn_sum, 1)], links, gains=gains, gains_link=1)
    gains.exchange(over_core, [result_z])
    place_z = place_z[None]
    out_first, out_second = finish([first_sum, second_sum], place_z, [result_z])
    links = stage([(attn_sum, 2)], links, gains=gains, gains_link=2)
    links = stage([(attn_sum, 3)], links, gains=gains, gains_link=3)
    grad_gains, out_attn = finish([attn_sum], place_z, [], gains, out_first)
    grad_gains = grad_gains.reshape(2, -1)

    normed, inverse = norm(tokens.astype(F32))
    grad_tokens = grad_mid[:rows] + norm_back(normed, inverse, gain_one, grad_h1)
    return (
        result,
        grad_tokens.astype(BF),
        grad_gains[0] / gain_one,
        out_attn[:, :q_width],
        out_attn[:, q_width : q_width + HD],
        out_attn[:, q_width + HD : q_width + 2 * HD],
        out_attn[:, q_width + 2 * HD :].T,
        grad_gains[1] / gain_two,
        jnp.concatenate((out_first[:, units:], out_second[:, : units - split]), axis=1),
        out_second[:, units - split :],
        out_first[:, :units].T,
    )


def solution(mesh):
    in_specs = (
        P(("dp", "tensor"), None),
        P(),
        P(None, "tensor"),
        P(None, "tensor"),
        P(None, "tensor"),
        P("tensor", None),
        P(),
        P(None, "tensor"),
        P(None, "tensor"),
        P("tensor", None),
        P(("dp", "tensor"), None),
        P("dp"),
    )
    out_specs = (
        P(("dp", "tensor"), None),
        P(("dp", "tensor"), None),
        P(),
        P("dp", "tensor"),
        P("dp", "tensor"),
        P("dp", "tensor"),
        P("tensor", "dp"),
        P(),
        P("dp", "tensor"),
        P("dp", "tensor"),
        P("tensor", "dp"),
    )
    return jax.shard_map(
        per_device, mesh=mesh, in_specs=in_specs, out_specs=out_specs, check_vma=False
    )
```

```python
import functools
import math

import jax
import jax.numpy as jnp
from jax import lax
from jax.experimental import pallas as pl
from jax.experimental.pallas import tpu as pltpu
from jax.sharding import PartitionSpec as P

HD = 64
EPSILON = 1e-05
THETA = 10000.0
MASKED = -1000000000.0
BF = jnp.bfloat16
F32 = jnp.float32
MIB = 1024 * 1024


def cost(time):
    return pl.CostEstimate(flops=int(time * 1e9), bytes_accessed=1024, transcendentals=0)


def dot(left, right):
    return jnp.dot(left, right, preferred_element_type=F32)


def dot_t(left, right):
    return lax.dot_general(left, right, (((0,), (0,)), ((), ())), preferred_element_type=F32)


def dot_rt(left, right):
    return lax.dot_general(left, right, (((1,), (1,)), ((), ())), preferred_element_type=F32)


def vmem():
    return pl.BlockSpec(memory_space=pltpu.VMEM)


def smem():
    return pl.BlockSpec(memory_space=pltpu.SMEM)


def hbm():
    return pl.BlockSpec(memory_space=pl.ANY)


def params(size):
    return pltpu.CompilerParams(vmem_limit_bytes=size * MIB)


def swap_halves(values):
    width = values.shape[1]
    lane = lax.broadcasted_iota(jnp.int32, values.shape, 1)
    return jnp.where(
        lane % HD < HD // 2,
        pltpu.roll(values, width - HD // 2, 1),
        pltpu.roll(values, HD // 2, 1),
    )


def wide(table, width):
    return jnp.concatenate([table] * (width // table.shape[1]), axis=1) if width > table.shape[1] else table[:, :width]


def places_of(place_t, ends, rows, shape, axis):
    index = lax.broadcasted_iota(jnp.int32, shape, axis)
    block = index // rows
    order = jnp.where(block == 0, 0, jnp.where(block == 1, 2, jnp.where(block == 2, 1, 3)))
    places = (place_t ^ order) * rows + index % rows
    opening = jnp.zeros(shape, jnp.int32)
    for end in ends:
        opening = jnp.maximum(opening, jnp.where(places >= end, end, 0))
    return places, opening


def doc_ends(place_ref, count):
    ends, total = [], jnp.int32(0)
    for i in range(count):
        total = total + place_ref[1 + i]
        ends.append(total)
    return ends


def attention_kernel(
    docs, place_ref, own, zpart, cpart, diag, gain, wq, wk, wv, wo, cos, sin, near,
    h1_ref, qkv_ref, o_ref, lse_ref, high_ref, low_ref, bias_ref,
):
    rows = own.shape[0]
    every = 4 * rows
    half = 2 * rows
    q_width = wq.shape[1]
    heads = q_width // HD
    gain_row = gain[...].astype(F32)
    for number, block in enumerate((own, zpart, cpart, diag)):
        values = block[...].astype(F32)
        inverse = lax.rsqrt(jnp.mean(values * values, axis=-1, keepdims=True) + EPSILON)
        h1_ref[number * rows : (number + 1) * rows, :] = (values * inverse * gain_row).astype(BF)
    h1 = h1_ref[...]
    joined = jnp.concatenate((wk[...], wv[...]), axis=0)
    table_c, table_s = cos[...], sin[...]

    def rope(values):
        width = values.shape[1]
        return values * wide(table_c, width) + swap_halves(values) * wide(table_s, width)

    scale = 1.0 / math.sqrt(HD)
    kv = dot_rt(h1, joined)
    lane = lax.broadcasted_iota(jnp.int32, kv.shape, 1)
    qkv_ref[:, q_width:] = jnp.where(lane < HD, rope(kv), kv).astype(BF)
    qkv_ref[:, :q_width] = rope(dot(h1, wq[...])).astype(BF)

    ends = doc_ends(place_ref, docs)
    places_q, opening_q = places_of(place_ref[0], ends, rows, (every, 1), 0)
    places_k, _ = places_of(place_ref[0], ends, rows, (1, every), 1)
    bias_ref[...] = jnp.where((places_k <= places_q) & (places_k >= opening_q), 0.0, MASKED)

    keys = qkv_ref[:, q_width : q_width + HD]
    kv_low = qkv_ref[:, q_width:]
    lane = lax.broadcasted_iota(jnp.int32, kv_low.shape, 1)
    ones_vals = jnp.where(lane < HD, jnp.ones_like(kv_low), kv_low)
    lse_lane = lax.broadcasted_iota(jnp.int32, (every, 128), 1)
    lse = jnp.zeros((every, 128), F32)
    for head in range(heads):
        query = qkv_ref[:, head * HD : (head + 1) * HD]
        scores = dot_rt(query, keys) * scale + bias_ref[...]
        highest = jnp.max(scores, axis=-1, keepdims=True)
        raised = jnp.exp(scores - highest)
        mixed = dot(raised.astype(BF), ones_vals)
        totals = mixed[:, :1]
        o_ref[:, head * HD : (head + 1) * HD] = (mixed[:, HD:] / totals).astype(BF)
        lse = jnp.where(lse_lane == head, highest + jnp.log(totals), lse)
    lse_ref[...] = lse.T[:heads, :]
    high_ref[...] = dot(o_ref[:half, :], wo[...])
    low_ref[...] = dot(o_ref[half:, :], wo[...]).astype(BF)


def attention(place_docs, blocks, gain, wq, wk, wv, wo, cos, sin, near):
    rows, width = blocks[0].shape
    every = rows * 4
    q_width = wq.shape[1]
    heads = q_width // HD
    shapes = (
        jax.ShapeDtypeStruct((every, width), BF),
        jax.ShapeDtypeStruct((every, q_width + 2 * HD), BF),
        jax.ShapeDtypeStruct((every, q_width), BF),
        jax.ShapeDtypeStruct((heads, every), F32),
        jax.ShapeDtypeStruct((2 * rows, width), F32),
        jax.ShapeDtypeStruct((2 * rows, width), BF),
    )
    return pl.pallas_call(
        functools.partial(attention_kernel, place_docs.shape[0] - 1),
        out_shape=shapes,
        in_specs=[smem()] + [vmem()] * 12,
        out_specs=[vmem()] * 6,
        scratch_shapes=[pltpu.VMEM((every, every), F32)],
        compiler_params=params(12),
        name="attention",
        cost_estimate=cost(11),
    )(place_docs, *blocks, gain, wq, wk.T, wv.T, wo, cos, sin, near)


SEND = ((1, 2), (3, 2))
KEEP = ((0, 3), (0, 1))


def gradient_body(place_ref, groups, outs, tile=512):
    place_x, place_y = place_ref[0], place_ref[1]
    at = 0
    for lefts, right, begin, width in groups:
        for jx in range(4):
            columns = []
            for jy in range(4):
                start = pl.multiple_of(((place_x ^ jx) * 4 + (place_y ^ jy)) * 128, 128)
                columns.append(jnp.concatenate([left[:, pl.ds(start, 128)] for left in lefts], axis=0))
            left = jnp.concatenate(columns, axis=1)
            for s in range(0, width, tile):
                n = min(tile, width - s)
                cube = dot_t(left, right[:, begin + s : begin + s + n]).astype(BF).reshape(4, 4, 32, n)
                for b in range(n // 128):
                    block = at + s // 128 + b
                    piece = cube[:, :, :, b * 128 : (b + 1) * 128]
                    for part in range(2):
                        for number, slots in enumerate((SEND[part], KEEP[part])):
                            if jx in slots:
                                outs[2 * part + number][slots.index(jx), :, block] = piece[:, part]
                            for slot in range(2):
                                outs[4 + 2 * part + number][slot, jx, block] = piece[slots[slot], 2 + part]
        at += width // 128


def gradient_shapes(width):
    return [jax.ShapeDtypeStruct((2, 4, width // 128, 32, 128), BF)] * 8


def mlp_kernel(tile, split, place_ref, h2_a, h2_b, dh_a, dh_b, wg, wu, cot_a, cot_b, near, hid_ref, dgate_ref, dup_ref, *outs):
    units = wg.shape[1]
    h2 = jnp.concatenate((h2_a[...], h2_b[...]), axis=0)
    for s in range(0, units, tile):
        cut = slice(s, min(s + tile, units))
        gate = dot(h2, wg[:, cut])
        up = dot(h2, wu[:, cut])
        dh = jnp.concatenate((dh_a[:, cut], dh_b[:, cut]), axis=0).astype(F32)
        sig = jax.nn.sigmoid(gate)
        active = gate * sig
        hid_ref[:, cut] = (active * up).astype(BF)
        dgate_ref[:, cut] = (dh * up * (sig + active * (1.0 - sig))).astype(BF)
        dup_ref[:, cut] = (dh * active).astype(BF)
    gradient_body(place_ref, [((cot_a, cot_b), hid_ref, 0, units), ((h2_a, h2_b), dgate_ref, 0, split)], outs)


def mlp(place_xy, h2_halves, dh, wg, wu, cot_halves, near, split, tile=512):
    half, width = h2_halves[0].shape
    every = 2 * half
    units = wg.shape[1]
    got = pl.pallas_call(
        functools.partial(mlp_kernel, tile, split),
        out_shape=[jax.ShapeDtypeStruct((every, units), BF)] * 3 + gradient_shapes(units + split),
        in_specs=[smem()] + [vmem()] * 9,
        out_specs=[vmem()] * 11,
        compiler_params=params(12),
        name="mlp",
        cost_estimate=cost(18),
    )(place_xy, *h2_halves, *dh, wg, wu, *cot_halves, near)
    return (*got[:3], got[3:])


def mlp_back_kernel(step, split, place_ref, dgate, dup, wg, wu, h2_a, h2_b, high_ref, low_ref, gain_ref, *outs):
    half, width = h2_a.shape
    for s in range(0, width, step):
        cut = slice(s, s + step)
        part = dot_rt(dgate[...], wg[cut, :]) + dot_rt(dup[...], wu[cut, :])
        high_ref[:, cut] = part[:half]
        low_ref[:, cut] = part[half:].astype(BF)
        gain_ref[:, cut] = jnp.sum(part[:half] * h2_a[:, cut].astype(F32), axis=0, keepdims=True) + jnp.sum(
            part[half:] * h2_b[:, cut].astype(F32), axis=0, keepdims=True
        )
    units = dup.shape[1]
    lefts = (h2_a, h2_b)
    gradient_body(place_ref, [(lefts, dgate, split, units - split), (lefts, dup, 0, units)], outs)


def mlp_back(place_xy, dgate, dup, wg, wu, h2_halves, split, step=512):
    half, width = h2_halves[0].shape
    got = pl.pallas_call(
        functools.partial(mlp_back_kernel, step, split),
        out_shape=[
            jax.ShapeDtypeStruct((half, width), F32),
            jax.ShapeDtypeStruct((half, width), BF),
            jax.ShapeDtypeStruct((1, width), F32),
        ]
        + gradient_shapes(2 * wg.shape[1] - split),
        in_specs=[smem()] + [vmem()] * 6,
        out_specs=[vmem()] * 11,
        compiler_params=params(12),
        name="mlp_back",
        cost_estimate=cost(14),
    )(place_xy, dgate, dup, wg, wu, *h2_halves)
    return (*got[:3], got[3:])


def touch_kernel(*refs):
    *sources, target = refs
    total = jnp.zeros(target.shape, F32)
    for source in sources:
        total = total + source[:16, :128].astype(F32)
    target[...] = total


def touch(*arrays):
    return pl.pallas_call(
        touch_kernel,
        out_shape=jax.ShapeDtypeStruct((16, 128), F32),
        in_specs=[vmem()] * len(arrays),
        out_specs=vmem(),
        compiler_params=params(12),
        name="touch",
        cost_estimate=cost(2),
    )(*arrays)


def pair_kernel(above, below, later, target):
    rows = above.shape[0]
    target[:rows] = above[...]
    target[rows:] = below[...]


def pair(above, below, later):
    rows, width = above.shape
    return pl.pallas_call(
        pair_kernel,
        out_shape=jax.ShapeDtypeStruct((2 * rows, width), above.dtype),
        in_specs=[vmem()] * 2 + [pl.BlockSpec(memory_space=pl.ANY)],
        out_specs=vmem(),
        compiler_params=params(4),
        name="pair",
        cost_estimate=cost(8),
    )(above, below, later)


def combine_kernel(sums, *refs):
    out = refs[-1]
    at = 0
    for count, terms in sums:
        total = None
        for number, start in terms:
            term = refs[number][start : start + count].astype(F32)
            total = term if total is None else total + term
        out[at : at + count] = total.astype(out.dtype)
        at += count


def combine(sums):
    arrays, plan = [], []
    for terms in sums:
        listed = []
        for array, start, count in terms:
            known = [i for i, a in enumerate(arrays) if a is array]
            if not known:
                arrays.append(array)
            listed.append((known[0] if known else len(arrays) - 1, start))
        plan.append((terms[0][2], listed))
    total = sum(count for count, _ in plan)
    return pl.pallas_call(
        functools.partial(combine_kernel, plan),
        out_shape=jax.ShapeDtypeStruct((total, 32, 128), BF),
        in_specs=[vmem()] * len(arrays),
        out_specs=vmem(),
        compiler_params=params(8),
        name="combine",
        cost_estimate=cost(0.5),
    )(*arrays)


def ends_kernel(sums, extra, place_ref, *refs):
    give, keep = refs[-2:]
    at = 0
    if extra:
        total = None
        for number, start in extra:
            term = refs[number][start : start + 1].astype(F32)
            total = term if total is None else total + term
        give[0:1] = total.astype(BF)
        keep[0:1] = total.astype(BF).astype(F32)
        at = 1
    for parts in sums:
        count = parts[0][0]
        totals = []
        for _, terms in parts:
            total = None
            for number, start in terms:
                term = refs[number][start : start + count].astype(F32)
                total = term if total is None else total + term
            totals.append(total)
        for half in range(2):
            cut = slice(at, at + count)
            give[cut] = jnp.where(place_ref[0] == 0, totals[2 + half], totals[half]).astype(BF)
            keep[cut] = jnp.where(place_ref[0] == 0, totals[half], totals[2 + half])
            at += count


def ends(place_z, sums, extra=()):
    arrays, plan = [], []
    for parts in sums:
        planned = []
        for terms in parts:
            listed = []
            for array, start, count in terms:
                known = [i for i, a in enumerate(arrays) if a is array]
                if not known:
                    arrays.append(array)
                listed.append((known[0] if known else len(arrays) - 1, start))
            planned.append((terms[0][2], listed))
        plan.append(planned)
    arrays += [array for array, _, _ in extra]
    more = [(len(arrays) - len(extra) + i, start) for i, (_, start, _) in enumerate(extra)]
    total = sum(2 * parts[0][0] for parts in plan) + bool(extra)
    return pl.pallas_call(
        functools.partial(ends_kernel, plan, more),
        out_shape=(jax.ShapeDtypeStruct((total, 32, 128), BF), jax.ShapeDtypeStruct((total, 32, 128), F32)),
        in_specs=[smem()] + [vmem()] * len(arrays),
        out_specs=[vmem()] * 2,
        compiler_params=params(16),
        name="ends",
        cost_estimate=cost(1),
    )(place_z, *arrays)


def attention_back_kernel(
    docs, place_ref, place_xy, mid_a, mid_b, qkv, lse_ref, h1, o_ref, wq, wk, wv, wo, cos, sin, gain_two, *refs
):
    dqkv_ref, high_ref, low_ref, gains, *outs, bias_ref, do_ref = refs
    half = mid_a.shape[0]
    rows, every = half // 2, 2 * half
    q_width = wq.shape[1]
    heads = q_width // HD
    width = wq.shape[0]
    scale = 1.0 / math.sqrt(HD)
    mid = jnp.concatenate((mid_a[...], mid_b[...]), axis=0)
    do_ref[...] = dot_rt(mid, wo[...]).astype(BF)
    ends = doc_ends(place_ref, docs)
    places_q, opening_q = places_of(place_ref[0], ends, rows, (1, every), 1)
    places_k, _ = places_of(place_ref[0], ends, rows, (every, 1), 0)
    bias_ref[...] = jnp.where((places_k <= places_q) & (places_k >= opening_q), 0.0, MASKED)
    keys = qkv[:, q_width : q_width + HD]
    vals = qkv[:, q_width + HD : q_width + 2 * HD]
    dk = jnp.zeros((every, HD), F32)
    dv = jnp.zeros((every, HD), F32)
    table_c, table_s = cos[...], sin[...]

    def unrope(values):
        wide_now = values.shape[1]
        return values * wide(table_c, wide_now) - swap_halves(values) * wide(table_s, wide_now)

    for pair in range(heads // 2):
        dqs = []
        for head in (2 * pair, 2 * pair + 1):
            cut = slice(head * HD, (head + 1) * HD)
            query = qkv[:, cut]
            grad_o = do_ref[:, cut]
            scores = dot_rt(keys, query) * scale + bias_ref[...]
            chances = jnp.exp(scores - lse_ref[head : head + 1, :])
            grad_chances = dot_rt(vals, grad_o)
            centre = jnp.sum(chances * grad_chances, axis=0, keepdims=True)
            grad_scores = (chances * (grad_chances - centre)).astype(BF)
            dv = dv + dot(chances.astype(BF), grad_o)
            dk = dk + dot(grad_scores, query)
            dqs.append(dot_t(grad_scores, keys))
        dq = jnp.concatenate(dqs, axis=1) * scale
        dqkv_ref[:, pair * 2 * HD : (pair + 1) * 2 * HD] = unrope(dq).astype(BF)
    both = jnp.concatenate((dk * scale, dv), axis=1)
    lane = lax.broadcasted_iota(jnp.int32, both.shape, 1)
    dqkv_ref[:, q_width:] = jnp.where(lane < HD, unrope(both), both).astype(BF)
    joined = jnp.concatenate((wk[...], wv[...]), axis=0)
    step = 512
    for s in range(0, width, step):
        part = dot_rt(dqkv_ref[:, :q_width], wq[s : s + step, :]) + dot(dqkv_ref[:, q_width:], joined[:, s : s + step])
        high_ref[:, s : s + step] = part[:half]
        low_ref[:, s : s + step] = part[half:].astype(BF)
        gain_one = jnp.sum(part * h1[:, s : s + step].astype(F32), axis=0, keepdims=True)
        for lane in range(0, step, 128):
            row = (s + lane) // 128
            gains[0, row : row + 1, :] = gain_one[:, lane : lane + 128]
            gains[0, width // 128 + row : width // 128 + row + 1, :] = gain_two[:, s + lane : s + lane + 128]
    gradient_body(place_xy, [((h1,), dqkv_ref, 0, q_width + 2 * HD), ((mid_a, mid_b), o_ref, 0, q_width)], outs)


def attention_back(place_docs, place_xy, mids, qkv, lse, h1, o, wq, wk, wv, wo, cos, sin, gain_two_part):
    half, width = mids[0].shape
    every = 2 * half
    q_width = wq.shape[1]
    got = pl.pallas_call(
        functools.partial(attention_back_kernel, place_docs.shape[0] - 1),
        out_shape=[
            jax.ShapeDtypeStruct((every, q_width + 2 * HD), BF),
            jax.ShapeDtypeStruct((half, width), F32),
            jax.ShapeDtypeStruct((half, width), BF),
            jax.ShapeDtypeStruct((1, width // 64, 128), F32),
        ]
        + gradient_shapes(2 * q_width + 2 * HD),
        in_specs=[smem()] * 2 + [vmem()] * 13,
        out_specs=[vmem()] * 12,
        scratch_shapes=[
            pltpu.VMEM((every, every), F32),
            pltpu.VMEM((every, q_width), BF),
        ],
        compiler_params=params(12),
        name="attention_back",
        cost_estimate=cost(19),
    )(place_docs, place_xy, *mids, qkv, lse, h1, o, wq, wk.T, wv.T, wo, cos, sin, gain_two_part)
    return (*got[1:4], got[4:])


def rotary_tables(offset):
    half_size = HD // 2
    freqs = THETA ** (-(jnp.arange(half_size, dtype=F32) * 2.0 / HD))
    angles = offset.astype(F32)[:, None] * freqs[None, :]
    cosine, sine = jnp.cos(angles), jnp.sin(angles)
    return jnp.concatenate((cosine,) * 4, axis=1), jnp.concatenate((-sine, sine) * 2, axis=1)


def over_core(values):
    return lax.ppermute(values, "tensor", [(t, t ^ 1) for t in range(4)])


def over_z(values):
    return lax.ppermute(values, "tensor", [(t, t ^ 2) for t in range(4)])


def over_x(values, xor):
    return lax.ppermute(values, "dp", [(d, d ^ (xor * 8)) for d in range(32)])


def over_y(values, xor):
    return lax.ppermute(values, "dp", [(d, d ^ (xor * 2)) for d in range(32)])


def over_z_hi(values):
    return lax.ppermute(values, "dp", [(d, d ^ 1) for d in range(32)])


def after(value, *others):
    return lax.optimization_barrier((value, *others))[0] if others else value


def add(*terms):
    total = terms[0].astype(F32)
    for term in terms[1:]:
        total = total + term.astype(F32)
    return total


def norm(values):
    inverse = lax.rsqrt(jnp.mean(values * values, axis=-1, keepdims=True) + EPSILON)
    return values * inverse, inverse


def norm_back(normed, inverse, gain, grads):
    scaled = grads * gain
    return inverse * (scaled - normed * jnp.mean(scaled * normed, axis=-1, keepdims=True))


LINKS = ((over_x, 1), (over_x, 3), (over_y, 1), (over_y, 3))
ROUTES = ((0, 1, 2, 3), (1, 0, 3, 2), (2, 3, 0, 1), (3, 2, 1, 0))


class Reduction:
    def __init__(self, arrays):
        self.blocks = arrays[0].shape[2]
        self.sends = [arrays[2 * part].reshape(-1, 32, 128) for part in range(4)]
        kept = [arrays[2 * part + 1].reshape(-1, 32, 128) for part in range(4)]
        self.held = [[(array, 0)] for array in kept]

    def terms(self, part, row, rows=1):
        n = self.blocks
        return [(array, start + row * n, rows * n) for array, start in self.held[part][:3]]

    def sum(self, part, step):
        n = self.blocks
        first, second = ((1, 3), (3, 1))[part % 2]
        held = self.held[part]
        if step == 0:
            return [(self.sends[part], 0, 8 * n)]
        if step == 1:
            return [(array, start + 4 * n, 4 * n) for array, start in held]
        if step == 2:
            return self.terms(part, min(first, 2), 2)
        near, far = (0, 1) if first == 1 else (1, 0)
        array, start = held[3]
        if step == 3:
            return self.terms(part, second) + [(array, start + far * n, n)]
        last, at = held[4]
        return self.terms(part, 0) + [(array, start + near * n, n), (last, at, n)]


class Gains:
    def __init__(self, block):
        self.held = [(block, 0)]

    def terms(self):
        return [(array, start, 1) for array, start in self.held]

    def exchange(self, hop, before):
        sent = sum(array[start : start + 1].astype(F32) for array, start in self.held).astype(BF)
        self.held = [(sent, 0), (hop(after(sent, *before)), 0)]


def takers(jobs, link):
    return [(r, part, step) for r, step in jobs for part in range(4) if ROUTES[part][step] == link]


def prepare(jobs, gains=None, gains_link=None):
    operands = []
    for link in range(4):
        taken = takers(jobs, link)
        if len(taken) == 1 and taken[0][2] == 0:
            operands.append(taken[0][0].sends[taken[0][1]])
            continue
        sums = [r.sum(part, step) for r, part, step in taken]
        operands.append(combine(sums + ([gains.terms()] if link == gains_link else [])))
    return operands


def send(jobs, operands, before=None, anchor=None, gains=None, gains_link=None):
    arrived = []
    for link, (operand, (hop, xor)) in enumerate(zip(operands, LINKS)):
        got = hop(after(operand, before[link]) if before else operand, xor)
        arrived.append(got)
        if anchor is not None:
            got = after(got, anchor)
        at = 0
        for r, part, step in takers(jobs, link):
            r.held[part].append((got, at))
            at += r.blocks * (8, 4, 2, 1)[step]
        if link == gains_link:
            gains.held = [(operand, at), (got, at)]
    return arrived


def stage(jobs, before=None, **more):
    return send(jobs, prepare(jobs, **more), before, **more)


def finish(reductions, place_z, before=(), gains=None, anchor=None):
    gives, keeps = ends(
        place_z,
        [[r.sum(part, 4) for part in range(4)] for r in reductions],
        gains.terms() if gains else (),
    )
    got = over_z_hi(after(gives, *before))
    if anchor is not None:
        got = after(got, anchor)
    at, rows = 0, []
    if gains:
        at = 1
        rows.append(add(keeps[0], got[0]))
    for r in reductions:
        cut = slice(at, at + 2 * r.blocks)
        total = add(keeps[cut], got[cut]).reshape(2, r.blocks, 32, 128)
        at += 2 * r.blocks
        rows.append(total.transpose(0, 2, 1, 3).reshape(64, r.blocks * 128))
    return rows


def chip_sums(high, low, *wait):
    rows = low.shape[0] // 2
    got = after(over_core(low), *wait)
    return add(high[:rows], got[:rows]), add(high[rows:], got[rows:])


def per_device(
    tokens,
    attn_gain,
    query_weight,
    key_weight,
    value_weight,
    out_weight,
    mlp_gain,
    gate_weight,
    up_weight,
    down_weight,
    cotangent,
    doc_lengths,
):
    rows = tokens.shape[0]
    place_dp = lax.axis_index("dp")
    place_t = lax.axis_index("tensor")
    place_z = place_dp % 2
    place_xy = jnp.stack((place_dp // 8, (place_dp // 2) % 4))
    q_width = query_weight.shape[1]
    gain_one, gain_two = attn_gain.astype(F32), mlp_gain.astype(F32)

    across = over_z(tokens)
    places = jnp.concatenate(
        [(place_t ^ j) * rows + jnp.arange(rows, dtype=jnp.int32) for j in (0, 2, 1, 3)]
    )
    opening, ending = jnp.zeros_like(places), jnp.int32(0)
    for number in range(doc_lengths.shape[0]):
        ending = ending + doc_lengths[number]
        opening = jnp.maximum(opening, jnp.where(places >= ending, ending, 0))
    cos, sin = rotary_tables(places - opening)
    place_docs = jnp.concatenate((place_t[None], doc_lengths))
    attn_row = attn_gain.reshape(1, -1)
    near = touch(query_weight, out_weight)
    across, cos, sin, place_docs, place_xy, attn_row, near = lax.optimization_barrier(
        (across, cos, sin, place_docs, place_xy, attn_row, near)
    )
    token_blocks = (tokens, across, over_core(tokens), over_core(across))

    cot_across = over_z(after(cotangent, across))
    h1, qkv, heads_out, lse, high, low = attention(
        place_docs, token_blocks, attn_row, query_weight, key_weight, value_weight, out_weight, cos, sin, near
    )
    cot_pair = pair(cotangent, cot_across, low)
    own, other = chip_sums(high, low, cot_pair)
    z_sums = over_z(jnp.concatenate((other.astype(BF), own.astype(BF)), axis=0))
    cot_halves = (cot_pair, over_core(after(cot_pair, own)))
    grad_hidden = [dot_rt(after(half, other), down_weight).astype(BF) for half in cot_halves]
    near = touch(after(gate_weight, *grad_hidden), up_weight)
    z_sums = after(z_sums, near)
    mid = jnp.concatenate((add(tokens, own, z_sums[:rows]), add(across, other, z_sums[rows:])), axis=0)
    normed_two, inverse_two = norm(mid)
    h2 = (normed_two * gain_two).astype(BF)
    h2 = (h2, over_core(h2))
    units = gate_weight.shape[1]
    split = units // 2 // 128 * 128 + 128
    hidden, grad_gate_val, grad_up_val, first = mlp(
        place_xy, h2, grad_hidden, gate_weight, up_weight, cot_halves, near, split
    )
    first_sum = Reduction(first)
    first_links = stage([(first_sum, 0)])
    high, low, gain_two_part, second = mlp_back(
        place_xy, after(grad_gate_val, first[0]), grad_up_val, gate_weight, up_weight, h2, split
    )
    own, other = chip_sums(high, low, *first_links)
    second_sum = Reduction(second)
    links = stage([(second_sum, 0)], first_links)
    z_sums = over_z(jnp.concatenate((other.astype(BF), own.astype(BF)), axis=0))
    mlp_part = dot(after(hidden, other, *first_links), down_weight).astype(BF)
    z_sums = after(z_sums, mlp_part)
    grad_h2 = jnp.concatenate((add(own, z_sums[:rows]), add(other, z_sums[rows:])), axis=0)
    grad_mid = cot_pair.astype(F32) + norm_back(normed_two, inverse_two, gain_two, grad_h2)
    mid_low = grad_mid.astype(BF)
    cut = rows + rows // 2
    mid_low = (mid_low, jnp.concatenate((over_core(mid_low[:cut]), over_core(mid_low[cut:])), axis=0))

    jobs = [(first_sum, 1), (second_sum, 1)]
    operands = prepare(jobs)
    result_got = over_core(after(mlp_part[2 * rows :], mid_low[1]))
    high, low, gains, attn = attention_back(
        place_docs, place_xy, mid_low, after(qkv, *operands), lse, h1, heads_out,
        query_weight, key_weight, value_weight, out_weight, cos, sin, gain_two_part,
    )
    links = send(jobs, operands, links, low)
    attn_sum = Reduction(attn)
    gains = Gains(gains)
    own, other = chip_sums(high, low)
    links = stage([(first_sum, 2), (second_sum, 2), (attn_sum, 0)], links, gains=gains, gains_link=0)
    grad_h1 = own + over_z(other.astype(BF)).astype(F32)
    result_chip = add(mlp_part[: 2 * rows], after(result_got, other))
    gains.exchange(over_z, [grad_h1])
    result_z = over_z(after(result_chip[rows:].astype(BF), grad_h1))
    result = (mid[:rows] + result_chip[:rows] + result_z.astype(F32)).astype(BF)
    links = stage([(first_sum, 3), (second_sum, 3), (attn_sum, 1)], links, gains=gains, gains_link=1)
    gains.exchange(over_core, [result_z])
    place_z = place_z[None]
    out_first, out_second = finish([first_sum, second_sum], place_z, [result_z])
    links = stage([(attn_sum, 2)], links, gains=gains, gains_link=2)
    links = stage([(attn_sum, 3)], links, gains=gains, gains_link=3)
    grad_gains, out_attn = finish([attn_sum], place_z, [], gains, out_first)
    grad_gains = grad_gains.reshape(2, -1)

    normed, inverse = norm(tokens.astype(F32))
    grad_tokens = grad_mid[:rows] + norm_back(normed, inverse, gain_one, grad_h1)
    return (
        result,
        grad_tokens.astype(BF),
        grad_gains[0] / gain_one,
        out_attn[:, :q_width],
        out_attn[:, q_width : q_width + HD],
        out_attn[:, q_width + HD : q_width + 2 * HD],
        out_attn[:, q_width + 2 * HD :].T,
        grad_gains[1] / gain_two,
        jnp.concatenate((out_first[:, units:], out_second[:, : units - split]), axis=1),
        out_second[:, units - split :],
        out_first[:, :units].T,
    )


def solution(mesh):
    in_specs = (
        P(("dp", "tensor"), None),
        P(),
        P(None, "tensor"),
        P(None, "tensor"),
        P(None, "tensor"),
        P("tensor", None),
        P(),
        P(None, "tensor"),
        P(None, "tensor"),
        P("tensor", None),
        P(("dp", "tensor"), None),
        P("dp"),
    )
    out_specs = (
        P(("dp", "tensor"), None),
        P(("dp", "tensor"), None),
        P(),
        P("dp", "tensor"),
        P("dp", "tensor"),
        P("dp", "tensor"),
        P("tensor", "dp"),
        P(),
        P("dp", "tensor"),
        P("dp", "tensor"),
        P("tensor", "dp"),
    )
    return jax.shard_map(
        per_device, mesh=mesh, in_specs=in_specs, out_specs=out_specs, check_vma=False
    )
```

```python
import functools
import math

import jax
import jax.numpy as jnp
from jax import lax
from jax.experimental import pallas as pl
from jax.experimental.pallas import tpu as pltpu
from jax.sharding import PartitionSpec as P

HD = 64
EPSILON = 1e-05
THETA = 10000.0
MASKED = -1000000000.0
BF = jnp.bfloat16
F32 = jnp.float32
MIB = 1024 * 1024


def cost(time):
    return pl.CostEstimate(flops=int(time * 1e9), bytes_accessed=1024, transcendentals=0)


def dot(left, right):
    return jnp.dot(left, right, preferred_element_type=F32)


def dot_t(left, right):
    return lax.dot_general(left, right, (((0,), (0,)), ((), ())), preferred_element_type=F32)


def dot_rt(left, right):
    return lax.dot_general(left, right, (((1,), (1,)), ((), ())), preferred_element_type=F32)


def vmem():
    return pl.BlockSpec(memory_space=pltpu.VMEM)


def smem():
    return pl.BlockSpec(memory_space=pltpu.SMEM)


def hbm():
    return pl.BlockSpec(memory_space=pl.ANY)


def params(size):
    return pltpu.CompilerParams(vmem_limit_bytes=size * MIB)


def swap_halves(values):
    width = values.shape[1]
    lane = lax.broadcasted_iota(jnp.int32, values.shape, 1)
    return jnp.where(
        lane % HD < HD // 2,
        pltpu.roll(values, width - HD // 2, 1),
        pltpu.roll(values, HD // 2, 1),
    )


def wide(table, width):
    return jnp.concatenate([table] * (width // table.shape[1]), axis=1) if width > table.shape[1] else table[:, :width]


def places_of(place_t, ends, rows, shape, axis):
    index = lax.broadcasted_iota(jnp.int32, shape, axis)
    block = index // rows
    order = jnp.where(block == 0, 0, jnp.where(block == 1, 2, jnp.where(block == 2, 1, 3)))
    places = (place_t ^ order) * rows + index % rows
    opening = jnp.zeros(shape, jnp.int32)
    for end in ends:
        opening = jnp.maximum(opening, jnp.where(places >= end, end, 0))
    return places, opening


def doc_ends(place_ref, count):
    ends, total = [], jnp.int32(0)
    for i in range(count):
        total = total + place_ref[1 + i]
        ends.append(total)
    return ends


def attention_kernel(
    docs, place_ref, own, zpart, cpart, diag, gain, wq, wk, wv, wo, cos, sin, near,
    h1_ref, qkv_ref, o_ref, lse_ref, high_ref, low_ref, bias_ref,
):
    rows = own.shape[0]
    every = 4 * rows
    half = 2 * rows
    q_width = wq.shape[1]
    heads = q_width // HD
    gain_row = gain[...].astype(F32)
    for number, block in enumerate((own, zpart, cpart, diag)):
        values = block[...].astype(F32)
        inverse = lax.rsqrt(jnp.mean(values * values, axis=-1, keepdims=True) + EPSILON)
        h1_ref[number * rows : (number + 1) * rows, :] = (values * inverse * gain_row).astype(BF)
    h1 = h1_ref[...]
    joined = jnp.concatenate((wk[...], wv[...]), axis=0)
    table_c, table_s = cos[...], sin[...]

    def rope(values):
        width = values.shape[1]
        return values * wide(table_c, width) + swap_halves(values) * wide(table_s, width)

    scale = 1.0 / math.sqrt(HD)
    kv = dot_rt(h1, joined)
    lane = lax.broadcasted_iota(jnp.int32, kv.shape, 1)
    qkv_ref[:, q_width:] = jnp.where(lane < HD, rope(kv), kv).astype(BF)
    qkv_ref[:, :q_width] = rope(dot(h1, wq[...])).astype(BF)

    ends = doc_ends(place_ref, docs)
    places_q, opening_q = places_of(place_ref[0], ends, rows, (every, 1), 0)
    places_k, _ = places_of(place_ref[0], ends, rows, (1, every), 1)
    bias_ref[...] = jnp.where((places_k <= places_q) & (places_k >= opening_q), 0.0, MASKED)

    keys = qkv_ref[:, q_width : q_width + HD]
    kv_low = qkv_ref[:, q_width:]
    lane = lax.broadcasted_iota(jnp.int32, kv_low.shape, 1)
    ones_vals = jnp.where(lane < HD, jnp.ones_like(kv_low), kv_low)
    lse_lane = lax.broadcasted_iota(jnp.int32, (every, 128), 1)
    lse = jnp.zeros((every, 128), F32)
    for head in range(heads):
        query = qkv_ref[:, head * HD : (head + 1) * HD]
        scores = dot_rt(query, keys) * scale + bias_ref[...]
        highest = jnp.max(scores, axis=-1, keepdims=True)
        raised = jnp.exp(scores - highest)
        mixed = dot(raised.astype(BF), ones_vals)
        totals = mixed[:, :1]
        o_ref[:, head * HD : (head + 1) * HD] = (mixed[:, HD:] / totals).astype(BF)
        lse = jnp.where(lse_lane == head, highest + jnp.log(totals), lse)
    lse_ref[...] = lse.T[:heads, :]
    high_ref[...] = dot(o_ref[:half, :], wo[...])
    low_ref[...] = dot(o_ref[half:, :], wo[...]).astype(BF)


def attention(place_docs, blocks, gain, wq, wk, wv, wo, cos, sin, near):
    rows, width = blocks[0].shape
    every = rows * 4
    q_width = wq.shape[1]
    heads = q_width // HD
    shapes = (
        jax.ShapeDtypeStruct((every, width), BF),
        jax.ShapeDtypeStruct((every, q_width + 2 * HD), BF),
        jax.ShapeDtypeStruct((every, q_width), BF),
        jax.ShapeDtypeStruct((heads, every), F32),
        jax.ShapeDtypeStruct((2 * rows, width), F32),
        jax.ShapeDtypeStruct((2 * rows, width), BF),
    )
    return pl.pallas_call(
        functools.partial(attention_kernel, place_docs.shape[0] - 1),
        out_shape=shapes,
        in_specs=[smem()] + [vmem()] * 12,
        out_specs=[vmem()] * 6,
        scratch_shapes=[pltpu.VMEM((every, every), F32)],
        compiler_params=params(12),
        name="attention",
        cost_estimate=cost(11),
    )(place_docs, *blocks, gain, wq, wk.T, wv.T, wo, cos, sin, near)


SEND = ((1, 2), (3, 2))
KEEP = ((0, 3), (0, 1))


def gradient_body(place_ref, groups, outs, tile=512):
    place_x, place_y = place_ref[0], place_ref[1]
    at = 0
    for lefts, right, begin, width in groups:
        for jx in range(4):
            columns = []
            for jy in range(4):
                start = pl.multiple_of(((place_x ^ jx) * 4 + (place_y ^ jy)) * 128, 128)
                columns.append(jnp.concatenate([left[:, pl.ds(start, 128)] for left in lefts], axis=0))
            left = jnp.concatenate(columns, axis=1)
            for s in range(0, width, tile):
                n = min(tile, width - s)
                cube = dot_t(left, right[:, begin + s : begin + s + n]).astype(BF).reshape(4, 4, 32, n)
                for b in range(n // 128):
                    block = at + s // 128 + b
                    piece = cube[:, :, :, b * 128 : (b + 1) * 128]
                    for part in range(2):
                        for number, slots in enumerate((SEND[part], KEEP[part])):
                            if jx in slots:
                                outs[2 * part + number][slots.index(jx), :, block] = piece[:, part]
                            for slot in range(2):
                                outs[4 + 2 * part + number][slot, jx, block] = piece[slots[slot], 2 + part]
        at += width // 128


def gradient_shapes(width):
    return [jax.ShapeDtypeStruct((2, 4, width // 128, 32, 128), BF)] * 8


def mlp_kernel(tile, split, place_ref, h2_a, h2_b, dh_a, dh_b, wg, wu, cot_a, cot_b, near, hid_ref, dgate_ref, dup_ref, *outs):
    units = wg.shape[1]
    h2 = jnp.concatenate((h2_a[...], h2_b[...]), axis=0)
    for s in range(0, units, tile):
        cut = slice(s, min(s + tile, units))
        gate = dot(h2, wg[:, cut])
        up = dot(h2, wu[:, cut])
        dh = jnp.concatenate((dh_a[:, cut], dh_b[:, cut]), axis=0).astype(F32)
        sig = jax.nn.sigmoid(gate)
        active = gate * sig
        hid_ref[:, cut] = (active * up).astype(BF)
        dgate_ref[:, cut] = (dh * up * (sig + active * (1.0 - sig))).astype(BF)
        dup_ref[:, cut] = (dh * active).astype(BF)
    gradient_body(place_ref, [((cot_a, cot_b), hid_ref, 0, units), ((h2_a, h2_b), dgate_ref, 0, split)], outs)


def mlp(place_xy, h2_halves, dh, wg, wu, cot_halves, near, split, tile=512):
    half, width = h2_halves[0].shape
    every = 2 * half
    units = wg.shape[1]
    got = pl.pallas_call(
        functools.partial(mlp_kernel, tile, split),
        out_shape=[jax.ShapeDtypeStruct((every, units), BF)] * 3 + gradient_shapes(units + split),
        in_specs=[smem()] + [vmem()] * 9,
        out_specs=[vmem()] * 11,
        compiler_params=params(12),
        name="mlp",
        cost_estimate=cost(18),
    )(place_xy, *h2_halves, *dh, wg, wu, *cot_halves, near)
    return (*got[:3], got[3:])


def mlp_back_kernel(step, split, place_ref, dgate, dup, wg, wu, h2_a, h2_b, high_ref, low_ref, gain_ref, *outs):
    half, width = h2_a.shape
    for s in range(0, width, step):
        cut = slice(s, s + step)
        part = dot_rt(dgate[...], wg[cut, :]) + dot_rt(dup[...], wu[cut, :])
        high_ref[:, cut] = part[:half]
        low_ref[:, cut] = part[half:].astype(BF)
        gain_ref[:, cut] = jnp.sum(part[:half] * h2_a[:, cut].astype(F32), axis=0, keepdims=True) + jnp.sum(
            part[half:] * h2_b[:, cut].astype(F32), axis=0, keepdims=True
        )
    units = dup.shape[1]
    lefts = (h2_a, h2_b)
    gradient_body(place_ref, [(lefts, dgate, split, units - split), (lefts, dup, 0, units)], outs)


def mlp_back(place_xy, dgate, dup, wg, wu, h2_halves, split, step=512):
    half, width = h2_halves[0].shape
    got = pl.pallas_call(
        functools.partial(mlp_back_kernel, step, split),
        out_shape=[
            jax.ShapeDtypeStruct((half, width), F32),
            jax.ShapeDtypeStruct((half, width), BF),
            jax.ShapeDtypeStruct((1, width), F32),
        ]
        + gradient_shapes(2 * wg.shape[1] - split),
        in_specs=[smem()] + [vmem()] * 6,
        out_specs=[vmem()] * 11,
        compiler_params=params(12),
        name="mlp_back",
        cost_estimate=cost(14),
    )(place_xy, dgate, dup, wg, wu, *h2_halves)
    return (*got[:3], got[3:])


def touch_kernel(*refs):
    *sources, target = refs
    total = jnp.zeros(target.shape, F32)
    for source in sources:
        total = total + source[:16, :128].astype(F32)
    target[...] = total


def touch(*arrays):
    return pl.pallas_call(
        touch_kernel,
        out_shape=jax.ShapeDtypeStruct((16, 128), F32),
        in_specs=[vmem()] * len(arrays),
        out_specs=vmem(),
        compiler_params=params(12),
        name="touch",
        cost_estimate=cost(2),
    )(*arrays)


def pair_kernel(above, below, later, target):
    rows = above.shape[0]
    target[:rows] = above[...]
    target[rows:] = below[...]


def pair(above, below, later):
    rows, width = above.shape
    return pl.pallas_call(
        pair_kernel,
        out_shape=jax.ShapeDtypeStruct((2 * rows, width), above.dtype),
        in_specs=[vmem()] * 2 + [pl.BlockSpec(memory_space=pl.ANY)],
        out_specs=vmem(),
        compiler_params=params(4),
        name="pair",
        cost_estimate=cost(8),
    )(above, below, later)


def combine_kernel(sums, *refs):
    out = refs[-1]
    at = 0
    for count, terms in sums:
        total = None
        for number, start in terms:
            term = refs[number][start : start + count].astype(F32)
            total = term if total is None else total + term
        out[at : at + count] = total.astype(out.dtype)
        at += count


def combine(sums):
    arrays, plan = [], []
    for terms in sums:
        listed = []
        for array, start, count in terms:
            known = [i for i, a in enumerate(arrays) if a is array]
            if not known:
                arrays.append(array)
            listed.append((known[0] if known else len(arrays) - 1, start))
        plan.append((terms[0][2], listed))
    total = sum(count for count, _ in plan)
    return pl.pallas_call(
        functools.partial(combine_kernel, plan),
        out_shape=jax.ShapeDtypeStruct((total, 32, 128), BF),
        in_specs=[vmem()] * len(arrays),
        out_specs=vmem(),
        compiler_params=params(8),
        name="combine",
        cost_estimate=cost(0.5),
    )(*arrays)


def ends_kernel(sums, extra, place_ref, *refs):
    give, keep = refs[-2:]
    at = 0
    if extra:
        total = None
        for number, start in extra:
            term = refs[number][start : start + 1].astype(F32)
            total = term if total is None else total + term
        give[0:1] = total.astype(BF)
        keep[0:1] = total.astype(BF).astype(F32)
        at = 1
    for parts in sums:
        count = parts[0][0]
        totals = []
        for _, terms in parts:
            total = None
            for number, start in terms:
                term = refs[number][start : start + count].astype(F32)
                total = term if total is None else total + term
            totals.append(total)
        for half in range(2):
            cut = slice(at, at + count)
            give[cut] = jnp.where(place_ref[0] == 0, totals[2 + half], totals[half]).astype(BF)
            keep[cut] = jnp.where(place_ref[0] == 0, totals[half], totals[2 + half])
            at += count


def ends(place_z, sums, extra=()):
    arrays, plan = [], []
    for parts in sums:
        planned = []
        for terms in parts:
            listed = []
            for array, start, count in terms:
                known = [i for i, a in enumerate(arrays) if a is array]
                if not known:
                    arrays.append(array)
                listed.append((known[0] if known else len(arrays) - 1, start))
            planned.append((terms[0][2], listed))
        plan.append(planned)
    arrays += [array for array, _, _ in extra]
    more = [(len(arrays) - len(extra) + i, start) for i, (_, start, _) in enumerate(extra)]
    total = sum(2 * parts[0][0] for parts in plan) + bool(extra)
    return pl.pallas_call(
        functools.partial(ends_kernel, plan, more),
        out_shape=(jax.ShapeDtypeStruct((total, 32, 128), BF), jax.ShapeDtypeStruct((total, 32, 128), F32)),
        in_specs=[smem()] + [vmem()] * len(arrays),
        out_specs=[vmem()] * 2,
        compiler_params=params(16),
        name="ends",
        cost_estimate=cost(1),
    )(place_z, *arrays)


def attention_back_kernel(
    docs, place_ref, place_xy, mid_a, mid_b, qkv, lse_ref, h1, o_ref, wq, wk, wv, wo, cos, sin, gain_two, *refs
):
    dqkv_ref, high_ref, low_ref, gains, *outs, bias_ref, do_ref = refs
    half = mid_a.shape[0]
    rows, every = half // 2, 2 * half
    q_width = wq.shape[1]
    heads = q_width // HD
    width = wq.shape[0]
    scale = 1.0 / math.sqrt(HD)
    mid = jnp.concatenate((mid_a[...], mid_b[...]), axis=0)
    do_ref[...] = dot_rt(mid, wo[...]).astype(BF)
    ends = doc_ends(place_ref, docs)
    places_q, opening_q = places_of(place_ref[0], ends, rows, (1, every), 1)
    places_k, _ = places_of(place_ref[0], ends, rows, (every, 1), 0)
    bias_ref[...] = jnp.where((places_k <= places_q) & (places_k >= opening_q), 0.0, MASKED)
    keys = qkv[:, q_width : q_width + HD]
    vals = qkv[:, q_width + HD : q_width + 2 * HD]
    dk = jnp.zeros((every, HD), F32)
    dv = jnp.zeros((every, HD), F32)
    table_c, table_s = cos[...], sin[...]

    def unrope(values):
        wide_now = values.shape[1]
        return values * wide(table_c, wide_now) - swap_halves(values) * wide(table_s, wide_now)

    for pair in range(heads // 2):
        dqs = []
        for head in (2 * pair, 2 * pair + 1):
            cut = slice(head * HD, (head + 1) * HD)
            query = qkv[:, cut]
            grad_o = do_ref[:, cut]
            scores = dot_rt(keys, query) * scale + bias_ref[...]
            chances = jnp.exp(scores - lse_ref[head : head + 1, :])
            grad_chances = dot_rt(vals, grad_o)
            centre = jnp.sum(chances * grad_chances, axis=0, keepdims=True)
            grad_scores = (chances * (grad_chances - centre)).astype(BF)
            dv = dv + dot(chances.astype(BF), grad_o)
            dk = dk + dot(grad_scores, query)
            dqs.append(dot_t(grad_scores, keys))
        dq = jnp.concatenate(dqs, axis=1) * scale
        dqkv_ref[:, pair * 2 * HD : (pair + 1) * 2 * HD] = unrope(dq).astype(BF)
    both = jnp.concatenate((dk * scale, dv), axis=1)
    lane = lax.broadcasted_iota(jnp.int32, both.shape, 1)
    dqkv_ref[:, q_width:] = jnp.where(lane < HD, unrope(both), both).astype(BF)
    joined = jnp.concatenate((wk[...], wv[...]), axis=0)
    step = 512
    for s in range(0, width, step):
        part = dot_rt(dqkv_ref[:, :q_width], wq[s : s + step, :]) + dot(dqkv_ref[:, q_width:], joined[:, s : s + step])
        high_ref[:, s : s + step] = part[:half]
        low_ref[:, s : s + step] = part[half:].astype(BF)
        gain_one = jnp.sum(part * h1[:, s : s + step].astype(F32), axis=0, keepdims=True)
        for lane in range(0, step, 128):
            row = (s + lane) // 128
            gains[0, row : row + 1, :] = gain_one[:, lane : lane + 128]
            gains[0, width // 128 + row : width // 128 + row + 1, :] = gain_two[:, s + lane : s + lane + 128]
    gradient_body(place_xy, [((h1,), dqkv_ref, 0, q_width + 2 * HD), ((mid_a, mid_b), o_ref, 0, q_width)], outs)


def attention_back(place_docs, place_xy, mids, qkv, lse, h1, o, wq, wk, wv, wo, cos, sin, gain_two_part):
    half, width = mids[0].shape
    every = 2 * half
    q_width = wq.shape[1]
    got = pl.pallas_call(
        functools.partial(attention_back_kernel, place_docs.shape[0] - 1),
        out_shape=[
            jax.ShapeDtypeStruct((every, q_width + 2 * HD), BF),
            jax.ShapeDtypeStruct((half, width), F32),
            jax.ShapeDtypeStruct((half, width), BF),
            jax.ShapeDtypeStruct((1, width // 64, 128), F32),
        ]
        + gradient_shapes(2 * q_width + 2 * HD),
        in_specs=[smem()] * 2 + [vmem()] * 13,
        out_specs=[vmem()] * 12,
        scratch_shapes=[
            pltpu.VMEM((every, every), F32),
            pltpu.VMEM((every, q_width), BF),
        ],
        compiler_params=params(12),
        name="attention_back",
        cost_estimate=cost(19),
    )(place_docs, place_xy, *mids, qkv, lse, h1, o, wq, wk.T, wv.T, wo, cos, sin, gain_two_part)
    return (*got[1:4], got[4:])


def place_kernel(plan, keep, got, *outs):
    for out, parts in zip(outs, plan):
        for start, blocks, first, width, to in parts:
            for half in range(2):
                for b in range(blocks):
                    low, high = max(128 * b, first), min(128 * (b + 1), first + width)
                    if low >= high:
                        continue
                    at = start + half * blocks + b
                    total = keep[at] + got[at].astype(F32)
                    out[32 * half : 32 * (half + 1), to + low - first : to + high - first] = total[:, low - 128 * b : high - 128 * b]


def place(keep, got, plan):
    widths = [sum(part[3] for part in parts) for parts in plan]
    return pl.pallas_call(
        functools.partial(place_kernel, plan),
        out_shape=[jax.ShapeDtypeStruct((64, width), F32) for width in widths],
        in_specs=[vmem()] * 2,
        out_specs=[vmem()] * len(plan),
        compiler_params=params(12),
        name="place",
        cost_estimate=cost(1),
    )(keep, got)


def rotary_tables(offset):
    half_size = HD // 2
    freqs = THETA ** (-(jnp.arange(half_size, dtype=F32) * 2.0 / HD))
    angles = offset.astype(F32)[:, None] * freqs[None, :]
    cosine, sine = jnp.cos(angles), jnp.sin(angles)
    return jnp.concatenate((cosine,) * 4, axis=1), jnp.concatenate((-sine, sine) * 2, axis=1)


def over_core(values):
    return lax.ppermute(values, "tensor", [(t, t ^ 1) for t in range(4)])


def over_z(values):
    return lax.ppermute(values, "tensor", [(t, t ^ 2) for t in range(4)])


def over_x(values, xor):
    return lax.ppermute(values, "dp", [(d, d ^ (xor * 8)) for d in range(32)])


def over_y(values, xor):
    return lax.ppermute(values, "dp", [(d, d ^ (xor * 2)) for d in range(32)])


def over_z_hi(values):
    return lax.ppermute(values, "dp", [(d, d ^ 1) for d in range(32)])


def after(value, *others):
    return lax.optimization_barrier((value, *others))[0] if others else value


def add(*terms):
    total = terms[0].astype(F32)
    for term in terms[1:]:
        total = total + term.astype(F32)
    return total


def norm(values):
    inverse = lax.rsqrt(jnp.mean(values * values, axis=-1, keepdims=True) + EPSILON)
    return values * inverse, inverse


def norm_back(normed, inverse, gain, grads):
    scaled = grads * gain
    return inverse * (scaled - normed * jnp.mean(scaled * normed, axis=-1, keepdims=True))


LINKS = ((over_x, 1), (over_x, 3), (over_y, 1), (over_y, 3))
ROUTES = ((0, 1, 2, 3), (1, 0, 3, 2), (2, 3, 0, 1), (3, 2, 1, 0))


class Reduction:
    def __init__(self, arrays, joined=False):
        self.joined = joined
        self.blocks = arrays[0].shape[2]
        self.sends = [arrays[2 * part].reshape(-1, 32, 128) for part in range(4)]
        self.kept = [[(arrays[2 * part + 1].reshape(-1, 32, 128), self.starts(0, 8))] for part in range(4)]
        self.near, self.far, self.last = {}, {}, {}

    def starts(self, at, rows):
        return {row: at + row * self.blocks for row in range(rows)}

    def route(self, part, step):
        return ROUTES[part - part % 2 if self.joined and step >= 2 else part][step]

    def order(self, part):
        return ((1, 3), (3, 1))[0 if self.joined else part % 2]

    def row(self, part, row, rows=1):
        return [(array, starts[row], rows * self.blocks) for array, starts in self.kept[part]]

    def sum(self, part, step):
        first, second = self.order(part)
        if step == 0:
            return [(self.sends[part], 0, 8 * self.blocks)]
        if step == 1:
            return self.row(part, 4, 4)
        if step == 2:
            return self.row(part, min(first, 2), 2)
        if step == 3:
            return self.row(part, second) + [self.far[part]]
        return self.row(part, 0) + self.near.get(part, []) + [self.last[part]]

    def take(self, part, step, got, at):
        n = self.blocks
        if step < 2:
            self.kept[part].append((got, self.starts(at, 8 - 4 * step)))
        elif step == 2:
            near, far = (0, 1) if self.order(part)[0] == 1 else (1, 0)
            self.near[part] = [(got, at + near * n, n)]
            self.far[part] = (got, at + far * n, n)
        else:
            self.last[part] = (got, at, n)


def fold(jobs):
    folded = []
    for part in range(4):
        sums, places = [], []
        at = 0
        for r, rows in jobs:
            rows = {"last": (0, r.order(part)[1]), "own": (0,)}.get(rows, rows)
            starts = {}
            for row in rows:
                terms = r.row(part, row)
                if row == 0:
                    terms = terms + r.near.get(part, [])
                sums.append(terms)
                starts[row] = at
                at += r.blocks
            r.near.pop(part, None)
            places.append((r, starts))
        array = combine(sums)
        folded.append(array)
        for r, starts in places:
            r.kept[part] = [(array, starts)]
    return folded


class Gains:
    def __init__(self, block):
        self.held = [(block, 0)]

    def terms(self):
        return [(array, start, 1) for array, start in self.held]

    def exchange(self, hop, before):
        sent = sum(array[start : start + 1].astype(F32) for array, start in self.held).astype(BF)
        self.held = [(sent, 0), (hop(after(sent, *before)), 0)]


def takers(jobs, link):
    return [(r, part, step) for r, step in jobs for part in range(4) if r.route(part, step) == link]


def prepare(jobs, gains=None, gains_link=None):
    operands = []
    for link in range(4):
        taken = takers(jobs, link)
        if not taken:
            operands.append(None)
            continue
        if len(taken) == 1 and taken[0][2] == 0:
            operands.append(taken[0][0].sends[taken[0][1]])
            continue
        sums = [r.sum(part, step) for r, part, step in taken]
        operands.append(combine(sums + ([gains.terms()] if link == gains_link else [])))
    return operands


def send(jobs, operands, before=None, anchor=(), gains=None, gains_link=None):
    arrived = []
    for link, (operand, (hop, xor)) in enumerate(zip(operands, LINKS)):
        if operand is None:
            arrived.append(before[link])
            continue
        got = hop(after(operand, *before[link]) if before else operand, xor)
        arrived.append((got,))
        got = after(got, *anchor)
        at = 0
        for r, part, step in takers(jobs, link):
            r.take(part, step, got, at)
            at += r.blocks * (8, 4, 2, 1)[step]
        if link == gains_link:
            gains.held = [(operand, at), (got, at)]
    return arrived


def stage(jobs, before=None, **more):
    return send(jobs, prepare(jobs, **more), before, **more)


def finish(reductions, place_z, plan, before=(), gains=None, anchor=None):
    keep, give = None, None
    give, keep = ends(
        place_z,
        [[r.sum(part, 4) for part in range(4)] for r in reductions],
        gains.terms() if gains else (),
    )
    got = over_z_hi(after(give, *before))
    if anchor is not None:
        got = after(got, anchor)
    outs = place(keep, got, plan)
    if gains:
        total = add(keep[0], got[0])
        total = total + over_core(total)
        outs = (*outs, total + over_z(total))
    return outs


def chip_sums(high, low, *wait):
    rows = low.shape[0] // 2
    got = after(over_core(low), *wait)
    return add(high[:rows], got[:rows]), add(high[rows:], got[rows:])


def per_device(
    tokens,
    attn_gain,
    query_weight,
    key_weight,
    value_weight,
    out_weight,
    mlp_gain,
    gate_weight,
    up_weight,
    down_weight,
    cotangent,
    doc_lengths,
):
    rows = tokens.shape[0]
    place_dp = lax.axis_index("dp")
    place_t = lax.axis_index("tensor")
    place_z = place_dp % 2
    place_xy = jnp.stack((place_dp // 8, (place_dp // 2) % 4))
    q_width = query_weight.shape[1]
    gain_one, gain_two = attn_gain.astype(F32), mlp_gain.astype(F32)

    across = over_z(tokens)
    places = jnp.concatenate(
        [(place_t ^ j) * rows + jnp.arange(rows, dtype=jnp.int32) for j in (0, 2, 1, 3)]
    )
    opening, ending = jnp.zeros_like(places), jnp.int32(0)
    for number in range(doc_lengths.shape[0]):
        ending = ending + doc_lengths[number]
        opening = jnp.maximum(opening, jnp.where(places >= ending, ending, 0))
    cos, sin = rotary_tables(places - opening)
    place_docs = jnp.concatenate((place_t[None], doc_lengths))
    attn_row = attn_gain.reshape(1, -1)
    near = touch(query_weight, out_weight)
    across, cos, sin, place_docs, place_xy, attn_row, near = lax.optimization_barrier(
        (across, cos, sin, place_docs, place_xy, attn_row, near)
    )
    token_blocks = (tokens, across, over_core(tokens), over_core(across))

    cot_across = over_z(after(cotangent, across))
    h1, qkv, heads_out, lse, high, low = attention(
        place_docs, token_blocks, attn_row, query_weight, key_weight, value_weight, out_weight, cos, sin, near
    )
    cot_pair = pair(cotangent, cot_across, low)
    own, other = chip_sums(high, low, cot_pair)
    z_sums = over_z(jnp.concatenate((other.astype(BF), own.astype(BF)), axis=0))
    cot_halves = (cot_pair, over_core(after(cot_pair, own)))
    grad_hidden = [dot_rt(after(half, other), down_weight).astype(BF) for half in cot_halves]
    near = touch(after(gate_weight, *grad_hidden), up_weight)
    z_sums = after(z_sums, near)
    mid = jnp.concatenate((add(tokens, own, z_sums[:rows]), add(across, other, z_sums[rows:])), axis=0)
    normed_two, inverse_two = norm(mid)
    h2 = (normed_two * gain_two).astype(BF)
    h2 = (h2, over_core(h2))
    units = gate_weight.shape[1]
    split = units // 2 // 128 * 128 + 128
    hidden, grad_gate_val, grad_up_val, first = mlp(
        place_xy, h2, grad_hidden, gate_weight, up_weight, cot_halves, near, split
    )
    first_sum = Reduction(first)
    first_links = stage([(first_sum, 0)])
    high, low, gain_two_part, second = mlp_back(
        place_xy, after(grad_gate_val, first[0]), grad_up_val, gate_weight, up_weight, h2, split
    )
    own, other = chip_sums(high, low, *[link[0] for link in first_links])
    second_sum = Reduction(second)
    links = stage([(second_sum, 0)], first_links)
    z_sums = over_z(jnp.concatenate((other.astype(BF), own.astype(BF)), axis=0))
    mlp_part = dot(after(hidden, other, *[link[0] for link in first_links]), down_weight).astype(BF)
    z_sums = after(z_sums, mlp_part, *fold([(first_sum, range(8))]))
    grad_h2 = jnp.concatenate((add(own, z_sums[:rows]), add(other, z_sums[rows:])), axis=0)
    grad_mid = cot_pair.astype(F32) + norm_back(normed_two, inverse_two, gain_two, grad_h2)
    mid_low = grad_mid.astype(BF)
    cut = rows + rows // 2
    mid_low = (mid_low, jnp.concatenate((over_core(mid_low[:cut]), over_core(mid_low[cut:])), axis=0))

    jobs = [(first_sum, 1), (second_sum, 1)]
    operands = prepare(jobs)
    high, low, gains, attn = attention_back(
        place_docs, place_xy, mid_low, after(qkv, *operands), lse, h1, heads_out,
        query_weight, key_weight, value_weight, out_weight, cos, sin, gain_two_part,
    )
    links = send(jobs, operands, links, (low,))
    attn_sum = Reduction(attn, joined=True)
    gains = Gains(gains)
    own, other = chip_sums(high, low, *[link[0] for link in links])
    jobs = [(first_sum, 2), (second_sum, 2), (attn_sum, 0)]
    operands = prepare(jobs, gains, 0)
    folded = fold([(first_sum, "last"), (second_sum, "last")])
    links = send(jobs, operands, links, folded, gains, 0)
    grad_h1 = own + over_z(other.astype(BF)).astype(F32)
    result_got = over_core(after(mlp_part[2 * rows :], grad_h1))
    result_chip = add(mlp_part[: 2 * rows], result_got)
    result_z = over_z(result_chip[rows:].astype(BF))
    result = (mid[:rows] + result_chip[:rows] + result_z.astype(F32)).astype(BF)
    jobs = [(first_sum, 3), (second_sum, 3), (attn_sum, 1)]
    operands = prepare(jobs, gains, 1)
    folded = fold([(first_sum, "own"), (second_sum, "own"), (attn_sum, range(4))])
    links = send(jobs, operands, links, folded, gains, 1)
    place_z = place_z[None]
    blocks, more = first_sum.blocks, second_sum.blocks
    plan = [
        [(0, blocks, 0, units, 0)],
        [(0, blocks, units, split, 0), (2 * blocks, more, 0, units - split, split)],
        [(2 * blocks, more, units - split, units, 0)],
    ]
    out_down, out_gate, out_up = finish([first_sum, second_sum], place_z, plan)
    links = stage([(attn_sum, 2)], links, gains=gains, gains_link=2)
    links = [(*link, result_z) for link in links]
    links = stage([(attn_sum, 3)], links, gains=gains, gains_link=3)
    cuts = ((0, q_width), (q_width, HD), (q_width + HD, HD), (q_width + 2 * HD, q_width))
    plan = [[(1, attn_sum.blocks, first, width, 0)] for first, width in cuts]
    out_query, out_key, out_value, out_out, grad_gains = finish([attn_sum], place_z, plan, [], gains, out_up)
    grad_gains = grad_gains.reshape(2, -1)

    normed, inverse = norm(tokens.astype(F32))
    grad_tokens = grad_mid[:rows] + norm_back(normed, inverse, gain_one, grad_h1)
    return (
        result,
        grad_tokens.astype(BF),
        grad_gains[0] / gain_one,
        out_query,
        out_key,
        out_value,
        out_out.T,
        grad_gains[1] / gain_two,
        out_gate,
        out_up,
        out_down.T,
    )


def solution(mesh):
    in_specs = (
        P(("dp", "tensor"), None),
        P(),
        P(None, "tensor"),
        P(None, "tensor"),
        P(None, "tensor"),
        P("tensor", None),
        P(),
        P(None, "tensor"),
        P(None, "tensor"),
        P("tensor", None),
        P(("dp", "tensor"), None),
        P("dp"),
    )
    out_specs = (
        P(("dp", "tensor"), None),
        P(("dp", "tensor"), None),
        P(),
        P("dp", "tensor"),
        P("dp", "tensor"),
        P("dp", "tensor"),
        P("tensor", "dp"),
        P(),
        P("dp", "tensor"),
        P("dp", "tensor"),
        P("tensor", "dp"),
    )
    return jax.shard_map(
        per_device, mesh=mesh, in_specs=in_specs, out_specs=out_specs, check_vma=False
    )
```

```python
import functools
import math

import jax
import jax.numpy as jnp
from jax import lax
from jax.experimental import pallas as pl
from jax.experimental.pallas import tpu as pltpu
from jax.sharding import PartitionSpec as P

HD = 64
EPSILON = 1e-05
THETA = 10000.0
MASKED = -1000000000.0
BF = jnp.bfloat16
F32 = jnp.float32
MIB = 1024 * 1024


def cost(time):
    return pl.CostEstimate(flops=int(time * 1e9), bytes_accessed=1024, transcendentals=0)


def dot(left, right):
    return jnp.dot(left, right, preferred_element_type=F32)


def dot_t(left, right):
    return lax.dot_general(left, right, (((0,), (0,)), ((), ())), preferred_element_type=F32)


def dot_rt(left, right):
    return lax.dot_general(left, right, (((1,), (1,)), ((), ())), preferred_element_type=F32)


def vmem():
    return pl.BlockSpec(memory_space=pltpu.VMEM)


def smem():
    return pl.BlockSpec(memory_space=pltpu.SMEM)


def hbm():
    return pl.BlockSpec(memory_space=pl.ANY)


def params(size):
    return pltpu.CompilerParams(vmem_limit_bytes=size * MIB)


def swap_halves(values):
    width = values.shape[1]
    lane = lax.broadcasted_iota(jnp.int32, values.shape, 1)
    return jnp.where(
        lane % HD < HD // 2,
        pltpu.roll(values, width - HD // 2, 1),
        pltpu.roll(values, HD // 2, 1),
    )


def wide(table, width):
    return jnp.concatenate([table] * (width // table.shape[1]), axis=1) if width > table.shape[1] else table[:, :width]


def places_of(place_t, ends, rows, shape, axis):
    index = lax.broadcasted_iota(jnp.int32, shape, axis)
    block = index // rows
    order = jnp.where(block == 0, 0, jnp.where(block == 1, 2, jnp.where(block == 2, 1, 3)))
    places = (place_t ^ order) * rows + index % rows
    opening = jnp.zeros(shape, jnp.int32)
    for end in ends:
        opening = jnp.maximum(opening, jnp.where(places >= end, end, 0))
    return places, opening


def doc_ends(place_ref, count):
    ends, total = [], jnp.int32(0)
    for i in range(count):
        total = total + place_ref[1 + i]
        ends.append(total)
    return ends


def attention_kernel(
    docs, place_ref, own, zpart, cpart, diag, gain, wq, wk, wv, wo, cos, sin, near,
    h1_ref, qkv_ref, o_ref, lse_ref, high_ref, low_ref, bias_ref,
):
    rows = own.shape[0]
    every = 4 * rows
    half = 2 * rows
    q_width = wq.shape[1]
    heads = q_width // HD
    gain_row = gain[...].astype(F32)
    for number, block in enumerate((own, zpart, cpart, diag)):
        values = block[...].astype(F32)
        inverse = lax.rsqrt(jnp.mean(values * values, axis=-1, keepdims=True) + EPSILON)
        h1_ref[number * rows : (number + 1) * rows, :] = (values * inverse * gain_row).astype(BF)
    h1 = h1_ref[...]
    joined = jnp.concatenate((wk[...], wv[...]), axis=0)
    table_c, table_s = cos[...], sin[...]

    def rope(values):
        width = values.shape[1]
        return values * wide(table_c, width) + swap_halves(values) * wide(table_s, width)

    scale = 1.0 / math.sqrt(HD)
    kv = dot_rt(h1, joined)
    lane = lax.broadcasted_iota(jnp.int32, kv.shape, 1)
    qkv_ref[:, q_width:] = jnp.where(lane < HD, rope(kv), kv).astype(BF)
    qkv_ref[:, :q_width] = rope(dot(h1, wq[...])).astype(BF)

    ends = doc_ends(place_ref, docs)
    places_q, opening_q = places_of(place_ref[0], ends, rows, (every, 1), 0)
    places_k, _ = places_of(place_ref[0], ends, rows, (1, every), 1)
    bias_ref[...] = jnp.where((places_k <= places_q) & (places_k >= opening_q), 0.0, MASKED)

    keys = qkv_ref[:, q_width : q_width + HD]
    kv_low = qkv_ref[:, q_width:]
    lane = lax.broadcasted_iota(jnp.int32, kv_low.shape, 1)
    ones_vals = jnp.where(lane < HD, jnp.ones_like(kv_low), kv_low)
    lse_lane = lax.broadcasted_iota(jnp.int32, (every, 128), 1)
    lse = jnp.zeros((every, 128), F32)
    for head in range(heads):
        query = qkv_ref[:, head * HD : (head + 1) * HD]
        scores = dot_rt(query, keys) * scale + bias_ref[...]
        highest = jnp.max(scores, axis=-1, keepdims=True)
        raised = jnp.exp(scores - highest)
        mixed = dot(raised.astype(BF), ones_vals)
        totals = mixed[:, :1]
        o_ref[:, head * HD : (head + 1) * HD] = (mixed[:, HD:] / totals).astype(BF)
        lse = jnp.where(lse_lane == head, highest + jnp.log(totals), lse)
    lse_ref[...] = lse.T[:heads, :]
    high_ref[...] = dot(o_ref[:half, :], wo[...])
    low_ref[...] = dot(o_ref[half:, :], wo[...]).astype(BF)


def attention(place_docs, blocks, gain, wq, wk, wv, wo, cos, sin, near):
    rows, width = blocks[0].shape
    every = rows * 4
    q_width = wq.shape[1]
    heads = q_width // HD
    shapes = (
        jax.ShapeDtypeStruct((every, width), BF),
        jax.ShapeDtypeStruct((every, q_width + 2 * HD), BF),
        jax.ShapeDtypeStruct((every, q_width), BF),
        jax.ShapeDtypeStruct((heads, every), F32),
        jax.ShapeDtypeStruct((2 * rows, width), F32),
        jax.ShapeDtypeStruct((2 * rows, width), BF),
    )
    return pl.pallas_call(
        functools.partial(attention_kernel, place_docs.shape[0] - 1),
        out_shape=shapes,
        in_specs=[smem()] + [vmem()] * 12,
        out_specs=[vmem()] * 6,
        scratch_shapes=[pltpu.VMEM((every, every), F32)],
        compiler_params=params(12),
        name="attention",
        cost_estimate=cost(11),
    )(place_docs, *blocks, gain, wq, wk.T, wv.T, wo, cos, sin, near)


SEND = ((1, 2), (3, 2))
KEEP = ((0, 3), (0, 1))


def gradient_body(place_ref, groups, outs, tile=512):
    place_x, place_y = place_ref[0], place_ref[1]
    at = 0
    for lefts, right, begin, width in groups:
        for jx in range(4):
            columns = []
            for jy in range(4):
                start = pl.multiple_of(((place_x ^ jx) * 4 + (place_y ^ jy)) * 128, 128)
                columns.append(jnp.concatenate([left[:, pl.ds(start, 128)] for left in lefts], axis=0))
            left = jnp.concatenate(columns, axis=1)
            for s in range(0, width, tile):
                n = min(tile, width - s)
                cube = dot_t(left, right[:, begin + s : begin + s + n]).astype(BF).reshape(4, 4, 32, n)
                for b in range(n // 128):
                    block = at + s // 128 + b
                    piece = cube[:, :, :, b * 128 : (b + 1) * 128]
                    for part in range(2):
                        for number, slots in enumerate((SEND[part], KEEP[part])):
                            if jx in slots:
                                outs[2 * part + number][slots.index(jx), :, block] = piece[:, part]
                            for slot in range(2):
                                outs[4 + 2 * part + number][slot, jx, block] = piece[slots[slot], 2 + part]
        at += width // 128


def gradient_shapes(width):
    return [jax.ShapeDtypeStruct((2, 4, width // 128, 32, 128), BF)] * 8


def mlp_kernel(tile, split, place_ref, h2_a, h2_b, wg, wu, wd, cot_a, cot_b, near, hid_ref, dgate_ref, dup_ref, *outs):
    units = wg.shape[1]
    h2 = jnp.concatenate((h2_a[...], h2_b[...]), axis=0)
    cot = jnp.concatenate((cot_a[...], cot_b[...]), axis=0)
    for s in range(0, units, tile):
        cut = slice(s, min(s + tile, units))
        gate = dot(h2, wg[:, cut])
        up = dot(h2, wu[:, cut])
        dh = dot_rt(cot, wd[cut, :])
        sig = jax.nn.sigmoid(gate)
        active = gate * sig
        hid_ref[:, cut] = (active * up).astype(BF)
        dgate_ref[:, cut] = (dh * up * (sig + active * (1.0 - sig))).astype(BF)
        dup_ref[:, cut] = (dh * active).astype(BF)
    gradient_body(place_ref, [((cot_a, cot_b), hid_ref, 0, units), ((h2_a, h2_b), dgate_ref, 0, split)], outs)


def mlp(place_xy, h2_halves, wg, wu, wd, cot_halves, near, split, tile=512):
    half, width = h2_halves[0].shape
    every = 2 * half
    units = wg.shape[1]
    got = pl.pallas_call(
        functools.partial(mlp_kernel, tile, split),
        out_shape=[jax.ShapeDtypeStruct((every, units), BF)] * 3 + gradient_shapes(units + split),
        in_specs=[smem()] + [vmem()] * 8,
        out_specs=[vmem()] * 11,
        compiler_params=params(14),
        name="mlp",
        cost_estimate=cost(18),
    )(place_xy, *h2_halves, wg, wu, wd, *cot_halves, near)
    return (*got[:3], got[3:])


def mlp_back_kernel(step, split, place_ref, hid, dgate, dup, wg, wu, wd, h2_a, h2_b, high_ref, low_ref, gain_ref, out_ref, *outs):
    half, width = h2_a.shape
    for s in range(0, width, step):
        cut = slice(s, s + step)
        part = dot_rt(dgate[...], wg[cut, :]) + dot_rt(dup[...], wu[cut, :])
        high_ref[:, cut] = part[:half]
        low_ref[:, cut] = part[half:].astype(BF)
        gain_ref[:, cut] = jnp.sum(part[:half] * h2_a[:, cut].astype(F32), axis=0, keepdims=True) + jnp.sum(
            part[half:] * h2_b[:, cut].astype(F32), axis=0, keepdims=True
        )
        out_ref[:, cut] = dot(hid[...], wd[:, cut]).astype(BF)
    units = dup.shape[1]
    lefts = (h2_a, h2_b)
    gradient_body(place_ref, [(lefts, dgate, split, units - split), (lefts, dup, 0, units)], outs)


def mlp_back(place_xy, hid, dgate, dup, wg, wu, wd, h2_halves, split, step=512):
    half, width = h2_halves[0].shape
    got = pl.pallas_call(
        functools.partial(mlp_back_kernel, step, split),
        out_shape=[
            jax.ShapeDtypeStruct((half, width), F32),
            jax.ShapeDtypeStruct((half, width), BF),
            jax.ShapeDtypeStruct((1, width), F32),
            jax.ShapeDtypeStruct((2 * half, width), BF),
        ]
        + gradient_shapes(2 * wg.shape[1] - split),
        in_specs=[smem()] + [vmem()] * 8,
        out_specs=[vmem()] * 12,
        compiler_params=params(12),
        name="mlp_back",
        cost_estimate=cost(18),
    )(place_xy, hid, dgate, dup, wg, wu, wd, *h2_halves)
    return (*got[:4], got[4:])


def touch_kernel(*refs):
    *sources, target = refs
    total = jnp.zeros(target.shape, F32)
    for source in sources:
        total = total + source[:16, :128].astype(F32)
    target[...] = total


def touch(*arrays):
    return pl.pallas_call(
        touch_kernel,
        out_shape=jax.ShapeDtypeStruct((16, 128), F32),
        in_specs=[vmem()] * len(arrays),
        out_specs=vmem(),
        compiler_params=params(12),
        name="touch",
        cost_estimate=cost(2),
    )(*arrays)


def pair_kernel(above, below, later, target):
    rows = above.shape[0]
    target[:rows] = above[...]
    target[rows:] = below[...]


def pair(above, below, later):
    rows, width = above.shape
    return pl.pallas_call(
        pair_kernel,
        out_shape=jax.ShapeDtypeStruct((2 * rows, width), above.dtype),
        in_specs=[vmem()] * 2 + [pl.BlockSpec(memory_space=pl.ANY)],
        out_specs=vmem(),
        compiler_params=params(4),
        name="pair",
        cost_estimate=cost(8),
    )(above, below, later)


def chip_kernel(high, got, *refs):
    total = high[...] + got[...].astype(F32)
    rows = total.shape[0] // 2
    chip, send = refs
    chip[...] = total[: chip.shape[0]]
    send[:rows] = total[rows:].astype(BF)
    if send.shape[0] > rows:
        send[rows:] = total[:rows].astype(BF)


def chip_sums(high, got, both=True):
    rows, width = high.shape[0] // 2, high.shape[1]
    count = 2 * rows if both else rows
    return pl.pallas_call(
        chip_kernel,
        out_shape=(jax.ShapeDtypeStruct((count, width), F32), jax.ShapeDtypeStruct((count, width), BF)),
        in_specs=[vmem()] * 2,
        out_specs=[vmem()] * 2,
        compiler_params=params(6),
        name="chip_sums",
        cost_estimate=cost(1),
    )(high, got)


def middle_kernel(own, across, chip, got, gain, mid_ref, h2_ref):
    mid = jnp.concatenate((own[...], across[...]), axis=0).astype(F32) + chip[...] + got[...].astype(F32)
    inverse = lax.rsqrt(jnp.mean(mid * mid, axis=-1, keepdims=True) + EPSILON)
    mid_ref[...] = mid
    h2_ref[...] = (mid * inverse * gain[...].astype(F32)).astype(BF)


def middle(own, across, chip, got, gain):
    return pl.pallas_call(
        middle_kernel,
        out_shape=(jax.ShapeDtypeStruct(chip.shape, F32), jax.ShapeDtypeStruct(chip.shape, BF)),
        in_specs=[vmem()] * 5,
        out_specs=[vmem()] * 2,
        compiler_params=params(8),
        name="middle",
        cost_estimate=cost(2),
    )(own, across, chip, got, gain)


def middle_back_kernel(mid_ref, cot, chip, got, gain, own, top, rest):
    mid = mid_ref[...]
    inverse = lax.rsqrt(jnp.mean(mid * mid, axis=-1, keepdims=True) + EPSILON)
    normed = mid * inverse
    scaled = (chip[...] + got[...].astype(F32)) * gain[...].astype(F32)
    grad = cot[...].astype(F32) + inverse * (scaled - normed * jnp.mean(scaled * normed, axis=-1, keepdims=True))
    own[...] = grad[: own.shape[0]]
    top[...] = grad[: top.shape[0]].astype(BF)
    rest[...] = grad[top.shape[0] :].astype(BF)


def middle_back(mid, cot, chip, got, gain, cut):
    half, width = mid.shape
    return pl.pallas_call(
        middle_back_kernel,
        out_shape=(
            jax.ShapeDtypeStruct((half // 2, width), F32),
            jax.ShapeDtypeStruct((cut, width), BF),
            jax.ShapeDtypeStruct((half - cut, width), BF),
        ),
        in_specs=[vmem()] * 5,
        out_specs=[vmem()] * 3,
        compiler_params=params(8),
        name="middle_back",
        cost_estimate=cost(2),
    )(mid, cot, chip, got, gain)


def combine_kernel(sums, *refs):
    out = refs[-1]
    at = 0
    for count, terms in sums:
        total = None
        for number, start in terms:
            term = refs[number][start : start + count].astype(F32)
            total = term if total is None else total + term
        out[at : at + count] = total.astype(out.dtype)
        at += count


def combine(sums):
    arrays, plan = [], []
    for terms in sums:
        listed = []
        for array, start, count in terms:
            known = [i for i, a in enumerate(arrays) if a is array]
            if not known:
                arrays.append(array)
            listed.append((known[0] if known else len(arrays) - 1, start))
        plan.append((terms[0][2], listed))
    total = sum(count for count, _ in plan)
    return pl.pallas_call(
        functools.partial(combine_kernel, plan),
        out_shape=jax.ShapeDtypeStruct((total, 32, 128), BF),
        in_specs=[vmem()] * len(arrays),
        out_specs=vmem(),
        compiler_params=params(8),
        name="combine",
        cost_estimate=cost(0.5),
    )(*arrays)


def ends_kernel(sums, extra, place_ref, *refs):
    give, keep = refs[-2:]
    at = 0
    if extra:
        total = None
        for number, start in extra:
            term = refs[number][start : start + 1].astype(F32)
            total = term if total is None else total + term
        give[0:1] = total.astype(BF)
        keep[0:1] = total.astype(BF).astype(F32)
        at = 1
    for parts in sums:
        count = parts[0][0]
        totals = []
        for _, terms in parts:
            total = None
            for number, start in terms:
                term = refs[number][start : start + count].astype(F32)
                total = term if total is None else total + term
            totals.append(total)
        for half in range(2):
            cut = slice(at, at + count)
            give[cut] = jnp.where(place_ref[2] == 0, totals[2 + half], totals[half]).astype(BF)
            keep[cut] = jnp.where(place_ref[2] == 0, totals[half], totals[2 + half])
            at += count


def ends(place, sums, extra=()):
    arrays, plan = [], []
    for parts in sums:
        planned = []
        for terms in parts:
            listed = []
            for array, start, count in terms:
                known = [i for i, a in enumerate(arrays) if a is array]
                if not known:
                    arrays.append(array)
                listed.append((known[0] if known else len(arrays) - 1, start))
            planned.append((terms[0][2], listed))
        plan.append(planned)
    arrays += [array for array, _, _ in extra]
    more = [(len(arrays) - len(extra) + i, start) for i, (_, start, _) in enumerate(extra)]
    total = sum(2 * parts[0][0] for parts in plan) + bool(extra)
    return pl.pallas_call(
        functools.partial(ends_kernel, plan, more),
        out_shape=(jax.ShapeDtypeStruct((total, 32, 128), BF), jax.ShapeDtypeStruct((total, 32, 128), F32)),
        in_specs=[smem()] + [vmem()] * len(arrays),
        out_specs=[vmem()] * 2,
        compiler_params=params(16),
        name="ends",
        cost_estimate=cost(1),
    )(place, *arrays)


def attention_back_kernel(
    docs, place_ref, place_xy, mid_a, mid_b, mid_c, mid_d, qkv, lse_ref, h1, o_ref, wq, wk, wv, wo, cos, sin, gain_two, *refs
):
    dqkv_ref, high_ref, low_ref, gains, *outs, bias_ref, do_ref = refs
    half = mid_a.shape[0] + mid_b.shape[0]
    rows, every = half // 2, 2 * half
    q_width = wq.shape[1]
    heads = q_width // HD
    width = wq.shape[0]
    scale = 1.0 / math.sqrt(HD)
    mid = jnp.concatenate((mid_a[...], mid_b[...], mid_c[...], mid_d[...]), axis=0)
    do_ref[...] = dot_rt(mid, wo[...]).astype(BF)
    ends = doc_ends(place_ref, docs)
    places_q, opening_q = places_of(place_ref[0], ends, rows, (1, every), 1)
    places_k, _ = places_of(place_ref[0], ends, rows, (every, 1), 0)
    bias_ref[...] = jnp.where((places_k <= places_q) & (places_k >= opening_q), 0.0, MASKED)
    keys = qkv[:, q_width : q_width + HD]
    vals = qkv[:, q_width + HD : q_width + 2 * HD]
    dk = jnp.zeros((every, HD), F32)
    dv = jnp.zeros((every, HD), F32)
    table_c, table_s = cos[...], sin[...]

    def unrope(values):
        wide_now = values.shape[1]
        return values * wide(table_c, wide_now) - swap_halves(values) * wide(table_s, wide_now)

    for pair in range(heads // 2):
        dqs = []
        for head in (2 * pair, 2 * pair + 1):
            cut = slice(head * HD, (head + 1) * HD)
            query = qkv[:, cut]
            grad_o = do_ref[:, cut]
            scores = dot_rt(keys, query) * scale + bias_ref[...]
            chances = jnp.exp(scores - lse_ref[head : head + 1, :])
            grad_chances = dot_rt(vals, grad_o)
            centre = jnp.sum(chances * grad_chances, axis=0, keepdims=True)
            grad_scores = (chances * (grad_chances - centre)).astype(BF)
            dv = dv + dot(chances.astype(BF), grad_o)
            dk = dk + dot(grad_scores, query)
            dqs.append(dot_t(grad_scores, keys))
        dq = jnp.concatenate(dqs, axis=1) * scale
        dqkv_ref[:, pair * 2 * HD : (pair + 1) * 2 * HD] = unrope(dq).astype(BF)
    both = jnp.concatenate((dk * scale, dv), axis=1)
    lane = lax.broadcasted_iota(jnp.int32, both.shape, 1)
    dqkv_ref[:, q_width:] = jnp.where(lane < HD, unrope(both), both).astype(BF)
    joined = jnp.concatenate((wk[...], wv[...]), axis=0)
    step = 512
    for s in range(0, width, step):
        part = dot_rt(dqkv_ref[:, :q_width], wq[s : s + step, :]) + dot(dqkv_ref[:, q_width:], joined[:, s : s + step])
        high_ref[:, s : s + step] = part[:half]
        low_ref[:, s : s + step] = part[half:].astype(BF)
        gain_one = jnp.sum(part * h1[:, s : s + step].astype(F32), axis=0, keepdims=True)
        for lane in range(0, step, 128):
            row = (s + lane) // 128
            gains[0, row : row + 1, :] = gain_one[:, lane : lane + 128]
            gains[0, width // 128 + row : width // 128 + row + 1, :] = gain_two[:, s + lane : s + lane + 128]
    gradient_body(place_xy, [((h1,), dqkv_ref, 0, q_width + 2 * HD), ((mid_a, mid_b, mid_c, mid_d), o_ref, 0, q_width)], outs)


def attention_back(place_docs, place_xy, mids, qkv, lse, h1, o, wq, wk, wv, wo, cos, sin, gain_two_part):
    half, width = mids[0].shape[0] + mids[1].shape[0], mids[0].shape[1]
    every = 2 * half
    q_width = wq.shape[1]
    got = pl.pallas_call(
        functools.partial(attention_back_kernel, place_docs.shape[0] - 1),
        out_shape=[
            jax.ShapeDtypeStruct((every, q_width + 2 * HD), BF),
            jax.ShapeDtypeStruct((half, width), F32),
            jax.ShapeDtypeStruct((half, width), BF),
            jax.ShapeDtypeStruct((1, width // 64, 128), F32),
        ]
        + gradient_shapes(2 * q_width + 2 * HD),
        in_specs=[smem()] * 2 + [vmem()] * 15,
        out_specs=[vmem()] * 12,
        scratch_shapes=[
            pltpu.VMEM((every, every), F32),
            pltpu.VMEM((every, q_width), BF),
        ],
        compiler_params=params(12),
        name="attention_back",
        cost_estimate=cost(19),
    )(place_docs, place_xy, *mids, qkv, lse, h1, o, wq, wk.T, wv.T, wo, cos, sin, gain_two_part)
    return (*got[1:4], got[4:])


def lay_out_kernel(plan, keep, got, *outs):
    for out, parts in zip(outs, plan):
        for start, blocks, first, width, to in parts:
            for half in range(2):
                for b in range(blocks):
                    low, high = max(128 * b, first), min(128 * (b + 1), first + width)
                    if low >= high:
                        continue
                    at = start + half * blocks + b
                    total = keep[at] + got[at].astype(F32)
                    out[32 * half : 32 * (half + 1), to + low - first : to + high - first] = total[:, low - 128 * b : high - 128 * b]


def lay_out(keep, got, plan):
    widths = [sum(part[3] for part in parts) for parts in plan]
    return pl.pallas_call(
        functools.partial(lay_out_kernel, plan),
        out_shape=[jax.ShapeDtypeStruct((64, width), F32) for width in widths],
        in_specs=[vmem()] * 2,
        out_specs=[vmem()] * len(plan),
        compiler_params=params(12),
        name="lay_out",
        cost_estimate=cost(1),
    )(keep, got)


def rotary_tables(offset):
    half_size = HD // 2
    freqs = THETA ** (-(jnp.arange(half_size, dtype=F32) * 2.0 / HD))
    angles = offset.astype(F32)[:, None] * freqs[None, :]
    cosine, sine = jnp.cos(angles), jnp.sin(angles)
    return jnp.concatenate((cosine,) * 4, axis=1), jnp.concatenate((-sine, sine) * 2, axis=1)


def over_core(values):
    return lax.ppermute(values, "tensor", [(t, t ^ 1) for t in range(4)])


def over_z(values):
    return lax.ppermute(values, "tensor", [(t, t ^ 2) for t in range(4)])


def over_diagonal(values):
    return lax.ppermute(values, "tensor", [(t, t ^ 3) for t in range(4)])


def over_x(values, xor):
    return lax.ppermute(values, "dp", [(d, d ^ (xor * 8)) for d in range(32)])


def over_y(values, xor):
    return lax.ppermute(values, "dp", [(d, d ^ (xor * 2)) for d in range(32)])


def over_z_hi(values):
    return lax.ppermute(values, "dp", [(d, d ^ 1) for d in range(32)])


def after(value, *others):
    return lax.optimization_barrier((value, *others))[0] if others else value


def add(*terms):
    total = terms[0].astype(F32)
    for term in terms[1:]:
        total = total + term.astype(F32)
    return total


def norm(values):
    inverse = lax.rsqrt(jnp.mean(values * values, axis=-1, keepdims=True) + EPSILON)
    return values * inverse, inverse


def norm_back(normed, inverse, gain, grads):
    scaled = grads * gain
    return inverse * (scaled - normed * jnp.mean(scaled * normed, axis=-1, keepdims=True))


LINKS = ((over_x, 1), (over_x, 3), (over_y, 1), (over_y, 3))
ROUTES = ((0, 1, 2, 3), (1, 0, 3, 2), (2, 3, 0, 1), (3, 2, 1, 0))


class Reduction:
    def __init__(self, arrays, joined=False):
        self.joined = joined
        self.blocks = arrays[0].shape[2]
        self.sends = [arrays[2 * part].reshape(-1, 32, 128) for part in range(4)]
        self.kept = [[(arrays[2 * part + 1].reshape(-1, 32, 128), self.starts(0, 8))] for part in range(4)]
        self.near, self.far, self.last = {}, {}, {}

    def starts(self, at, rows):
        return {row: at + row * self.blocks for row in range(rows)}

    def route(self, part, step):
        return ROUTES[part - part % 2 if self.joined and step >= 2 else part][step]

    def order(self, part):
        return ((1, 3), (3, 1))[0 if self.joined else part % 2]

    def row(self, part, row, rows=1):
        return [(array, starts[row], rows * self.blocks) for array, starts in self.kept[part]]

    def sum(self, part, step):
        first, second = self.order(part)
        if step == 0:
            return [(self.sends[part], 0, 8 * self.blocks)]
        if step == 1:
            return self.row(part, 4, 4)
        if step == 2:
            return self.row(part, min(first, 2), 2)
        if step == 3:
            return self.row(part, second) + [self.far[part]]
        return self.row(part, 0) + self.near.get(part, []) + [self.last[part]]

    def take(self, part, step, got, at):
        n = self.blocks
        if step < 2:
            self.kept[part].append((got, self.starts(at, 8 - 4 * step)))
        elif step == 2:
            near, far = (0, 1) if self.order(part)[0] == 1 else (1, 0)
            self.near[part] = [(got, at + near * n, n)]
            self.far[part] = (got, at + far * n, n)
        else:
            self.last[part] = (got, at, n)


def fold(jobs):
    folded = []
    for part in range(4):
        sums, places = [], []
        at = 0
        for r, rows in jobs:
            rows = {"last": (0, r.order(part)[1]), "own": (0,)}.get(rows, rows)
            starts = {}
            for row in rows:
                terms = r.row(part, row)
                if row == 0:
                    terms = terms + r.near.get(part, [])
                sums.append(terms)
                starts[row] = at
                at += r.blocks
            r.near.pop(part, None)
            places.append((r, starts))
        array = combine(sums)
        folded.append(array)
        for r, starts in places:
            r.kept[part] = [(array, starts)]
    return folded


class Gains:
    def __init__(self, block):
        self.held = [(block, 0)]

    def terms(self):
        return [(array, start, 1) for array, start in self.held]

    def exchange(self, hop, before):
        sent = sum(array[start : start + 1].astype(F32) for array, start in self.held).astype(BF)
        self.held = [(sent, 0), (hop(after(sent, *before)), 0)]


def takers(jobs, link):
    return [(r, part, step) for r, step in jobs for part in range(4) if r.route(part, step) == link]


def prepare(jobs, gains=None, gains_link=None):
    operands = []
    for link in range(4):
        taken = takers(jobs, link)
        if not taken:
            operands.append(None)
            continue
        if len(taken) == 1 and taken[0][2] == 0:
            operands.append(taken[0][0].sends[taken[0][1]])
            continue
        sums = [r.sum(part, step) for r, part, step in taken]
        operands.append(combine(sums + ([gains.terms()] if link == gains_link else [])))
    return operands


def send(jobs, operands, before=None, anchor=(), gains=None, gains_link=None):
    arrived = []
    for link, (operand, (hop, xor)) in enumerate(zip(operands, LINKS)):
        if operand is None:
            arrived.append(before[link])
            continue
        got = hop(after(operand, *before[link]) if before else operand, xor)
        arrived.append((got,))
        got = after(got, *anchor)
        at = 0
        for r, part, step in takers(jobs, link):
            r.take(part, step, got, at)
            at += r.blocks * (8, 4, 2, 1)[step]
        if link == gains_link:
            gains.held = [(operand, at), (got, at)]
    return arrived


def stage(jobs, before=None, **more):
    return send(jobs, prepare(jobs, **more), before, **more)


def finish(reductions, place, plan, before=(), gains=None, anchor=None):
    keep, give = None, None
    give, keep = ends(
        place,
        [[r.sum(part, 4) for part in range(4)] for r in reductions],
        gains.terms() if gains else (),
    )
    got = over_z_hi(after(give, *before))
    if anchor is not None:
        got = after(got, anchor)
    outs = lay_out(keep, got, plan)
    if gains:
        total = add(keep[0], got[0])
        outs = (*outs, (total + over_core(total)) + (over_z(total) + over_diagonal(total)))
    return outs


def per_device(
    tokens,
    attn_gain,
    query_weight,
    key_weight,
    value_weight,
    out_weight,
    mlp_gain,
    gate_weight,
    up_weight,
    down_weight,
    cotangent,
    doc_lengths,
):
    rows = tokens.shape[0]
    place_dp = lax.axis_index("dp")
    place_t = lax.axis_index("tensor")
    place_xy = jnp.stack((place_dp // 8, (place_dp // 2) % 4, place_dp % 2))
    q_width = query_weight.shape[1]
    gain_one, gain_two = attn_gain.astype(F32), mlp_gain.astype(F32)

    across = over_z(tokens)
    places = jnp.concatenate(
        [(place_t ^ j) * rows + jnp.arange(rows, dtype=jnp.int32) for j in (0, 2, 1, 3)]
    )
    opening, ending = jnp.zeros_like(places), jnp.int32(0)
    for number in range(doc_lengths.shape[0]):
        ending = ending + doc_lengths[number]
        opening = jnp.maximum(opening, jnp.where(places >= ending, ending, 0))
    cos, sin = rotary_tables(places - opening)
    place_docs = jnp.concatenate((place_t[None], doc_lengths))
    attn_row, mlp_row = attn_gain.reshape(1, -1), mlp_gain.reshape(1, -1)
    near = touch(query_weight, out_weight)
    across, cos, sin, place_docs, place_xy, attn_row, mlp_row, near = lax.optimization_barrier(
        (across, cos, sin, place_docs, place_xy, attn_row, mlp_row, near)
    )
    token_blocks = (tokens, across, over_core(tokens), over_core(across))

    cot_across = over_z(after(cotangent, across))
    h1, qkv, heads_out, lse, high, low = attention(
        place_docs, token_blocks, attn_row, query_weight, key_weight, value_weight, out_weight, cos, sin, near
    )
    cot_pair = pair(cotangent, cot_across, low)
    chip, low = chip_sums(high, after(over_core(low), cot_pair))
    z_sums = over_z(low)
    cot_halves = (cot_pair, over_core(after(cot_pair, chip)))
    near = touch(after(gate_weight, cot_halves[1]), up_weight, down_weight)
    mid, h2 = middle(tokens, across, chip, after(z_sums, near), mlp_row)
    h2 = (h2, over_core(h2))
    units = gate_weight.shape[1]
    split = units // 2 // 128 * 128 + 128
    hidden, grad_gate_val, grad_up_val, first = mlp(
        place_xy, h2, gate_weight, up_weight, down_weight, cot_halves, near, split
    )
    first_sum = Reduction(first)
    first_links = stage([(first_sum, 0)])
    high, low, gain_two_part, mlp_part, second = mlp_back(
        place_xy, hidden, after(grad_gate_val, first[0]), grad_up_val, gate_weight, up_weight, down_weight, h2, split
    )
    chip, low = chip_sums(high, after(over_core(low), *[link[0] for link in first_links]))
    second_sum = Reduction(second)
    links = stage([(second_sum, 0)], first_links)
    z_sums = after(over_z(low), *fold([(first_sum, range(8))]))
    grad_own, *mid_low = middle_back(mid, cot_pair, chip, z_sums, mlp_row, rows + rows // 2)
    mid_low = (*mid_low, over_core(mid_low[0]), over_core(mid_low[1]))

    jobs = [(first_sum, 1), (second_sum, 1)]
    operands = prepare(jobs)
    high, low, gains, attn = attention_back(
        place_docs, place_xy, mid_low, after(qkv, *operands), lse, h1, heads_out,
        query_weight, key_weight, value_weight, out_weight, cos, sin, gain_two_part,
    )
    links = send(jobs, operands, links, (low,))
    attn_sum = Reduction(attn, joined=True)
    gains = Gains(gains)
    own, other = chip_sums(high, after(over_core(low), *[link[0] for link in links]), False)
    jobs = [(first_sum, 2), (second_sum, 2), (attn_sum, 0)]
    operands = prepare(jobs, gains, 0)
    folded = fold([(first_sum, "last"), (second_sum, "last")])
    links = send(jobs, operands, links, folded, gains, 0)
    grad_h1 = own + over_z(other).astype(F32)
    result_got = over_core(after(mlp_part[2 * rows :], grad_h1))
    result_chip = add(mlp_part[: 2 * rows], result_got)
    result_z = over_z(result_chip[rows:].astype(BF))
    result = (mid[:rows] + result_chip[:rows] + result_z.astype(F32)).astype(BF)
    jobs = [(first_sum, 3), (second_sum, 3), (attn_sum, 1)]
    operands = prepare(jobs, gains, 1)
    folded = fold([(first_sum, "own"), (second_sum, "own"), (attn_sum, range(4))])
    links = send(jobs, operands, links, folded, gains, 1)
    blocks, more = first_sum.blocks, second_sum.blocks
    plan = [
        [(0, blocks, 0, units, 0)],
        [(0, blocks, units, split, 0), (2 * blocks, more, 0, units - split, split)],
        [(2 * blocks, more, units - split, units, 0)],
    ]
    out_down, out_gate, out_up = finish([first_sum, second_sum], place_xy, plan)
    links = stage([(attn_sum, 2)], links, gains=gains, gains_link=2)
    links = [(*link, result_z) for link in links]
    links = stage([(attn_sum, 3)], links, gains=gains, gains_link=3)
    cuts = ((0, q_width), (q_width, HD), (q_width + HD, HD), (q_width + 2 * HD, q_width))
    plan = [[(1, attn_sum.blocks, first, width, 0)] for first, width in cuts]
    out_query, out_key, out_value, out_out, grad_gains = finish([attn_sum], place_xy, plan, [], gains, out_up)
    grad_gains = grad_gains.reshape(2, -1)

    normed, inverse = norm(tokens.astype(F32))
    grad_tokens = grad_own + norm_back(normed, inverse, gain_one, grad_h1)
    return (
        result,
        grad_tokens.astype(BF),
        grad_gains[0] / gain_one,
        out_query,
        out_key,
        out_value,
        out_out.T,
        grad_gains[1] / gain_two,
        out_gate,
        out_up,
        out_down.T,
    )


def solution(mesh):
    in_specs = (
        P(("dp", "tensor"), None),
        P(),
        P(None, "tensor"),
        P(None, "tensor"),
        P(None, "tensor"),
        P("tensor", None),
        P(),
        P(None, "tensor"),
        P(None, "tensor"),
        P("tensor", None),
        P(("dp", "tensor"), None),
        P("dp"),
    )
    out_specs = (
        P(("dp", "tensor"), None),
        P(("dp", "tensor"), None),
        P(),
        P("dp", "tensor"),
        P("dp", "tensor"),
        P("dp", "tensor"),
        P("tensor", "dp"),
        P(),
        P("dp", "tensor"),
        P("dp", "tensor"),
        P("tensor", "dp"),
    )
    return jax.shard_map(
        per_device, mesh=mesh, in_specs=in_specs, out_specs=out_specs, check_vma=False
    )
```

```python
import functools
import math

import jax
import jax.numpy as jnp
from jax import lax
from jax.experimental import pallas as pl
from jax.experimental.pallas import tpu as pltpu
from jax.sharding import PartitionSpec as P

HD = 64
EPSILON = 1e-05
THETA = 10000.0
MASKED = -1000000000.0
BF = jnp.bfloat16
F32 = jnp.float32
MIB = 1024 * 1024


def cost(time):
    return pl.CostEstimate(flops=int(time * 1e9), bytes_accessed=1024, transcendentals=0)


def dot(left, right):
    return jnp.dot(left, right, preferred_element_type=F32)


def dot_t(left, right):
    return lax.dot_general(left, right, (((0,), (0,)), ((), ())), preferred_element_type=F32)


def dot_rt(left, right):
    return lax.dot_general(left, right, (((1,), (1,)), ((), ())), preferred_element_type=F32)


def vmem():
    return pl.BlockSpec(memory_space=pltpu.VMEM)


def smem():
    return pl.BlockSpec(memory_space=pltpu.SMEM)


def hbm():
    return pl.BlockSpec(memory_space=pl.ANY)


def params(size):
    return pltpu.CompilerParams(vmem_limit_bytes=size * MIB)


def swap_halves(values):
    width = values.shape[1]
    lane = lax.broadcasted_iota(jnp.int32, values.shape, 1)
    return jnp.where(
        lane % HD < HD // 2,
        pltpu.roll(values, width - HD // 2, 1),
        pltpu.roll(values, HD // 2, 1),
    )


def wide(table, width):
    return jnp.concatenate([table] * (width // table.shape[1]), axis=1) if width > table.shape[1] else table[:, :width]


def places_of(place_t, ends, rows, shape, axis):
    index = lax.broadcasted_iota(jnp.int32, shape, axis)
    block = index // rows
    order = jnp.where(block == 0, 0, jnp.where(block == 1, 2, jnp.where(block == 2, 1, 3)))
    places = (place_t ^ order) * rows + index % rows
    opening = jnp.zeros(shape, jnp.int32)
    for end in ends:
        opening = jnp.maximum(opening, jnp.where(places >= end, end, 0))
    return places, opening


def doc_ends(place_ref, count):
    ends, total = [], jnp.int32(0)
    for i in range(count):
        total = total + place_ref[1 + i]
        ends.append(total)
    return ends


def attention_kernel(
    docs, place_ref, own, zpart, cpart, diag, gain, wq, wk, wv, wo, cos, sin, near,
    h1_ref, qkv_ref, o_ref, lse_ref, high_ref, low_ref, bias_ref,
):
    rows = own.shape[0]
    every = 4 * rows
    half = 2 * rows
    q_width = wq.shape[1]
    heads = q_width // HD
    gain_row = gain[...].astype(F32)
    for number, block in enumerate((own, zpart, cpart, diag)):
        values = block[...].astype(F32)
        inverse = lax.rsqrt(jnp.mean(values * values, axis=-1, keepdims=True) + EPSILON)
        h1_ref[number * rows : (number + 1) * rows, :] = (values * inverse * gain_row).astype(BF)
    h1 = h1_ref[...]
    joined = jnp.concatenate((wk[...], wv[...]), axis=0)
    table_c, table_s = cos[...], sin[...]

    def rope(values):
        width = values.shape[1]
        return values * wide(table_c, width) + swap_halves(values) * wide(table_s, width)

    scale = 1.0 / math.sqrt(HD)
    kv = dot_rt(h1, joined)
    lane = lax.broadcasted_iota(jnp.int32, kv.shape, 1)
    qkv_ref[:, q_width:] = jnp.where(lane < HD, rope(kv), kv).astype(BF)
    qkv_ref[:, :q_width] = rope(dot(h1, wq[...])).astype(BF)

    ends = doc_ends(place_ref, docs)
    places_q, opening_q = places_of(place_ref[0], ends, rows, (every, 1), 0)
    places_k, _ = places_of(place_ref[0], ends, rows, (1, every), 1)
    bias_ref[...] = jnp.where((places_k <= places_q) & (places_k >= opening_q), 0.0, MASKED)

    keys = qkv_ref[:, q_width : q_width + HD]
    kv_low = qkv_ref[:, q_width:]
    lane = lax.broadcasted_iota(jnp.int32, kv_low.shape, 1)
    ones_vals = jnp.where(lane < HD, jnp.ones_like(kv_low), kv_low)
    lse_lane = lax.broadcasted_iota(jnp.int32, (every, 128), 1)
    lse = jnp.zeros((every, 128), F32)
    for head in range(heads):
        query = qkv_ref[:, head * HD : (head + 1) * HD]
        scores = dot_rt(query, keys) * scale + bias_ref[...]
        highest = jnp.max(scores, axis=-1, keepdims=True)
        raised = jnp.exp(scores - highest)
        mixed = dot(raised.astype(BF), ones_vals)
        totals = mixed[:, :1]
        o_ref[:, head * HD : (head + 1) * HD] = (mixed[:, HD:] / totals).astype(BF)
        lse = jnp.where(lse_lane == head, highest + jnp.log(totals), lse)
    lse_ref[...] = lse.T[:heads, :]
    high_ref[...] = dot(o_ref[:half, :], wo[...])
    low_ref[...] = dot(o_ref[half:, :], wo[...]).astype(BF)


def attention(place_docs, blocks, gain, wq, wk, wv, wo, cos, sin, near):
    rows, width = blocks[0].shape
    every = rows * 4
    q_width = wq.shape[1]
    heads = q_width // HD
    shapes = (
        jax.ShapeDtypeStruct((every, width), BF),
        jax.ShapeDtypeStruct((every, q_width + 2 * HD), BF),
        jax.ShapeDtypeStruct((every, q_width), BF),
        jax.ShapeDtypeStruct((heads, every), F32),
        jax.ShapeDtypeStruct((2 * rows, width), F32),
        jax.ShapeDtypeStruct((2 * rows, width), BF),
    )
    return pl.pallas_call(
        functools.partial(attention_kernel, place_docs.shape[0] - 1),
        out_shape=shapes,
        in_specs=[smem()] + [vmem()] * 12,
        out_specs=[vmem()] * 6,
        scratch_shapes=[pltpu.VMEM((every, every), F32)],
        compiler_params=params(12),
        name="attention",
        cost_estimate=cost(11),
    )(place_docs, *blocks, gain, wq, wk.T, wv.T, wo, cos, sin, near)


SEND = ((1, 2), (3, 2))
KEEP = ((0, 3), (0, 1))


def rows_of(block, cut):
    if isinstance(block, tuple):
        ref, first, rows = block
        return ref[first : first + rows, cut]
    return block[:, cut]


def gradient_body(place_ref, groups, outs, tile=512):
    place_x, place_y = place_ref[0], place_ref[1]
    at = 0
    for lefts, rights, begin, width in groups:
        for jx in range(4):
            columns = []
            for jy in range(4):
                start = pl.multiple_of(((place_x ^ jx) * 4 + (place_y ^ jy)) * 128, 128)
                columns.append(jnp.concatenate([rows_of(left, pl.ds(start, 128)) for left in lefts], axis=0))
            left = jnp.concatenate(columns, axis=1)
            for s in range(0, width, tile):
                n = min(tile, width - s)
                right = jnp.concatenate([rows_of(block, slice(begin + s, begin + s + n)) for block in rights], axis=0)
                cube = dot_t(left, right).astype(BF).reshape(4, 4, 32, n)
                for b in range(n // 128):
                    block = at + s // 128 + b
                    piece = cube[:, :, :, b * 128 : (b + 1) * 128]
                    for part in range(2):
                        for number, slots in enumerate((SEND[part], KEEP[part])):
                            if jx in slots:
                                outs[2 * part + number][slots.index(jx), :, block] = piece[:, part]
                            for slot in range(2):
                                outs[4 + 2 * part + number][slot, jx, block] = piece[slots[slot], 2 + part]
        at += width // 128


def gradient_shapes(width):
    return [jax.ShapeDtypeStruct((2, 4, width // 128, 32, 128), BF)] * 8


def hidden_body(tile, h2_own, h2_core, wg, wu, wd, cot, hid_ref, dgate_ref, dup_ref):
    units = wg.shape[1]
    h2 = jnp.concatenate((h2_own[...], h2_core[...]), axis=0)
    for s in range(0, units, tile):
        cut = slice(s, min(s + tile, units))
        gate = dot(h2, wg[:, cut])
        up = dot(h2, wu[:, cut])
        dh = dot_rt(cot, wd[cut, :])
        sig = jax.nn.sigmoid(gate)
        active = gate * sig
        hid_ref[:, cut] = (active * up).astype(BF)
        dgate_ref[:, cut] = (dh * up * (sig + active * (1.0 - sig))).astype(BF)
        dup_ref[:, cut] = (dh * active).astype(BF)


def mlp_kernel(tile, h2_own, h2_core, wg, wu, wd, cot_a, cot_b, near, hid_ref, dgate_ref, dup_ref):
    rows = h2_own.shape[0]
    cot = jnp.concatenate((cot_a[:rows], cot_b[:rows]), axis=0)
    hidden_body(tile, h2_own, h2_core, wg, wu, wd, cot, hid_ref, dgate_ref, dup_ref)


def mlp(h2_own, h2_core, wg, wu, wd, cot_halves, near, tile=512):
    shape = jax.ShapeDtypeStruct((2 * h2_own.shape[0], wg.shape[1]), BF)
    return pl.pallas_call(
        functools.partial(mlp_kernel, tile),
        out_shape=[shape] * 3,
        in_specs=[vmem()] * 8,
        out_specs=[vmem()] * 3,
        compiler_params=params(12),
        name="mlp",
        cost_estimate=cost(0.01),
    )(h2_own, h2_core, wg, wu, wd, *cot_halves, near)


def mlp_rest_kernel(
    tile, split, place_ref, h2_own, h2_core, wg, wu, wd, cot_a, cot_b, h2_a, h2_b, hid_a, dgate_a,
    hid_ref, dgate_ref, dup_ref, *outs,
):
    rows = h2_own.shape[0]
    units = wg.shape[1]
    cot = jnp.concatenate((cot_a[rows:], cot_b[rows:]), axis=0)
    hidden_body(tile, h2_own, h2_core, wg, wu, wd, cot, hid_ref, dgate_ref, dup_ref)
    cots = [(ref, first, rows) for first in (0, rows) for ref in (cot_a, cot_b)]
    h2 = (h2_a, h2_b, h2_own, h2_core)
    gradient_body(place_ref, [(cots, (hid_a, hid_ref), 0, units), (h2, (dgate_a, dgate_ref), 0, split)], outs)


def mlp_rest(place_xy, h2_own, h2_core, wg, wu, wd, cot_halves, h2_a, h2_b, hid_a, dgate_a, split, tile=512):
    units = wg.shape[1]
    shape = jax.ShapeDtypeStruct((2 * h2_own.shape[0], units), BF)
    got = pl.pallas_call(
        functools.partial(mlp_rest_kernel, tile, split),
        out_shape=[shape] * 3 + gradient_shapes(units + split),
        in_specs=[smem()] + [vmem()] * 11,
        out_specs=[vmem()] * 11,
        compiler_params=params(14),
        name="mlp_rest",
        cost_estimate=cost(13),
    )(place_xy, h2_own, h2_core, wg, wu, wd, *cot_halves, h2_a, h2_b, hid_a, dgate_a)
    return (*got[:3], got[3:])


def mlp_back_kernel(
    step, split, place_ref, dgate_a, dgate_b, dup_a, dup_b, wg, wu, h2_a, h2_b, h2_c, h2_d,
    high_ref, low_ref, gain_ref, *outs,
):
    h2 = (h2_a, h2_b, h2_c, h2_d)
    rows, width = h2_a.shape
    units = dup_a.shape[1]
    dgate = jnp.concatenate((dgate_a[...], dgate_b[...]), axis=0)
    dup = jnp.concatenate((dup_a[...], dup_b[...]), axis=0)
    for s in range(0, width, step):
        cut = slice(s, s + step)
        part = dot_rt(dgate, wg[cut, :]) + dot_rt(dup, wu[cut, :])
        gain = jnp.zeros((1, step), F32)
        for number, block in enumerate(h2):
            piece = part[number * rows : (number + 1) * rows]
            gain = gain + jnp.sum(piece * block[:, cut].astype(F32), axis=0, keepdims=True)
            place = slice(number // 2 * rows, (number // 2 + 1) * rows)
            if number % 2:
                low_ref[place, cut] = piece.astype(BF)
            else:
                high_ref[place, cut] = piece
        gain_ref[:, cut] = gain
    gradient_body(place_ref, [(h2, (dgate_a, dgate_b), split, units - split), (h2, (dup_a, dup_b), 0, units)], outs)


def mlp_back(place_xy, dgates, dups, wg, wu, h2, split, step=512):
    rows, width = h2[0].shape
    got = pl.pallas_call(
        functools.partial(mlp_back_kernel, step, split),
        out_shape=[
            jax.ShapeDtypeStruct((2 * rows, width), F32),
            jax.ShapeDtypeStruct((2 * rows, width), BF),
            jax.ShapeDtypeStruct((1, width), F32),
        ]
        + gradient_shapes(2 * wg.shape[1] - split),
        in_specs=[smem()] + [vmem()] * 10,
        out_specs=[vmem()] * 11,
        compiler_params=params(12),
        name="mlp_back",
        cost_estimate=cost(14),
    )(place_xy, *dgates, *dups, wg, wu, *h2)
    return (*got[:3], got[3:])


def touch_kernel(*refs):
    *sources, target = refs
    total = jnp.zeros(target.shape, F32)
    for source in sources:
        total = total + source[:16, :128].astype(F32)
    target[...] = total


def touch(*arrays):
    return pl.pallas_call(
        touch_kernel,
        out_shape=jax.ShapeDtypeStruct((16, 128), F32),
        in_specs=[vmem()] * len(arrays),
        out_specs=vmem(),
        compiler_params=params(12),
        name="touch",
        cost_estimate=cost(2),
    )(*arrays)


def pair_kernel(above, below, later, target):
    rows = above.shape[0]
    target[:rows] = above[...]
    target[rows:] = below[...]


def pair(above, below, later):
    rows, width = above.shape
    return pl.pallas_call(
        pair_kernel,
        out_shape=jax.ShapeDtypeStruct((2 * rows, width), above.dtype),
        in_specs=[vmem()] * 2 + [pl.BlockSpec(memory_space=pl.ANY)],
        out_specs=vmem(),
        compiler_params=params(4),
        name="pair",
        cost_estimate=cost(8),
    )(above, below, later)


def chip_kernel(high, got, chip, *sends):
    total = high[...] + got[...].astype(F32)
    rows = total.shape[0] // 2
    chip[...] = total[: chip.shape[0]]
    sends[0][:rows, :] = total[rows:].astype(BF)
    if len(sends) > 1:
        sends[1][...] = total[:rows].astype(BF)
    elif sends[0].shape[0] > rows:
        sends[0][rows:, :] = total[:rows].astype(BF)


def chip_sums(high, got, blocks):
    rows, width = high.shape[0] // 2, high.shape[1]
    sends = [jax.ShapeDtypeStruct((count * rows, width), BF) for count in blocks]
    return pl.pallas_call(
        chip_kernel,
        out_shape=[jax.ShapeDtypeStruct((sum(blocks) * rows, width), F32)] + sends,
        in_specs=[vmem()] * 2,
        out_specs=[vmem()] * (1 + len(sends)),
        compiler_params=params(6),
        name="chip_sums",
        cost_estimate=cost(1),
    )(high, got)


def middle_kernel(number, tokens, chip, got, gain, mid_ref, h2_ref):
    rows = tokens.shape[0]
    mid = tokens[...].astype(F32) + chip[number * rows : (number + 1) * rows, :] + got[...].astype(F32)
    inverse = lax.rsqrt(jnp.mean(mid * mid, axis=-1, keepdims=True) + EPSILON)
    mid_ref[...] = mid
    h2_ref[...] = (mid * inverse * gain[...].astype(F32)).astype(BF)


def middle(number, tokens, chip, got, gain):
    return pl.pallas_call(
        functools.partial(middle_kernel, number),
        out_shape=(jax.ShapeDtypeStruct(tokens.shape, F32), jax.ShapeDtypeStruct(tokens.shape, BF)),
        in_specs=[vmem()] * 4,
        out_specs=[vmem()] * 2,
        compiler_params=params(8),
        name="middle",
        cost_estimate=cost(1),
    )(tokens, chip, got, gain)


def middle_back_kernel(mid_own, mid_across, cot, chip, got, gain, own, top, rest):
    mid = jnp.concatenate((mid_own[...], mid_across[...]), axis=0)
    inverse = lax.rsqrt(jnp.mean(mid * mid, axis=-1, keepdims=True) + EPSILON)
    normed = mid * inverse
    scaled = (chip[...] + got[...].astype(F32)) * gain[...].astype(F32)
    grad = cot[...].astype(F32) + inverse * (scaled - normed * jnp.mean(scaled * normed, axis=-1, keepdims=True))
    own[...] = grad[: own.shape[0]]
    top[...] = grad[: top.shape[0]].astype(BF)
    rest[...] = grad[top.shape[0] :].astype(BF)


def middle_back(mids, cot, chip, got, gain, cut):
    half, width = chip.shape
    return pl.pallas_call(
        middle_back_kernel,
        out_shape=(
            jax.ShapeDtypeStruct((half // 2, width), F32),
            jax.ShapeDtypeStruct((cut, width), BF),
            jax.ShapeDtypeStruct((half - cut, width), BF),
        ),
        in_specs=[vmem()] * 6,
        out_specs=[vmem()] * 3,
        compiler_params=params(8),
        name="middle_back",
        cost_estimate=cost(2),
    )(*mids, cot, chip, got, gain)


def output_kernel(step, hid_a, hid_b, wd, high_ref, low_ref):
    rows = hid_a.shape[0] // 2
    hid = jnp.concatenate((hid_a[...], hid_b[...]), axis=0)
    for s in range(0, wd.shape[1], step):
        cut = slice(s, s + step)
        part = dot(hid, wd[:, cut]).astype(BF)
        for number in range(4):
            target = low_ref if number % 2 else high_ref
            target[number // 2 * rows : (number // 2 + 1) * rows, cut] = part[number * rows : (number + 1) * rows]


def output(hid_a, hid_b, wd, step=512):
    shape = jax.ShapeDtypeStruct((hid_a.shape[0], wd.shape[1]), BF)
    return pl.pallas_call(
        functools.partial(output_kernel, step),
        out_shape=[shape] * 2,
        in_specs=[vmem()] * 3,
        out_specs=[vmem()] * 2,
        compiler_params=params(8),
        name="output",
        cost_estimate=cost(4),
    )(hid_a, hid_b, wd)


def combine_kernel(sums, *refs):
    out = refs[-1]
    at = 0
    for count, terms in sums:
        total = None
        for number, start in terms:
            term = refs[number][start : start + count].astype(F32)
            total = term if total is None else total + term
        out[at : at + count] = total.astype(out.dtype)
        at += count


def combine(sums, time=0.5):
    arrays, plan = [], []
    for terms in sums:
        listed = []
        for array, start, count in terms:
            known = [i for i, a in enumerate(arrays) if a is array]
            if not known:
                arrays.append(array)
            listed.append((known[0] if known else len(arrays) - 1, start))
        plan.append((terms[0][2], listed))
    total = sum(count for count, _ in plan)
    return pl.pallas_call(
        functools.partial(combine_kernel, plan),
        out_shape=jax.ShapeDtypeStruct((total, 32, 128), BF),
        in_specs=[vmem()] * len(arrays),
        out_specs=vmem(),
        compiler_params=params(8),
        name="combine",
        cost_estimate=cost(time),
    )(*arrays)


def ends_kernel(sums, extra, place_ref, *refs):
    give, keep = refs[-2:]
    at = 0
    if extra:
        total = None
        for number, start in extra:
            term = refs[number][start : start + 1].astype(F32)
            total = term if total is None else total + term
        give[0:1] = total.astype(BF)
        keep[0:1] = total.astype(BF).astype(F32)
        at = 1
    for parts in sums:
        count = parts[0][0]
        totals = []
        for _, terms in parts:
            total = None
            for number, start in terms:
                term = refs[number][start : start + count].astype(F32)
                total = term if total is None else total + term
            totals.append(total)
        for half in range(2):
            cut = slice(at, at + count)
            give[cut] = jnp.where(place_ref[2] == 0, totals[2 + half], totals[half]).astype(BF)
            keep[cut] = jnp.where(place_ref[2] == 0, totals[half], totals[2 + half])
            at += count


def ends(place, sums, extra=()):
    arrays, plan = [], []
    for parts in sums:
        planned = []
        for terms in parts:
            listed = []
            for array, start, count in terms:
                known = [i for i, a in enumerate(arrays) if a is array]
                if not known:
                    arrays.append(array)
                listed.append((known[0] if known else len(arrays) - 1, start))
            planned.append((terms[0][2], listed))
        plan.append(planned)
    arrays += [array for array, _, _ in extra]
    more = [(len(arrays) - len(extra) + i, start) for i, (_, start, _) in enumerate(extra)]
    total = sum(2 * parts[0][0] for parts in plan) + bool(extra)
    return pl.pallas_call(
        functools.partial(ends_kernel, plan, more),
        out_shape=(jax.ShapeDtypeStruct((total, 32, 128), BF), jax.ShapeDtypeStruct((total, 32, 128), F32)),
        in_specs=[smem()] + [vmem()] * len(arrays),
        out_specs=[vmem()] * 2,
        compiler_params=params(16),
        name="ends",
        cost_estimate=cost(1),
    )(place, *arrays)


def attention_back_kernel(
    docs, place_ref, place_xy, mid_a, mid_b, mid_c, mid_d, qkv, lse_ref, h1, o_ref, wq, wk, wv, wo, cos, sin, gain_two, *refs
):
    dqkv_ref, high_ref, low_ref, gains, *outs, bias_ref, do_ref = refs
    half = mid_a.shape[0] + mid_b.shape[0]
    rows, every = half // 2, 2 * half
    q_width = wq.shape[1]
    heads = q_width // HD
    width = wq.shape[0]
    scale = 1.0 / math.sqrt(HD)
    mid = jnp.concatenate((mid_a[...], mid_b[...], mid_c[...], mid_d[...]), axis=0)
    do_ref[...] = dot_rt(mid, wo[...]).astype(BF)
    ends = doc_ends(place_ref, docs)
    places_q, opening_q = places_of(place_ref[0], ends, rows, (1, every), 1)
    places_k, _ = places_of(place_ref[0], ends, rows, (every, 1), 0)
    bias_ref[...] = jnp.where((places_k <= places_q) & (places_k >= opening_q), 0.0, MASKED)
    keys = qkv[:, q_width : q_width + HD]
    vals = qkv[:, q_width + HD : q_width + 2 * HD]
    dk = jnp.zeros((every, HD), F32)
    dv = jnp.zeros((every, HD), F32)
    table_c, table_s = cos[...], sin[...]

    def unrope(values):
        wide_now = values.shape[1]
        return values * wide(table_c, wide_now) - swap_halves(values) * wide(table_s, wide_now)

    for pair in range(heads // 2):
        dqs = []
        for head in (2 * pair, 2 * pair + 1):
            cut = slice(head * HD, (head + 1) * HD)
            query = qkv[:, cut]
            grad_o = do_ref[:, cut]
            scores = dot_rt(keys, query) * scale + bias_ref[...]
            chances = jnp.exp(scores - lse_ref[head : head + 1, :])
            grad_chances = dot_rt(vals, grad_o)
            centre = jnp.sum(chances * grad_chances, axis=0, keepdims=True)
            grad_scores = (chances * (grad_chances - centre)).astype(BF)
            dv = dv + dot(chances.astype(BF), grad_o)
            dk = dk + dot(grad_scores, query)
            dqs.append(dot_t(grad_scores, keys))
        dq = jnp.concatenate(dqs, axis=1) * scale
        dqkv_ref[:, pair * 2 * HD : (pair + 1) * 2 * HD] = unrope(dq).astype(BF)
    both = jnp.concatenate((dk * scale, dv), axis=1)
    lane = lax.broadcasted_iota(jnp.int32, both.shape, 1)
    dqkv_ref[:, q_width:] = jnp.where(lane < HD, unrope(both), both).astype(BF)
    joined = jnp.concatenate((wk[...], wv[...]), axis=0)
    step = 512
    for s in range(0, width, step):
        part = dot_rt(dqkv_ref[:, :q_width], wq[s : s + step, :]) + dot(dqkv_ref[:, q_width:], joined[:, s : s + step])
        high_ref[:, s : s + step] = part[:half]
        low_ref[:, s : s + step] = part[half:].astype(BF)
        gain_one = jnp.sum(part * h1[:, s : s + step].astype(F32), axis=0, keepdims=True)
        for lane in range(0, step, 128):
            row = (s + lane) // 128
            gains[0, row : row + 1, :] = gain_one[:, lane : lane + 128]
            gains[0, width // 128 + row : width // 128 + row + 1, :] = gain_two[:, s + lane : s + lane + 128]
    gradient_body(place_xy, [((h1,), (dqkv_ref,), 0, q_width + 2 * HD), ((mid_a, mid_b, mid_c, mid_d), (o_ref,), 0, q_width)], outs)


def attention_back(place_docs, place_xy, mids, qkv, lse, h1, o, wq, wk, wv, wo, cos, sin, gain_two_part):
    half, width = mids[0].shape[0] + mids[1].shape[0], mids[0].shape[1]
    every = 2 * half
    q_width = wq.shape[1]
    got = pl.pallas_call(
        functools.partial(attention_back_kernel, place_docs.shape[0] - 1),
        out_shape=[
            jax.ShapeDtypeStruct((every, q_width + 2 * HD), BF),
            jax.ShapeDtypeStruct((half, width), F32),
            jax.ShapeDtypeStruct((half, width), BF),
            jax.ShapeDtypeStruct((1, width // 64, 128), F32),
        ]
        + gradient_shapes(2 * q_width + 2 * HD),
        in_specs=[smem()] * 2 + [vmem()] * 15,
        out_specs=[vmem()] * 12,
        scratch_shapes=[
            pltpu.VMEM((every, every), F32),
            pltpu.VMEM((every, q_width), BF),
        ],
        compiler_params=params(12),
        name="attention_back",
        cost_estimate=cost(19),
    )(place_docs, place_xy, *mids, qkv, lse, h1, o, wq, wk.T, wv.T, wo, cos, sin, gain_two_part)
    return (*got[1:4], got[4:])


def lay_out_kernel(plan, keep, got, *outs):
    for out, parts in zip(outs, plan):
        for start, blocks, first, width, to in parts:
            for half in range(2):
                for b in range(blocks):
                    low, high = max(128 * b, first), min(128 * (b + 1), first + width)
                    if low >= high:
                        continue
                    at = start + half * blocks + b
                    total = keep[at] + got[at].astype(F32)
                    out[32 * half : 32 * (half + 1), to + low - first : to + high - first] = total[:, low - 128 * b : high - 128 * b]


def lay_out(keep, got, plan):
    widths = [sum(part[3] for part in parts) for parts in plan]
    return pl.pallas_call(
        functools.partial(lay_out_kernel, plan),
        out_shape=[jax.ShapeDtypeStruct((64, width), F32) for width in widths],
        in_specs=[vmem()] * 2,
        out_specs=[vmem()] * len(plan),
        compiler_params=params(12),
        name="lay_out",
        cost_estimate=cost(1),
    )(keep, got)


def rotary_tables(offset):
    half_size = HD // 2
    freqs = THETA ** (-(jnp.arange(half_size, dtype=F32) * 2.0 / HD))
    angles = offset.astype(F32)[:, None] * freqs[None, :]
    cosine, sine = jnp.cos(angles), jnp.sin(angles)
    return jnp.concatenate((cosine,) * 4, axis=1), jnp.concatenate((-sine, sine) * 2, axis=1)


def over_core(values):
    return lax.ppermute(values, "tensor", [(t, t ^ 1) for t in range(4)])


def over_z(values):
    return lax.ppermute(values, "tensor", [(t, t ^ 2) for t in range(4)])


def over_diagonal(values):
    return lax.ppermute(values, "tensor", [(t, t ^ 3) for t in range(4)])


def over_x(values, xor):
    return lax.ppermute(values, "dp", [(d, d ^ (xor * 8)) for d in range(32)])


def over_y(values, xor):
    return lax.ppermute(values, "dp", [(d, d ^ (xor * 2)) for d in range(32)])


def over_z_hi(values):
    return lax.ppermute(values, "dp", [(d, d ^ 1) for d in range(32)])


def after(value, *others):
    return lax.optimization_barrier((value, *others))[0] if others else value


def add(*terms):
    total = terms[0].astype(F32)
    for term in terms[1:]:
        total = total + term.astype(F32)
    return total


def norm(values):
    inverse = lax.rsqrt(jnp.mean(values * values, axis=-1, keepdims=True) + EPSILON)
    return values * inverse, inverse


def norm_back(normed, inverse, gain, grads):
    scaled = grads * gain
    return inverse * (scaled - normed * jnp.mean(scaled * normed, axis=-1, keepdims=True))


LINKS = ((over_x, 1), (over_x, 3), (over_y, 1), (over_y, 3))
ROUTES = ((0, 1, 2, 3), (1, 0, 3, 2), (2, 3, 0, 1), (3, 2, 1, 0))


class Reduction:
    def __init__(self, arrays, joined=False):
        self.joined = joined
        self.blocks = arrays[0].shape[2]
        self.sends = [arrays[2 * part].reshape(-1, 32, 128) for part in range(4)]
        self.kept = [[(arrays[2 * part + 1].reshape(-1, 32, 128), self.starts(0, 8))] for part in range(4)]
        self.near, self.far, self.last = {}, {}, {}

    def starts(self, at, rows):
        return {row: at + row * self.blocks for row in range(rows)}

    def route(self, part, step):
        return ROUTES[part - part % 2 if self.joined and step >= 2 else part][step]

    def order(self, part):
        return ((1, 3), (3, 1))[0 if self.joined else part % 2]

    def row(self, part, row, rows=1):
        return [(array, starts[row], rows * self.blocks) for array, starts in self.kept[part]]

    def sum(self, part, step):
        first, second = self.order(part)
        if step == 0:
            return [(self.sends[part], 0, 8 * self.blocks)]
        if step == 1:
            return self.row(part, 4, 4)
        if step == 2:
            return self.row(part, min(first, 2), 2)
        if step == 3:
            return self.row(part, second) + [self.far[part]]
        return self.row(part, 0) + self.near.get(part, []) + [self.last[part]]

    def take(self, part, step, got, at):
        n = self.blocks
        if step < 2:
            self.kept[part].append((got, self.starts(at, 8 - 4 * step)))
        elif step == 2:
            near, far = (0, 1) if self.order(part)[0] == 1 else (1, 0)
            self.near[part] = [(got, at + near * n, n)]
            self.far[part] = (got, at + far * n, n)
        else:
            self.last[part] = (got, at, n)


def fold(jobs, time=0.5):
    folded = []
    for part in range(4):
        sums, places = [], []
        at = 0
        for r, rows in jobs:
            rows = {"last": (0, r.order(part)[1]), "own": (0,)}.get(rows, rows)
            starts = {}
            for row in rows:
                terms = r.row(part, row)
                if row == 0:
                    terms = terms + r.near.get(part, [])
                sums.append(terms)
                starts[row] = at
                at += r.blocks
            r.near.pop(part, None)
            places.append((r, starts))
        array = combine(sums, time)
        folded.append(array)
        for r, starts in places:
            r.kept[part] = [(array, starts)]
    return folded


class Gains:
    def __init__(self, block):
        self.held = [(block, 0)]

    def terms(self):
        return [(array, start, 1) for array, start in self.held]

    def exchange(self, hop, before):
        sent = sum(array[start : start + 1].astype(F32) for array, start in self.held).astype(BF)
        self.held = [(sent, 0), (hop(after(sent, *before)), 0)]


def takers(jobs, link):
    return [(r, part, step) for r, step in jobs for part in range(4) if r.route(part, step) == link]


def prepare(jobs, gains=None, gains_link=None):
    operands = []
    for link in range(4):
        taken = takers(jobs, link)
        if not taken:
            operands.append(None)
            continue
        if len(taken) == 1 and taken[0][2] == 0:
            operands.append(taken[0][0].sends[taken[0][1]])
            continue
        sums = [r.sum(part, step) for r, part, step in taken]
        operands.append(combine(sums + ([gains.terms()] if link == gains_link else [])))
    return operands


def send(jobs, operands, before=None, anchor=(), gains=None, gains_link=None):
    arrived = []
    for link, (operand, (hop, xor)) in enumerate(zip(operands, LINKS)):
        if operand is None:
            arrived.append(before[link])
            continue
        got = hop(after(operand, *before[link]) if before else operand, xor)
        arrived.append((got,))
        got = after(got, *anchor)
        at = 0
        for r, part, step in takers(jobs, link):
            r.take(part, step, got, at)
            at += r.blocks * (8, 4, 2, 1)[step]
        if link == gains_link:
            gains.held = [(operand, at), (got, at)]
    return arrived


def stage(jobs, before=None, **more):
    return send(jobs, prepare(jobs, **more), before, **more)


def finish(reductions, place, plan, before=(), gains=None, anchor=None):
    keep, give = None, None
    give, keep = ends(
        place,
        [[r.sum(part, 4) for part in range(4)] for r in reductions],
        gains.terms() if gains else (),
    )
    got = over_z_hi(after(give, *before))
    if anchor is not None:
        got = after(got, anchor)
    outs = lay_out(keep, got, plan)
    if gains:
        total = add(keep[0], got[0])
        outs = (*outs, (total + over_core(total)) + (over_z(total) + over_diagonal(total)))
    return outs


def per_device(
    tokens,
    attn_gain,
    query_weight,
    key_weight,
    value_weight,
    out_weight,
    mlp_gain,
    gate_weight,
    up_weight,
    down_weight,
    cotangent,
    doc_lengths,
):
    rows = tokens.shape[0]
    place_dp = lax.axis_index("dp")
    place_t = lax.axis_index("tensor")
    place_xy = jnp.stack((place_dp // 8, (place_dp // 2) % 4, place_dp % 2))
    q_width = query_weight.shape[1]
    gain_one, gain_two = attn_gain.astype(F32), mlp_gain.astype(F32)

    across = over_z(tokens)
    places = jnp.concatenate(
        [(place_t ^ j) * rows + jnp.arange(rows, dtype=jnp.int32) for j in (0, 2, 1, 3)]
    )
    opening, ending = jnp.zeros_like(places), jnp.int32(0)
    for number in range(doc_lengths.shape[0]):
        ending = ending + doc_lengths[number]
        opening = jnp.maximum(opening, jnp.where(places >= ending, ending, 0))
    cos, sin = rotary_tables(places - opening)
    place_docs = jnp.concatenate((place_t[None], doc_lengths))
    attn_row, mlp_row = attn_gain.reshape(1, -1), mlp_gain.reshape(1, -1)
    near = touch(query_weight, out_weight)
    across, cos, sin, place_docs, place_xy, attn_row, mlp_row, near = lax.optimization_barrier(
        (across, cos, sin, place_docs, place_xy, attn_row, mlp_row, near)
    )
    token_blocks = (tokens, across, over_core(tokens), over_core(across))

    cot_across = over_z(after(cotangent, across))
    h1, qkv, heads_out, lse, high, low = attention(
        place_docs, token_blocks, attn_row, query_weight, key_weight, value_weight, out_weight, cos, sin, near
    )
    cot_pair = pair(cotangent, cot_across, low)
    chip, *sends = chip_sums(high, after(over_core(low), cot_pair), (1, 1))
    z_sums = [over_z(block) for block in sends]
    cot_halves = (cot_pair, over_core(after(cot_pair, chip)))
    near = touch(after(gate_weight, cot_halves[1]), up_weight, down_weight)
    units = gate_weight.shape[1]
    split = units // 2 // 128 * 128 + 128
    weights = (gate_weight, up_weight, down_weight)
    mid_own, h2_own = middle(0, tokens, chip, after(z_sums[0], near), mlp_row)
    h2_core = over_core(h2_own)
    hidden_a, dgate_a, dup_a = mlp(h2_own, h2_core, *weights, cot_halves, near)
    mid_across, h2_across = middle(1, across, chip, after(z_sums[1], hidden_a), mlp_row)
    h2 = (h2_own, h2_core, h2_across, over_core(h2_across))
    hidden_b, dgate_b, dup_b, first = mlp_rest(
        place_xy, *h2[2:], *weights, cot_halves, *h2[:2], hidden_a, dgate_a, split
    )
    first_sum = Reduction(first)
    first_links = stage([(first_sum, 0)])
    high, low, gain_two_part, second = mlp_back(
        place_xy, (dgate_a, after(dgate_b, first[0])), (dup_a, dup_b), gate_weight, up_weight, h2, split
    )
    chip, low = chip_sums(high, after(over_core(low), *[link[0] for link in first_links]), (2,))
    second_sum = Reduction(second)
    links = stage([(second_sum, 0)], first_links)
    z_sums = after(over_z(low), *fold([(first_sum, range(8))]))
    grad_own, *mid_low = middle_back((mid_own, mid_across), cot_pair, chip, z_sums, mlp_row, rows + rows // 2)
    mid_low = (*mid_low, over_core(mid_low[0]), over_core(mid_low[1]))

    jobs = [(first_sum, 1), (second_sum, 1)]
    operands = prepare(jobs)
    high, low, gains, attn = attention_back(
        place_docs, place_xy, mid_low, after(qkv, *operands), lse, h1, heads_out,
        query_weight, key_weight, value_weight, out_weight, cos, sin, gain_two_part,
    )
    links = send(jobs, operands, links, (low,))
    attn_sum = Reduction(attn, joined=True)
    gains = Gains(gains)
    own, other = chip_sums(high, after(over_core(low), *[link[0] for link in links]), (1,))
    jobs = [(first_sum, 2), (second_sum, 2), (attn_sum, 0)]
    operands = prepare(jobs, gains, 0)
    folded = fold([(first_sum, "last"), (second_sum, "last")])
    out_high, out_low = output(hidden_a, after(hidden_b, low), down_weight)
    links = send(jobs, operands, links, (*folded, out_low), gains, 0)
    grad_h1 = own + over_z(other).astype(F32)
    result_got = over_core(after(out_low, grad_h1))
    result_chip = add(out_high, result_got)
    result_z = over_z(result_chip[rows:].astype(BF))
    result = (mid_own + result_chip[:rows] + result_z.astype(F32)).astype(BF)
    jobs = [(first_sum, 3), (second_sum, 3), (attn_sum, 1)]
    operands = prepare(jobs, gains, 1)
    folded = fold([(first_sum, "own"), (second_sum, "own"), (attn_sum, range(4))])
    links = send(jobs, operands, links, folded, gains, 1)
    blocks, more = first_sum.blocks, second_sum.blocks
    plan = [
        [(0, blocks, 0, units, 0)],
        [(0, blocks, units, split, 0), (2 * blocks, more, 0, units - split, split)],
        [(2 * blocks, more, units - split, units, 0)],
    ]
    out_down, out_gate, out_up = finish([first_sum, second_sum], place_xy, plan)
    links = stage([(attn_sum, 2)], links, gains=gains, gains_link=2)
    links = [(*link, result_z) for link in links]
    links = stage([(attn_sum, 3)], links, gains=gains, gains_link=3)
    cuts = ((0, q_width), (q_width, HD), (q_width + HD, HD), (q_width + 2 * HD, q_width))
    plan = [[(1, attn_sum.blocks, first, width, 0)] for first, width in cuts]
    out_query, out_key, out_value, out_out, grad_gains = finish([attn_sum], place_xy, plan, [], gains, out_up)
    grad_gains = grad_gains.reshape(2, -1)

    normed, inverse = norm(tokens.astype(F32))
    grad_tokens = grad_own + norm_back(normed, inverse, gain_one, grad_h1)
    return (
        result,
        grad_tokens.astype(BF),
        grad_gains[0] / gain_one,
        out_query,
        out_key,
        out_value,
        out_out.T,
        grad_gains[1] / gain_two,
        out_gate,
        out_up,
        out_down.T,
    )


def solution(mesh):
    in_specs = (
        P(("dp", "tensor"), None),
        P(),
        P(None, "tensor"),
        P(None, "tensor"),
        P(None, "tensor"),
        P("tensor", None),
        P(),
        P(None, "tensor"),
        P(None, "tensor"),
        P("tensor", None),
        P(("dp", "tensor"), None),
        P("dp"),
    )
    out_specs = (
        P(("dp", "tensor"), None),
        P(("dp", "tensor"), None),
        P(),
        P("dp", "tensor"),
        P("dp", "tensor"),
        P("dp", "tensor"),
        P("tensor", "dp"),
        P(),
        P("dp", "tensor"),
        P("dp", "tensor"),
        P("tensor", "dp"),
    )
    return jax.shard_map(
        per_device, mesh=mesh, in_specs=in_specs, out_specs=out_specs, check_vma=False
    )
```

```python
import functools
import math

import jax
import jax.numpy as jnp
from jax import lax
from jax.experimental import pallas as pl
from jax.experimental.pallas import tpu as pltpu
from jax.sharding import PartitionSpec as P

HD = 64
EPSILON = 1e-05
THETA = 10000.0
MASKED = -1000000000.0
BF = jnp.bfloat16
F32 = jnp.float32
MIB = 1024 * 1024


def cost(time):
    return pl.CostEstimate(flops=int(time * 1e9), bytes_accessed=1024, transcendentals=0)


def dot(left, right):
    return jnp.dot(left, right, preferred_element_type=F32)


def dot_t(left, right):
    return lax.dot_general(left, right, (((0,), (0,)), ((), ())), preferred_element_type=F32)


def dot_rt(left, right):
    return lax.dot_general(left, right, (((1,), (1,)), ((), ())), preferred_element_type=F32)


def vmem():
    return pl.BlockSpec(memory_space=pltpu.VMEM)


def smem():
    return pl.BlockSpec(memory_space=pltpu.SMEM)


def hbm():
    return pl.BlockSpec(memory_space=pl.ANY)


def params(size):
    return pltpu.CompilerParams(vmem_limit_bytes=size * MIB)


def swap_halves(values):
    width = values.shape[1]
    lane = lax.broadcasted_iota(jnp.int32, values.shape, 1)
    return jnp.where(
        lane % HD < HD // 2,
        pltpu.roll(values, width - HD // 2, 1),
        pltpu.roll(values, HD // 2, 1),
    )


def wide(table, width):
    return jnp.concatenate([table] * (width // table.shape[1]), axis=1) if width > table.shape[1] else table[:, :width]


def places_of(place_t, ends, rows, shape, axis):
    index = lax.broadcasted_iota(jnp.int32, shape, axis)
    block = index // rows
    order = jnp.where(block == 0, 0, jnp.where(block == 1, 2, jnp.where(block == 2, 1, 3)))
    places = (place_t ^ order) * rows + index % rows
    opening = jnp.zeros(shape, jnp.int32)
    for end in ends:
        opening = jnp.maximum(opening, jnp.where(places >= end, end, 0))
    return places, opening


def doc_ends(place_ref, count):
    ends, total = [], jnp.int32(0)
    for i in range(count):
        total = total + place_ref[1 + i]
        ends.append(total)
    return ends


def attention_kernel(
    docs, place_ref, own, zpart, cpart, diag, gain, wq, wk, wv, wo, cos, sin, near,
    h1_ref, qkv_ref, o_ref, lse_ref, high_ref, low_ref, bias_ref,
):
    rows = own.shape[0]
    every = 4 * rows
    half = 2 * rows
    q_width = wq.shape[1]
    heads = q_width // HD
    gain_row = gain[...].astype(F32)
    for number, block in enumerate((own, zpart, cpart, diag)):
        values = block[...].astype(F32)
        inverse = lax.rsqrt(jnp.mean(values * values, axis=-1, keepdims=True) + EPSILON)
        h1_ref[number * rows : (number + 1) * rows, :] = (values * inverse * gain_row).astype(BF)
    h1 = h1_ref[...]
    joined = jnp.concatenate((wk[...], wv[...]), axis=0)
    table_c, table_s = cos[...], sin[...]

    def rope(values):
        width = values.shape[1]
        return values * wide(table_c, width) + swap_halves(values) * wide(table_s, width)

    scale = 1.0 / math.sqrt(HD)
    kv = dot_rt(h1, joined)
    lane = lax.broadcasted_iota(jnp.int32, kv.shape, 1)
    qkv_ref[:, q_width:] = jnp.where(lane < HD, rope(kv), kv).astype(BF)
    qkv_ref[:, :q_width] = rope(dot(h1, wq[...])).astype(BF)

    ends = doc_ends(place_ref, docs)
    places_q, opening_q = places_of(place_ref[0], ends, rows, (every, 1), 0)
    places_k, _ = places_of(place_ref[0], ends, rows, (1, every), 1)
    bias_ref[...] = jnp.where((places_k <= places_q) & (places_k >= opening_q), 0.0, MASKED)

    keys = qkv_ref[:, q_width : q_width + HD]
    kv_low = qkv_ref[:, q_width:]
    lane = lax.broadcasted_iota(jnp.int32, kv_low.shape, 1)
    ones_vals = jnp.where(lane < HD, jnp.ones_like(kv_low), kv_low)
    lse_lane = lax.broadcasted_iota(jnp.int32, (every, 128), 1)
    lse = jnp.zeros((every, 128), F32)
    for head in range(heads):
        query = qkv_ref[:, head * HD : (head + 1) * HD]
        scores = dot_rt(query, keys) * scale + bias_ref[...]
        highest = jnp.max(scores, axis=-1, keepdims=True)
        raised = jnp.exp(scores - highest)
        mixed = dot(raised.astype(BF), ones_vals)
        totals = mixed[:, :1]
        o_ref[:, head * HD : (head + 1) * HD] = (mixed[:, HD:] / totals).astype(BF)
        lse = jnp.where(lse_lane == head, highest + jnp.log(totals), lse)
    lse_ref[...] = lse.T[:heads, :]
    high_ref[...] = dot(o_ref[:half, :], wo[...])
    low_ref[...] = dot(o_ref[half:, :], wo[...]).astype(BF)


def attention(place_docs, blocks, gain, wq, wk, wv, wo, cos, sin, near):
    rows, width = blocks[0].shape
    every = rows * 4
    q_width = wq.shape[1]
    heads = q_width // HD
    shapes = (
        jax.ShapeDtypeStruct((every, width), BF),
        jax.ShapeDtypeStruct((every, q_width + 2 * HD), BF),
        jax.ShapeDtypeStruct((every, q_width), BF),
        jax.ShapeDtypeStruct((heads, every), F32),
        jax.ShapeDtypeStruct((2 * rows, width), F32),
        jax.ShapeDtypeStruct((2 * rows, width), BF),
    )
    return pl.pallas_call(
        functools.partial(attention_kernel, place_docs.shape[0] - 1),
        out_shape=shapes,
        in_specs=[smem()] + [vmem()] * 12,
        out_specs=[vmem()] * 6,
        scratch_shapes=[pltpu.VMEM((every, every), F32)],
        compiler_params=params(12),
        name="attention",
        cost_estimate=cost(11),
    )(place_docs, *blocks, gain, wq, wk.T, wv.T, wo, cos, sin, near)


SEND = ((1, 2), (3, 2))
KEEP = ((0, 3), (0, 1))


def gradient_body(place_ref, groups, outs, tile=512):
    place_x, place_y = place_ref[0], place_ref[1]
    at = 0
    for lefts, right, begin, width in groups:
        for jx in range(4):
            columns = []
            for jy in range(4):
                start = pl.multiple_of(((place_x ^ jx) * 4 + (place_y ^ jy)) * 128, 128)
                columns.append(jnp.concatenate([left[:, pl.ds(start, 128)] for left in lefts], axis=0))
            left = jnp.concatenate(columns, axis=1)
            for s in range(0, width, tile):
                n = min(tile, width - s)
                cube = dot_t(left, right[:, begin + s : begin + s + n]).astype(BF).reshape(4, 4, 32, n)
                for b in range(n // 128):
                    block = at + s // 128 + b
                    piece = cube[:, :, :, b * 128 : (b + 1) * 128]
                    for part in range(2):
                        for number, slots in enumerate((SEND[part], KEEP[part])):
                            if jx in slots:
                                outs[2 * part + number][slots.index(jx), :, block] = piece[:, part]
                            for slot in range(2):
                                outs[4 + 2 * part + number][slot, jx, block] = piece[slots[slot], 2 + part]
        at += width // 128


def gradient_shapes(width):
    return [jax.ShapeDtypeStruct((2, 4, width // 128, 32, 128), BF)] * 8


def mlp_kernel(tile, split, place_ref, h2_a, h2_b, wg, wu, wd, cot_a, cot_b, near, hid_ref, dgate_ref, dup_ref, *outs):
    units = wg.shape[1]
    h2 = jnp.concatenate((h2_a[...], h2_b[...]), axis=0)
    cot = jnp.concatenate((cot_a[...], cot_b[...]), axis=0)
    for s in range(0, units, tile):
        cut = slice(s, min(s + tile, units))
        gate = dot(h2, wg[:, cut])
        up = dot(h2, wu[:, cut])
        dh = dot_rt(cot, wd[cut, :])
        sig = jax.nn.sigmoid(gate)
        active = gate * sig
        hid_ref[:, cut] = (active * up).astype(BF)
        dgate_ref[:, cut] = (dh * up * (sig + active * (1.0 - sig))).astype(BF)
        dup_ref[:, cut] = (dh * active).astype(BF)
    gradient_body(place_ref, [((cot_a, cot_b), hid_ref, 0, units), ((h2_a, h2_b), dgate_ref, 0, split)], outs)


def mlp(place_xy, h2_halves, wg, wu, wd, cot_halves, near, split, tile=512):
    half, width = h2_halves[0].shape
    every = 2 * half
    units = wg.shape[1]
    got = pl.pallas_call(
        functools.partial(mlp_kernel, tile, split),
        out_shape=[jax.ShapeDtypeStruct((every, units), BF)] * 3 + gradient_shapes(units + split),
        in_specs=[smem()] + [vmem()] * 8,
        out_specs=[vmem()] * 11,
        compiler_params=params(14),
        name="mlp",
        cost_estimate=cost(18),
    )(place_xy, *h2_halves, wg, wu, wd, *cot_halves, near)
    return (*got[:3], got[3:])


def mlp_back_kernel(step, split, place_ref, dgate, dup, wg, wu, h2_a, h2_b, high_ref, low_ref, gain_ref, *outs):
    half, width = h2_a.shape
    for s in range(0, width, step):
        cut = slice(s, s + step)
        part = dot_rt(dgate[...], wg[cut, :]) + dot_rt(dup[...], wu[cut, :])
        high_ref[:, cut] = part[:half]
        low_ref[:, cut] = part[half:].astype(BF)
        gain_ref[:, cut] = jnp.sum(part[:half] * h2_a[:, cut].astype(F32), axis=0, keepdims=True) + jnp.sum(
            part[half:] * h2_b[:, cut].astype(F32), axis=0, keepdims=True
        )
    units = dup.shape[1]
    lefts = (h2_a, h2_b)
    gradient_body(place_ref, [(lefts, dgate, split, units - split), (lefts, dup, 0, units)], outs)


def mlp_back(place_xy, dgate, dup, wg, wu, h2_halves, split, step=512):
    half, width = h2_halves[0].shape
    got = pl.pallas_call(
        functools.partial(mlp_back_kernel, step, split),
        out_shape=[
            jax.ShapeDtypeStruct((half, width), F32),
            jax.ShapeDtypeStruct((half, width), BF),
            jax.ShapeDtypeStruct((1, width), F32),
        ]
        + gradient_shapes(2 * wg.shape[1] - split),
        in_specs=[smem()] + [vmem()] * 6,
        out_specs=[vmem()] * 11,
        compiler_params=params(12),
        name="mlp_back",
        cost_estimate=cost(14),
    )(place_xy, dgate, dup, wg, wu, *h2_halves)
    return (*got[:3], got[3:])


def touch_kernel(*refs):
    *sources, target = refs
    total = jnp.zeros(target.shape, F32)
    for source in sources:
        total = total + source[:16, :128].astype(F32)
    target[...] = total


def touch(*arrays):
    return pl.pallas_call(
        touch_kernel,
        out_shape=jax.ShapeDtypeStruct((16, 128), F32),
        in_specs=[vmem()] * len(arrays),
        out_specs=vmem(),
        compiler_params=params(12),
        name="touch",
        cost_estimate=cost(2),
    )(*arrays)


def pair_kernel(above, below, later, target):
    rows = above.shape[0]
    target[:rows] = above[...]
    target[rows:] = below[...]


def pair(above, below, later):
    rows, width = above.shape
    return pl.pallas_call(
        pair_kernel,
        out_shape=jax.ShapeDtypeStruct((2 * rows, width), above.dtype),
        in_specs=[vmem()] * 2 + [pl.BlockSpec(memory_space=pl.ANY)],
        out_specs=vmem(),
        compiler_params=params(4),
        name="pair",
        cost_estimate=cost(8),
    )(above, below, later)


def chip_kernel(high, got, *refs):
    total = high[...] + got[...].astype(F32)
    rows = total.shape[0] // 2
    chip, send = refs
    chip[...] = total[: chip.shape[0]]
    send[:rows] = total[rows:].astype(BF)
    if send.shape[0] > rows:
        send[rows:] = total[:rows].astype(BF)


def chip_sums(high, got, both=True):
    rows, width = high.shape[0] // 2, high.shape[1]
    count = 2 * rows if both else rows
    return pl.pallas_call(
        chip_kernel,
        out_shape=(jax.ShapeDtypeStruct((count, width), F32), jax.ShapeDtypeStruct((count, width), BF)),
        in_specs=[vmem()] * 2,
        out_specs=[vmem()] * 2,
        compiler_params=params(6),
        name="chip_sums",
        cost_estimate=cost(1),
    )(high, got)


def middle_kernel(own, across, chip, got, gain, mid_ref, h2_ref):
    mid = jnp.concatenate((own[...], across[...]), axis=0).astype(F32) + chip[...] + got[...].astype(F32)
    inverse = lax.rsqrt(jnp.mean(mid * mid, axis=-1, keepdims=True) + EPSILON)
    mid_ref[...] = mid
    h2_ref[...] = (mid * inverse * gain[...].astype(F32)).astype(BF)


def middle(own, across, chip, got, gain):
    return pl.pallas_call(
        middle_kernel,
        out_shape=(jax.ShapeDtypeStruct(chip.shape, F32), jax.ShapeDtypeStruct(chip.shape, BF)),
        in_specs=[vmem()] * 5,
        out_specs=[vmem()] * 2,
        compiler_params=params(8),
        name="middle",
        cost_estimate=cost(2),
    )(own, across, chip, got, gain)


def middle_back_kernel(mid_ref, cot, chip, got, gain, own, top, rest):
    mid = mid_ref[...]
    inverse = lax.rsqrt(jnp.mean(mid * mid, axis=-1, keepdims=True) + EPSILON)
    normed = mid * inverse
    scaled = (chip[...] + got[...].astype(F32)) * gain[...].astype(F32)
    grad = cot[...].astype(F32) + inverse * (scaled - normed * jnp.mean(scaled * normed, axis=-1, keepdims=True))
    own[...] = grad[: own.shape[0]]
    top[...] = grad[: top.shape[0]].astype(BF)
    rest[...] = grad[top.shape[0] :].astype(BF)


def middle_back(mid, cot, chip, got, gain, cut):
    half, width = mid.shape
    return pl.pallas_call(
        middle_back_kernel,
        out_shape=(
            jax.ShapeDtypeStruct((half // 2, width), F32),
            jax.ShapeDtypeStruct((cut, width), BF),
            jax.ShapeDtypeStruct((half - cut, width), BF),
        ),
        in_specs=[vmem()] * 5,
        out_specs=[vmem()] * 3,
        compiler_params=params(8),
        name="middle_back",
        cost_estimate=cost(2),
    )(mid, cot, chip, got, gain)


def output_kernel(step, hid, wd, high_ref, low_ref):
    half = high_ref.shape[0]
    for s in range(0, wd.shape[1], step):
        cut = slice(s, s + step)
        part = dot(hid[...], wd[:, cut])
        high_ref[:, cut] = part[:half].astype(BF)
        low_ref[:, cut] = part[half:].astype(BF)


def output(hid, wd, step=512):
    shape = jax.ShapeDtypeStruct((hid.shape[0] // 2, wd.shape[1]), BF)
    return pl.pallas_call(
        functools.partial(output_kernel, step),
        out_shape=[shape] * 2,
        in_specs=[vmem()] * 2,
        out_specs=[vmem()] * 2,
        compiler_params=params(8),
        name="output",
        cost_estimate=cost(4),
    )(hid, wd)


def combine_kernel(sums, *refs):
    out = refs[-1]
    at = 0
    for count, terms in sums:
        total = None
        for number, start in terms:
            term = refs[number][start : start + count].astype(F32)
            total = term if total is None else total + term
        out[at : at + count] = total.astype(out.dtype)
        at += count


def combine(sums, time=0.5):
    arrays, plan = [], []
    for terms in sums:
        listed = []
        for array, start, count in terms:
            known = [i for i, a in enumerate(arrays) if a is array]
            if not known:
                arrays.append(array)
            listed.append((known[0] if known else len(arrays) - 1, start))
        plan.append((terms[0][2], listed))
    total = sum(count for count, _ in plan)
    return pl.pallas_call(
        functools.partial(combine_kernel, plan),
        out_shape=jax.ShapeDtypeStruct((total, 32, 128), BF),
        in_specs=[vmem()] * len(arrays),
        out_specs=vmem(),
        compiler_params=params(8),
        name="combine",
        cost_estimate=cost(time),
    )(*arrays)


def ends_kernel(sums, extra, place_ref, *refs):
    give, keep = refs[-2:]
    at = 0
    if extra:
        total = None
        for number, start in extra:
            term = refs[number][start : start + 1].astype(F32)
            total = term if total is None else total + term
        give[0:1] = total.astype(BF)
        keep[0:1] = total.astype(BF).astype(F32)
        at = 1
    for parts in sums:
        count = parts[0][0]
        totals = []
        for _, terms in parts:
            total = None
            for number, start in terms:
                term = refs[number][start : start + count].astype(F32)
                total = term if total is None else total + term
            totals.append(total)
        for half in range(2):
            cut = slice(at, at + count)
            give[cut] = jnp.where(place_ref[2] == 0, totals[2 + half], totals[half]).astype(BF)
            keep[cut] = jnp.where(place_ref[2] == 0, totals[half], totals[2 + half])
            at += count


def ends(place, sums, extra=()):
    arrays, plan = [], []
    for parts in sums:
        planned = []
        for terms in parts:
            listed = []
            for array, start, count in terms:
                known = [i for i, a in enumerate(arrays) if a is array]
                if not known:
                    arrays.append(array)
                listed.append((known[0] if known else len(arrays) - 1, start))
            planned.append((terms[0][2], listed))
        plan.append(planned)
    arrays += [array for array, _, _ in extra]
    more = [(len(arrays) - len(extra) + i, start) for i, (_, start, _) in enumerate(extra)]
    total = sum(2 * parts[0][0] for parts in plan) + bool(extra)
    return pl.pallas_call(
        functools.partial(ends_kernel, plan, more),
        out_shape=(jax.ShapeDtypeStruct((total, 32, 128), BF), jax.ShapeDtypeStruct((total, 32, 128), F32)),
        in_specs=[smem()] + [vmem()] * len(arrays),
        out_specs=[vmem()] * 2,
        compiler_params=params(16),
        name="ends",
        cost_estimate=cost(1),
    )(place, *arrays)


def attention_back_kernel(
    docs, place_ref, place_xy, mid_a, mid_b, mid_c, mid_d, qkv, lse_ref, h1, o_ref, wq, wk, wv, wo, cos, sin, gain_two, *refs
):
    dqkv_ref, high_ref, low_ref, gains, *outs, bias_ref, do_ref = refs
    half = mid_a.shape[0] + mid_b.shape[0]
    rows, every = half // 2, 2 * half
    q_width = wq.shape[1]
    heads = q_width // HD
    width = wq.shape[0]
    scale = 1.0 / math.sqrt(HD)
    mid = jnp.concatenate((mid_a[...], mid_b[...], mid_c[...], mid_d[...]), axis=0)
    do_ref[...] = dot_rt(mid, wo[...]).astype(BF)
    ends = doc_ends(place_ref, docs)
    places_q, opening_q = places_of(place_ref[0], ends, rows, (1, every), 1)
    places_k, _ = places_of(place_ref[0], ends, rows, (every, 1), 0)
    bias_ref[...] = jnp.where((places_k <= places_q) & (places_k >= opening_q), 0.0, MASKED)
    keys = qkv[:, q_width : q_width + HD]
    vals = qkv[:, q_width + HD : q_width + 2 * HD]
    dk = jnp.zeros((every, HD), F32)
    dv = jnp.zeros((every, HD), F32)
    table_c, table_s = cos[...], sin[...]

    def unrope(values):
        wide_now = values.shape[1]
        return values * wide(table_c, wide_now) - swap_halves(values) * wide(table_s, wide_now)

    for pair in range(heads // 2):
        dqs = []
        for head in (2 * pair, 2 * pair + 1):
            cut = slice(head * HD, (head + 1) * HD)
            query = qkv[:, cut]
            grad_o = do_ref[:, cut]
            scores = dot_rt(keys, query) * scale + bias_ref[...]
            chances = jnp.exp(scores - lse_ref[head : head + 1, :])
            grad_chances = dot_rt(vals, grad_o)
            centre = jnp.sum(chances * grad_chances, axis=0, keepdims=True)
            grad_scores = (chances * (grad_chances - centre)).astype(BF)
            dv = dv + dot(chances.astype(BF), grad_o)
            dk = dk + dot(grad_scores, query)
            dqs.append(dot_t(grad_scores, keys))
        dq = jnp.concatenate(dqs, axis=1) * scale
        dqkv_ref[:, pair * 2 * HD : (pair + 1) * 2 * HD] = unrope(dq).astype(BF)
    both = jnp.concatenate((dk * scale, dv), axis=1)
    lane = lax.broadcasted_iota(jnp.int32, both.shape, 1)
    dqkv_ref[:, q_width:] = jnp.where(lane < HD, unrope(both), both).astype(BF)
    joined = jnp.concatenate((wk[...], wv[...]), axis=0)
    step = 512
    for s in range(0, width, step):
        part = dot_rt(dqkv_ref[:, :q_width], wq[s : s + step, :]) + dot(dqkv_ref[:, q_width:], joined[:, s : s + step])
        high_ref[:, s : s + step] = part[:half]
        low_ref[:, s : s + step] = part[half:].astype(BF)
        gain_one = jnp.sum(part * h1[:, s : s + step].astype(F32), axis=0, keepdims=True)
        for lane in range(0, step, 128):
            row = (s + lane) // 128
            gains[0, row : row + 1, :] = gain_one[:, lane : lane + 128]
            gains[0, width // 128 + row : width // 128 + row + 1, :] = gain_two[:, s + lane : s + lane + 128]
    gradient_body(place_xy, [((h1,), dqkv_ref, 0, q_width + 2 * HD), ((mid_a, mid_b, mid_c, mid_d), o_ref, 0, q_width)], outs)


def attention_back(place_docs, place_xy, mids, qkv, lse, h1, o, wq, wk, wv, wo, cos, sin, gain_two_part):
    half, width = mids[0].shape[0] + mids[1].shape[0], mids[0].shape[1]
    every = 2 * half
    q_width = wq.shape[1]
    got = pl.pallas_call(
        functools.partial(attention_back_kernel, place_docs.shape[0] - 1),
        out_shape=[
            jax.ShapeDtypeStruct((every, q_width + 2 * HD), BF),
            jax.ShapeDtypeStruct((half, width), F32),
            jax.ShapeDtypeStruct((half, width), BF),
            jax.ShapeDtypeStruct((1, width // 64, 128), F32),
        ]
        + gradient_shapes(2 * q_width + 2 * HD),
        in_specs=[smem()] * 2 + [vmem()] * 15,
        out_specs=[vmem()] * 12,
        scratch_shapes=[
            pltpu.VMEM((every, every), F32),
            pltpu.VMEM((every, q_width), BF),
        ],
        compiler_params=params(12),
        name="attention_back",
        cost_estimate=cost(19),
    )(place_docs, place_xy, *mids, qkv, lse, h1, o, wq, wk.T, wv.T, wo, cos, sin, gain_two_part)
    return (*got[1:4], got[4:])


def lay_out_kernel(plan, keep, got, *outs):
    for out, parts in zip(outs, plan):
        for start, blocks, first, width, to in parts:
            for half in range(2):
                for b in range(blocks):
                    low, high = max(128 * b, first), min(128 * (b + 1), first + width)
                    if low >= high:
                        continue
                    at = start + half * blocks + b
                    total = keep[at] + got[at].astype(F32)
                    out[32 * half : 32 * (half + 1), to + low - first : to + high - first] = total[:, low - 128 * b : high - 128 * b]


def lay_out(keep, got, plan):
    widths = [sum(part[3] for part in parts) for parts in plan]
    return pl.pallas_call(
        functools.partial(lay_out_kernel, plan),
        out_shape=[jax.ShapeDtypeStruct((64, width), F32) for width in widths],
        in_specs=[vmem()] * 2,
        out_specs=[vmem()] * len(plan),
        compiler_params=params(12),
        name="lay_out",
        cost_estimate=cost(1),
    )(keep, got)


def rotary_tables(offset):
    half_size = HD // 2
    freqs = THETA ** (-(jnp.arange(half_size, dtype=F32) * 2.0 / HD))
    angles = offset.astype(F32)[:, None] * freqs[None, :]
    cosine, sine = jnp.cos(angles), jnp.sin(angles)
    return jnp.concatenate((cosine,) * 4, axis=1), jnp.concatenate((-sine, sine) * 2, axis=1)


def over_core(values):
    return lax.ppermute(values, "tensor", [(t, t ^ 1) for t in range(4)])


def over_z(values):
    return lax.ppermute(values, "tensor", [(t, t ^ 2) for t in range(4)])


def over_diagonal(values):
    return lax.ppermute(values, "tensor", [(t, t ^ 3) for t in range(4)])


def over_x(values, xor):
    return lax.ppermute(values, "dp", [(d, d ^ (xor * 8)) for d in range(32)])


def over_y(values, xor):
    return lax.ppermute(values, "dp", [(d, d ^ (xor * 2)) for d in range(32)])


def over_z_hi(values):
    return lax.ppermute(values, "dp", [(d, d ^ 1) for d in range(32)])


def after(value, *others):
    return lax.optimization_barrier((value, *others))[0] if others else value


def add(*terms):
    total = terms[0].astype(F32)
    for term in terms[1:]:
        total = total + term.astype(F32)
    return total


def norm(values):
    inverse = lax.rsqrt(jnp.mean(values * values, axis=-1, keepdims=True) + EPSILON)
    return values * inverse, inverse


def norm_back(normed, inverse, gain, grads):
    scaled = grads * gain
    return inverse * (scaled - normed * jnp.mean(scaled * normed, axis=-1, keepdims=True))


LINKS = ((over_x, 1), (over_x, 3), (over_y, 1), (over_y, 3))
ROUTES = ((0, 1, 2, 3), (1, 0, 3, 2), (2, 3, 0, 1), (3, 2, 1, 0))


class Reduction:
    def __init__(self, arrays, joined=False):
        self.joined = joined
        self.blocks = arrays[0].shape[2]
        self.sends = [arrays[2 * part].reshape(-1, 32, 128) for part in range(4)]
        self.kept = [[(arrays[2 * part + 1].reshape(-1, 32, 128), self.starts(0, 8))] for part in range(4)]
        self.near, self.far, self.last = {}, {}, {}

    def starts(self, at, rows):
        return {row: at + row * self.blocks for row in range(rows)}

    def route(self, part, step):
        return ROUTES[part - part % 2 if self.joined and step >= 2 else part][step]

    def order(self, part):
        return ((1, 3), (3, 1))[0 if self.joined else part % 2]

    def row(self, part, row, rows=1):
        return [(array, starts[row], rows * self.blocks) for array, starts in self.kept[part]]

    def sum(self, part, step):
        first, second = self.order(part)
        if step == 0:
            return [(self.sends[part], 0, 8 * self.blocks)]
        if step == 1:
            return self.row(part, 4, 4)
        if step == 2:
            return self.row(part, min(first, 2), 2)
        if step == 3:
            return self.row(part, second) + [self.far[part]]
        return self.row(part, 0) + self.near.get(part, []) + [self.last[part]]

    def take(self, part, step, got, at):
        n = self.blocks
        if step < 2:
            self.kept[part].append((got, self.starts(at, 8 - 4 * step)))
        elif step == 2:
            near, far = (0, 1) if self.order(part)[0] == 1 else (1, 0)
            self.near[part] = [(got, at + near * n, n)]
            self.far[part] = (got, at + far * n, n)
        else:
            self.last[part] = (got, at, n)


def fold(jobs, time=0.5):
    folded = []
    for part in range(4):
        sums, places = [], []
        at = 0
        for r, rows in jobs:
            rows = {"last": (0, r.order(part)[1]), "own": (0,)}.get(rows, rows)
            starts = {}
            for row in rows:
                terms = r.row(part, row)
                if row == 0:
                    terms = terms + r.near.get(part, [])
                sums.append(terms)
                starts[row] = at
                at += r.blocks
            r.near.pop(part, None)
            places.append((r, starts))
        array = combine(sums, time)
        folded.append(array)
        for r, starts in places:
            r.kept[part] = [(array, starts)]
    return folded


class Gains:
    def __init__(self, block):
        self.held = [(block, 0)]

    def terms(self):
        return [(array, start, 1) for array, start in self.held]

    def exchange(self, hop, before):
        sent = sum(array[start : start + 1].astype(F32) for array, start in self.held).astype(BF)
        self.held = [(sent, 0), (hop(after(sent, *before)), 0)]


def takers(jobs, link):
    return [(r, part, step) for r, step in jobs for part in range(4) if r.route(part, step) == link]


def prepare(jobs, gains=None, gains_link=None):
    operands = []
    for link in range(4):
        taken = takers(jobs, link)
        if not taken:
            operands.append(None)
            continue
        if len(taken) == 1 and taken[0][2] == 0:
            operands.append(taken[0][0].sends[taken[0][1]])
            continue
        sums = [r.sum(part, step) for r, part, step in taken]
        operands.append(combine(sums + ([gains.terms()] if link == gains_link else [])))
    return operands


def send(jobs, operands, before=None, anchor=(), gains=None, gains_link=None):
    arrived = []
    for link, (operand, (hop, xor)) in enumerate(zip(operands, LINKS)):
        if operand is None:
            arrived.append(before[link])
            continue
        got = hop(after(operand, *before[link]) if before else operand, xor)
        arrived.append((got,))
        got = after(got, *anchor)
        at = 0
        for r, part, step in takers(jobs, link):
            r.take(part, step, got, at)
            at += r.blocks * (8, 4, 2, 1)[step]
        if link == gains_link:
            gains.held = [(operand, at), (got, at)]
    return arrived


def stage(jobs, before=None, **more):
    return send(jobs, prepare(jobs, **more), before, **more)


def finish(reductions, place, plan, before=(), gains=None, anchor=None):
    keep, give = None, None
    give, keep = ends(
        place,
        [[r.sum(part, 4) for part in range(4)] for r in reductions],
        gains.terms() if gains else (),
    )
    got = over_z_hi(after(give, *before))
    if anchor is not None:
        got = after(got, anchor)
    outs = lay_out(keep, got, plan)
    if gains:
        total = add(keep[0], got[0])
        outs = (*outs, (total + over_core(total)) + (over_z(total) + over_diagonal(total)))
    return outs


def per_device(
    tokens,
    attn_gain,
    query_weight,
    key_weight,
    value_weight,
    out_weight,
    mlp_gain,
    gate_weight,
    up_weight,
    down_weight,
    cotangent,
    doc_lengths,
):
    rows = tokens.shape[0]
    place_dp = lax.axis_index("dp")
    place_t = lax.axis_index("tensor")
    place_xy = jnp.stack((place_dp // 8, (place_dp // 2) % 4, place_dp % 2))
    q_width = query_weight.shape[1]
    gain_one, gain_two = attn_gain.astype(F32), mlp_gain.astype(F32)

    across = over_z(tokens)
    places = jnp.concatenate(
        [(place_t ^ j) * rows + jnp.arange(rows, dtype=jnp.int32) for j in (0, 2, 1, 3)]
    )
    opening, ending = jnp.zeros_like(places), jnp.int32(0)
    for number in range(doc_lengths.shape[0]):
        ending = ending + doc_lengths[number]
        opening = jnp.maximum(opening, jnp.where(places >= ending, ending, 0))
    cos, sin = rotary_tables(places - opening)
    place_docs = jnp.concatenate((place_t[None], doc_lengths))
    attn_row, mlp_row = attn_gain.reshape(1, -1), mlp_gain.reshape(1, -1)
    near = touch(query_weight, out_weight)
    across, cos, sin, place_docs, place_xy, attn_row, mlp_row, near = lax.optimization_barrier(
        (across, cos, sin, place_docs, place_xy, attn_row, mlp_row, near)
    )
    token_blocks = (tokens, across, over_core(tokens), over_core(across))

    cot_across = over_z(after(cotangent, across))
    h1, qkv, heads_out, lse, high, low = attention(
        place_docs, token_blocks, attn_row, query_weight, key_weight, value_weight, out_weight, cos, sin, near
    )
    cot_pair = pair(cotangent, cot_across, low)
    chip, low = chip_sums(high, after(over_core(low), cot_pair))
    z_sums = over_z(low)
    cot_halves = (cot_pair, over_core(after(cot_pair, chip)))
    near = touch(after(gate_weight, cot_halves[1]), up_weight, down_weight)
    mid, h2 = middle(tokens, across, chip, after(z_sums, near), mlp_row)
    h2 = (h2, over_core(h2))
    units = gate_weight.shape[1]
    split = units // 2 // 128 * 128 + 128
    hidden, grad_gate_val, grad_up_val, first = mlp(
        place_xy, h2, gate_weight, up_weight, down_weight, cot_halves, near, split
    )
    first_sum = Reduction(first)
    first_links = stage([(first_sum, 0)])
    high, low, gain_two_part, second = mlp_back(
        place_xy, after(grad_gate_val, first[0]), grad_up_val, gate_weight, up_weight, h2, split
    )
    chip, low = chip_sums(high, after(over_core(low), *[link[0] for link in first_links]))
    second_sum = Reduction(second)
    links = stage([(second_sum, 0)], first_links)
    z_sums = after(over_z(low), *fold([(first_sum, range(8))]))
    grad_own, *mid_low = middle_back(mid, cot_pair, chip, z_sums, mlp_row, rows + rows // 2)
    mid_low = (*mid_low, over_core(mid_low[0]), over_core(mid_low[1]))

    jobs = [(first_sum, 1), (second_sum, 1)]
    operands = prepare(jobs)
    high, low, gains, attn = attention_back(
        place_docs, place_xy, mid_low, after(qkv, *operands), lse, h1, heads_out,
        query_weight, key_weight, value_weight, out_weight, cos, sin, gain_two_part,
    )
    links = send(jobs, operands, links, (low,))
    attn_sum = Reduction(attn, joined=True)
    gains = Gains(gains)
    own, other = chip_sums(high, after(over_core(low), *[link[0] for link in links]), False)
    jobs = [(first_sum, 2), (second_sum, 2), (attn_sum, 0)]
    operands = prepare(jobs, gains, 0)
    folded = fold([(first_sum, "last"), (second_sum, "last")])
    out_high, out_low = output(after(hidden, low), down_weight)
    links = send(jobs, operands, links, (*folded, out_low), gains, 0)
    grad_h1 = own + over_z(other).astype(F32)
    result_got = over_core(after(out_low, grad_h1))
    result_chip = add(out_high, result_got)
    result_z = over_z(result_chip[rows:].astype(BF))
    result = (mid[:rows] + result_chip[:rows] + result_z.astype(F32)).astype(BF)
    jobs = [(first_sum, 3), (second_sum, 3), (attn_sum, 1)]
    operands = prepare(jobs, gains, 1)
    folded = fold([(first_sum, "own"), (second_sum, "own"), (attn_sum, range(4))])
    links = send(jobs, operands, links, folded, gains, 1)
    blocks, more = first_sum.blocks, second_sum.blocks
    plan = [
        [(0, blocks, 0, units, 0)],
        [(0, blocks, units, split, 0), (2 * blocks, more, 0, units - split, split)],
        [(2 * blocks, more, units - split, units, 0)],
    ]
    out_down, out_gate, out_up = finish([first_sum, second_sum], place_xy, plan)
    links = stage([(attn_sum, 2)], links, gains=gains, gains_link=2)
    links = [(*link, result_z) for link in links]
    links = stage([(attn_sum, 3)], links, gains=gains, gains_link=3)
    cuts = ((0, q_width), (q_width, HD), (q_width + HD, HD), (q_width + 2 * HD, q_width))
    plan = [[(1, attn_sum.blocks, first, width, 0)] for first, width in cuts]
    out_query, out_key, out_value, out_out, grad_gains = finish([attn_sum], place_xy, plan, [], gains, out_up)
    grad_gains = grad_gains.reshape(2, -1)

    normed, inverse = norm(tokens.astype(F32))
    grad_tokens = grad_own + norm_back(normed, inverse, gain_one, grad_h1)
    return (
        result,
        grad_tokens.astype(BF),
        grad_gains[0] / gain_one,
        out_query,
        out_key,
        out_value,
        out_out.T,
        grad_gains[1] / gain_two,
        out_gate,
        out_up,
        out_down.T,
    )


def solution(mesh):
    in_specs = (
        P(("dp", "tensor"), None),
        P(),
        P(None, "tensor"),
        P(None, "tensor"),
        P(None, "tensor"),
        P("tensor", None),
        P(),
        P(None, "tensor"),
        P(None, "tensor"),
        P("tensor", None),
        P(("dp", "tensor"), None),
        P("dp"),
    )
    out_specs = (
        P(("dp", "tensor"), None),
        P(("dp", "tensor"), None),
        P(),
        P("dp", "tensor"),
        P("dp", "tensor"),
        P("dp", "tensor"),
        P("tensor", "dp"),
        P(),
        P("dp", "tensor"),
        P("dp", "tensor"),
        P("tensor", "dp"),
    )
    return jax.shard_map(
        per_device, mesh=mesh, in_specs=in_specs, out_specs=out_specs, check_vma=False
    )
```

```python
import functools
import math

import jax
import jax.numpy as jnp
from jax import lax
from jax.experimental import pallas as pl
from jax.experimental.pallas import tpu as pltpu
from jax.sharding import PartitionSpec as P

HD = 64
EPSILON = 1e-05
THETA = 10000.0
MASKED = -1000000000.0
BF = jnp.bfloat16
F32 = jnp.float32
MIB = 1024 * 1024


def cost(time):
    return pl.CostEstimate(flops=int(time * 1e9), bytes_accessed=1024, transcendentals=0)


def dot(left, right):
    return jnp.dot(left, right, preferred_element_type=F32)


def dot_t(left, right):
    return lax.dot_general(left, right, (((0,), (0,)), ((), ())), preferred_element_type=F32)


def dot_rt(left, right):
    return lax.dot_general(left, right, (((1,), (1,)), ((), ())), preferred_element_type=F32)


def vmem():
    return pl.BlockSpec(memory_space=pltpu.VMEM)


def smem():
    return pl.BlockSpec(memory_space=pltpu.SMEM)


def hbm():
    return pl.BlockSpec(memory_space=pl.ANY)


def params(size):
    return pltpu.CompilerParams(vmem_limit_bytes=size * MIB)


def swap_halves(values):
    width = values.shape[1]
    lane = lax.broadcasted_iota(jnp.int32, values.shape, 1)
    return jnp.where(
        lane % HD < HD // 2,
        pltpu.roll(values, width - HD // 2, 1),
        pltpu.roll(values, HD // 2, 1),
    )


def wide(table, width):
    return jnp.concatenate([table] * (width // table.shape[1]), axis=1) if width > table.shape[1] else table[:, :width]


def places_of(place_t, ends, rows, shape, axis):
    index = lax.broadcasted_iota(jnp.int32, shape, axis)
    block = index // rows
    order = jnp.where(block == 0, 0, jnp.where(block == 1, 2, jnp.where(block == 2, 1, 3)))
    places = (place_t ^ order) * rows + index % rows
    opening = jnp.zeros(shape, jnp.int32)
    for end in ends:
        opening = jnp.maximum(opening, jnp.where(places >= end, end, 0))
    return places, opening


def doc_ends(place_ref, count):
    ends, total = [], jnp.int32(0)
    for i in range(count):
        total = total + place_ref[1 + i]
        ends.append(total)
    return ends


def attention_kernel(
    docs, place_ref, own, zpart, cpart, diag, gain, wq, wk, wv, wo, cos, sin, near,
    h1_ref, qkv_ref, o_ref, lse_ref, high_ref, low_ref, bias_ref,
):
    rows = own.shape[0]
    every = 4 * rows
    half = 2 * rows
    q_width = wq.shape[1]
    heads = q_width // HD
    gain_row = gain[...].astype(F32)
    for number, block in enumerate((own, zpart, cpart, diag)):
        values = block[...].astype(F32)
        inverse = lax.rsqrt(jnp.mean(values * values, axis=-1, keepdims=True) + EPSILON)
        h1_ref[number * rows : (number + 1) * rows, :] = (values * inverse * gain_row).astype(BF)
    h1 = h1_ref[...]
    joined = jnp.concatenate((wk[...], wv[...]), axis=0)
    table_c, table_s = cos[...], sin[...]

    def rope(values):
        width = values.shape[1]
        return values * wide(table_c, width) + swap_halves(values) * wide(table_s, width)

    scale = 1.0 / math.sqrt(HD)
    kv = dot_rt(h1, joined)
    lane = lax.broadcasted_iota(jnp.int32, kv.shape, 1)
    qkv_ref[:, q_width:] = jnp.where(lane < HD, rope(kv), kv).astype(BF)
    qkv_ref[:, :q_width] = rope(dot(h1, wq[...])).astype(BF)

    ends = doc_ends(place_ref, docs)
    places_q, opening_q = places_of(place_ref[0], ends, rows, (every, 1), 0)
    places_k, _ = places_of(place_ref[0], ends, rows, (1, every), 1)
    bias_ref[...] = jnp.where((places_k <= places_q) & (places_k >= opening_q), 0.0, MASKED)

    keys = qkv_ref[:, q_width : q_width + HD]
    kv_low = qkv_ref[:, q_width:]
    lane = lax.broadcasted_iota(jnp.int32, kv_low.shape, 1)
    ones_vals = jnp.where(lane < HD, jnp.ones_like(kv_low), kv_low)
    lse_lane = lax.broadcasted_iota(jnp.int32, (every, 128), 1)
    lse = jnp.zeros((every, 128), F32)
    for head in range(heads):
        query = qkv_ref[:, head * HD : (head + 1) * HD]
        scores = dot_rt(query, keys) * scale + bias_ref[...]
        highest = jnp.max(scores, axis=-1, keepdims=True)
        raised = jnp.exp(scores - highest)
        mixed = dot(raised.astype(BF), ones_vals)
        totals = mixed[:, :1]
        o_ref[:, head * HD : (head + 1) * HD] = (mixed[:, HD:] / totals).astype(BF)
        lse = jnp.where(lse_lane == head, highest + jnp.log(totals), lse)
    lse_ref[...] = lse.T[:heads, :]
    high_ref[...] = dot(o_ref[:half, :], wo[...])
    low_ref[...] = dot(o_ref[half:, :], wo[...]).astype(BF)


def attention(place_docs, blocks, gain, wq, wk, wv, wo, cos, sin, near):
    rows, width = blocks[0].shape
    every = rows * 4
    q_width = wq.shape[1]
    heads = q_width // HD
    shapes = (
        jax.ShapeDtypeStruct((every, width), BF),
        jax.ShapeDtypeStruct((every, q_width + 2 * HD), BF),
        jax.ShapeDtypeStruct((every, q_width), BF),
        jax.ShapeDtypeStruct((heads, every), F32),
        jax.ShapeDtypeStruct((2 * rows, width), F32),
        jax.ShapeDtypeStruct((2 * rows, width), BF),
    )
    return pl.pallas_call(
        functools.partial(attention_kernel, place_docs.shape[0] - 1),
        out_shape=shapes,
        in_specs=[smem()] + [vmem()] * 12,
        out_specs=[vmem()] * 6,
        scratch_shapes=[pltpu.VMEM((every, every), F32)],
        compiler_params=params(12),
        name="attention",
        cost_estimate=cost(11),
    )(place_docs, *blocks, gain, wq, wk.T, wv.T, wo, cos, sin, near)


SEND = ((1, 2), (3, 2))
KEEP = ((0, 3), (0, 1))


def gradient_body(place_ref, groups, outs, tile=512):
    place_x, place_y = place_ref[0], place_ref[1]
    at = 0
    for lefts, right, begin, width in groups:
        for jx in range(4):
            columns = []
            for jy in range(4):
                start = pl.multiple_of(((place_x ^ jx) * 4 + (place_y ^ jy)) * 128, 128)
                columns.append(jnp.concatenate([left[:, pl.ds(start, 128)] for left in lefts], axis=0))
            left = jnp.concatenate(columns, axis=1)
            for s in range(0, width, tile):
                n = min(tile, width - s)
                cube = dot_t(left, right[:, begin + s : begin + s + n]).astype(BF).reshape(4, 4, 32, n)
                for b in range(n // 128):
                    block = at + s // 128 + b
                    piece = cube[:, :, :, b * 128 : (b + 1) * 128]
                    for part in range(2):
                        for number, slots in enumerate((SEND[part], KEEP[part])):
                            if jx in slots:
                                outs[2 * part + number][slots.index(jx), :, block] = piece[:, part]
                            for slot in range(2):
                                outs[4 + 2 * part + number][slot, jx, block] = piece[slots[slot], 2 + part]
        at += width // 128


def gradient_shapes(width):
    return [jax.ShapeDtypeStruct((2, 4, width // 128, 32, 128), BF)] * 8


def mlp_kernel(tile, split, place_ref, h2_a, h2_b, wg, wu, wd, cot_a, cot_b, near, hid_ref, dgate_ref, dup_ref, *outs):
    units = wg.shape[1]
    h2 = jnp.concatenate((h2_a[...], h2_b[...]), axis=0)
    cot = jnp.concatenate((cot_a[...], cot_b[...]), axis=0)
    for s in range(0, units, tile):
        cut = slice(s, min(s + tile, units))
        gate = dot(h2, wg[:, cut])
        up = dot(h2, wu[:, cut])
        dh = dot_rt(cot, wd[cut, :])
        sig = jax.nn.sigmoid(gate)
        active = gate * sig
        hid_ref[:, cut] = (active * up).astype(BF)
        dgate_ref[:, cut] = (dh * up * (sig + active * (1.0 - sig))).astype(BF)
        dup_ref[:, cut] = (dh * active).astype(BF)
    gradient_body(place_ref, [((cot_a, cot_b), hid_ref, 0, units), ((h2_a, h2_b), dgate_ref, 0, split)], outs)


def mlp(place_xy, h2_halves, wg, wu, wd, cot_halves, near, split, tile=512):
    half, width = h2_halves[0].shape
    every = 2 * half
    units = wg.shape[1]
    got = pl.pallas_call(
        functools.partial(mlp_kernel, tile, split),
        out_shape=[jax.ShapeDtypeStruct((every, units), BF)] * 3 + gradient_shapes(units + split),
        in_specs=[smem()] + [vmem()] * 8,
        out_specs=[vmem()] * 11,
        compiler_params=params(14),
        name="mlp",
        cost_estimate=cost(18),
    )(place_xy, *h2_halves, wg, wu, wd, *cot_halves, near)
    return (*got[:3], got[3:])


def mlp_back_kernel(step, split, place_ref, dgate, dup, wg, wu, h2_a, h2_b, high_ref, low_ref, gain_ref, *outs):
    half, width = h2_a.shape
    for s in range(0, width, step):
        cut = slice(s, s + step)
        part = dot_rt(dgate[...], wg[cut, :]) + dot_rt(dup[...], wu[cut, :])
        high_ref[:, cut] = part[:half]
        low_ref[:, cut] = part[half:].astype(BF)
        gain_ref[:, cut] = jnp.sum(part[:half] * h2_a[:, cut].astype(F32), axis=0, keepdims=True) + jnp.sum(
            part[half:] * h2_b[:, cut].astype(F32), axis=0, keepdims=True
        )
    units = dup.shape[1]
    lefts = (h2_a, h2_b)
    gradient_body(place_ref, [(lefts, dgate, split, units - split), (lefts, dup, 0, units)], outs)


def mlp_back(place_xy, dgate, dup, wg, wu, h2_halves, split, step=512):
    half, width = h2_halves[0].shape
    got = pl.pallas_call(
        functools.partial(mlp_back_kernel, step, split),
        out_shape=[
            jax.ShapeDtypeStruct((half, width), F32),
            jax.ShapeDtypeStruct((half, width), BF),
            jax.ShapeDtypeStruct((1, width), F32),
        ]
        + gradient_shapes(2 * wg.shape[1] - split),
        in_specs=[smem()] + [vmem()] * 6,
        out_specs=[vmem()] * 11,
        compiler_params=params(12),
        name="mlp_back",
        cost_estimate=cost(14),
    )(place_xy, dgate, dup, wg, wu, *h2_halves)
    return (*got[:3], got[3:])


def touch_kernel(*refs):
    *sources, target = refs
    total = jnp.zeros(target.shape, F32)
    for source in sources:
        total = total + source[:16, :128].astype(F32)
    target[...] = total


def touch(*arrays):
    return pl.pallas_call(
        touch_kernel,
        out_shape=jax.ShapeDtypeStruct((16, 128), F32),
        in_specs=[vmem()] * len(arrays),
        out_specs=vmem(),
        compiler_params=params(12),
        name="touch",
        cost_estimate=cost(2),
    )(*arrays)


def pair_kernel(above, below, later, target):
    rows = above.shape[0]
    target[:rows] = above[...]
    target[rows:] = below[...]


def pair(above, below, later):
    rows, width = above.shape
    return pl.pallas_call(
        pair_kernel,
        out_shape=jax.ShapeDtypeStruct((2 * rows, width), above.dtype),
        in_specs=[vmem()] * 2 + [pl.BlockSpec(memory_space=pl.ANY)],
        out_specs=vmem(),
        compiler_params=params(4),
        name="pair",
        cost_estimate=cost(8),
    )(above, below, later)


def chip_kernel(high, got, *refs):
    total = high[...] + got[...].astype(F32)
    rows = total.shape[0] // 2
    chip, send = refs
    chip[...] = total[: chip.shape[0]]
    send[:rows] = total[rows:].astype(BF)
    if send.shape[0] > rows:
        send[rows:] = total[:rows].astype(BF)


def chip_sums(high, got, both=True):
    rows, width = high.shape[0] // 2, high.shape[1]
    count = 2 * rows if both else rows
    return pl.pallas_call(
        chip_kernel,
        out_shape=(jax.ShapeDtypeStruct((count, width), F32), jax.ShapeDtypeStruct((count, width), BF)),
        in_specs=[vmem()] * 2,
        out_specs=[vmem()] * 2,
        compiler_params=params(6),
        name="chip_sums",
        cost_estimate=cost(1),
    )(high, got)


def middle_kernel(own, across, chip, got, gain, mid_ref, h2_ref):
    mid = jnp.concatenate((own[...], across[...]), axis=0).astype(F32) + chip[...] + got[...].astype(F32)
    inverse = lax.rsqrt(jnp.mean(mid * mid, axis=-1, keepdims=True) + EPSILON)
    mid_ref[...] = mid
    h2_ref[...] = (mid * inverse * gain[...].astype(F32)).astype(BF)


def middle(own, across, chip, got, gain):
    return pl.pallas_call(
        middle_kernel,
        out_shape=(jax.ShapeDtypeStruct(chip.shape, F32), jax.ShapeDtypeStruct(chip.shape, BF)),
        in_specs=[vmem()] * 5,
        out_specs=[vmem()] * 2,
        compiler_params=params(8),
        name="middle",
        cost_estimate=cost(2),
    )(own, across, chip, got, gain)


def middle_back_kernel(mid_ref, cot, chip, got, gain, own, top, rest):
    mid = mid_ref[...]
    inverse = lax.rsqrt(jnp.mean(mid * mid, axis=-1, keepdims=True) + EPSILON)
    normed = mid * inverse
    scaled = (chip[...] + got[...].astype(F32)) * gain[...].astype(F32)
    grad = cot[...].astype(F32) + inverse * (scaled - normed * jnp.mean(scaled * normed, axis=-1, keepdims=True))
    own[...] = grad[: own.shape[0]]
    top[...] = grad[: top.shape[0]].astype(BF)
    rest[...] = grad[top.shape[0] :].astype(BF)


def middle_back(mid, cot, chip, got, gain, cut):
    half, width = mid.shape
    return pl.pallas_call(
        middle_back_kernel,
        out_shape=(
            jax.ShapeDtypeStruct((half // 2, width), F32),
            jax.ShapeDtypeStruct((cut, width), BF),
            jax.ShapeDtypeStruct((half - cut, width), BF),
        ),
        in_specs=[vmem()] * 5,
        out_specs=[vmem()] * 3,
        compiler_params=params(8),
        name="middle_back",
        cost_estimate=cost(2),
    )(mid, cot, chip, got, gain)


def output_kernel(step, hid, wd, high_ref, low_ref):
    half = high_ref.shape[0]
    for s in range(0, wd.shape[1], step):
        cut = slice(s, s + step)
        part = dot(hid[...], wd[:, cut])
        high_ref[:, cut] = part[:half].astype(BF)
        low_ref[:, cut] = part[half:].astype(BF)


def output(hid, wd, step=512):
    shape = jax.ShapeDtypeStruct((hid.shape[0] // 2, wd.shape[1]), BF)
    return pl.pallas_call(
        functools.partial(output_kernel, step),
        out_shape=[shape] * 2,
        in_specs=[vmem()] * 2,
        out_specs=[vmem()] * 2,
        compiler_params=params(8),
        name="output",
        cost_estimate=cost(4),
    )(hid, wd)


def combine_kernel(sums, *refs):
    out = refs[-1]
    at = 0
    for count, terms in sums:
        total = None
        for number, start in terms:
            term = refs[number][start : start + count].astype(F32)
            total = term if total is None else total + term
        out[at : at + count] = total.astype(out.dtype)
        at += count


def combine(sums, time=0.5):
    arrays, plan = [], []
    for terms in sums:
        listed = []
        for array, start, count in terms:
            known = [i for i, a in enumerate(arrays) if a is array]
            if not known:
                arrays.append(array)
            listed.append((known[0] if known else len(arrays) - 1, start))
        plan.append((terms[0][2], listed))
    total = sum(count for count, _ in plan)
    return pl.pallas_call(
        functools.partial(combine_kernel, plan),
        out_shape=jax.ShapeDtypeStruct((total, 32, 128), BF),
        in_specs=[vmem()] * len(arrays),
        out_specs=vmem(),
        compiler_params=params(8),
        name="combine",
        cost_estimate=cost(time),
    )(*arrays)


def ends_kernel(sums, extra, place_ref, *refs):
    give, keep = refs[-2:]
    at = 0
    if extra:
        total = None
        for number, start in extra:
            term = refs[number][start : start + 1].astype(F32)
            total = term if total is None else total + term
        give[0:1] = total.astype(BF)
        keep[0:1] = total.astype(BF).astype(F32)
        at = 1
    for parts in sums:
        count = parts[0][0]
        totals = []
        for _, terms in parts:
            total = None
            for number, start in terms:
                term = refs[number][start : start + count].astype(F32)
                total = term if total is None else total + term
            totals.append(total)
        for half in range(2):
            cut = slice(at, at + count)
            give[cut] = jnp.where(place_ref[2] == 0, totals[2 + half], totals[half]).astype(BF)
            keep[cut] = jnp.where(place_ref[2] == 0, totals[half], totals[2 + half])
            at += count


def ends(place, sums, extra=()):
    arrays, plan = [], []
    for parts in sums:
        planned = []
        for terms in parts:
            listed = []
            for array, start, count in terms:
                known = [i for i, a in enumerate(arrays) if a is array]
                if not known:
                    arrays.append(array)
                listed.append((known[0] if known else len(arrays) - 1, start))
            planned.append((terms[0][2], listed))
        plan.append(planned)
    arrays += [array for array, _, _ in extra]
    more = [(len(arrays) - len(extra) + i, start) for i, (_, start, _) in enumerate(extra)]
    total = sum(2 * parts[0][0] for parts in plan) + bool(extra)
    return pl.pallas_call(
        functools.partial(ends_kernel, plan, more),
        out_shape=(jax.ShapeDtypeStruct((total, 32, 128), BF), jax.ShapeDtypeStruct((total, 32, 128), F32)),
        in_specs=[smem()] + [vmem()] * len(arrays),
        out_specs=[vmem()] * 2,
        compiler_params=params(16),
        name="ends",
        cost_estimate=cost(1),
    )(place, *arrays)


def attention_back_kernel(
    docs, place_ref, place_xy, mid_a, mid_b, mid_c, mid_d, qkv, lse_ref, h1, o_ref, wq, wk, wv, wo, cos, sin, gain_two, *refs
):
    dqkv_ref, high_ref, low_ref, gains, *outs, bias_ref, do_ref = refs
    half = mid_a.shape[0] + mid_b.shape[0]
    rows, every = half // 2, 2 * half
    q_width = wq.shape[1]
    heads = q_width // HD
    width = wq.shape[0]
    scale = 1.0 / math.sqrt(HD)
    mid = jnp.concatenate((mid_a[...], mid_b[...], mid_c[...], mid_d[...]), axis=0)
    do_ref[...] = dot_rt(mid, wo[...]).astype(BF)
    ends = doc_ends(place_ref, docs)
    places_q, opening_q = places_of(place_ref[0], ends, rows, (1, every), 1)
    places_k, _ = places_of(place_ref[0], ends, rows, (every, 1), 0)
    bias_ref[...] = jnp.where((places_k <= places_q) & (places_k >= opening_q), 0.0, MASKED)
    keys = qkv[:, q_width : q_width + HD]
    vals = qkv[:, q_width + HD : q_width + 2 * HD]
    dk = jnp.zeros((every, HD), F32)
    dv = jnp.zeros((every, HD), F32)
    table_c, table_s = cos[...], sin[...]

    def unrope(values):
        wide_now = values.shape[1]
        return values * wide(table_c, wide_now) - swap_halves(values) * wide(table_s, wide_now)

    for pair in range(heads // 2):
        dqs = []
        for head in (2 * pair, 2 * pair + 1):
            cut = slice(head * HD, (head + 1) * HD)
            query = qkv[:, cut]
            grad_o = do_ref[:, cut]
            scores = dot_rt(keys, query) * scale + bias_ref[...]
            chances = jnp.exp(scores - lse_ref[head : head + 1, :])
            grad_chances = dot_rt(vals, grad_o)
            centre = jnp.sum(chances * grad_chances, axis=0, keepdims=True)
            grad_scores = (chances * (grad_chances - centre)).astype(BF)
            dv = dv + dot(chances.astype(BF), grad_o)
            dk = dk + dot(grad_scores, query)
            dqs.append(dot_t(grad_scores, keys))
        dq = jnp.concatenate(dqs, axis=1) * scale
        dqkv_ref[:, pair * 2 * HD : (pair + 1) * 2 * HD] = unrope(dq).astype(BF)
    both = jnp.concatenate((dk * scale, dv), axis=1)
    lane = lax.broadcasted_iota(jnp.int32, both.shape, 1)
    dqkv_ref[:, q_width:] = jnp.where(lane < HD, unrope(both), both).astype(BF)
    joined = jnp.concatenate((wk[...], wv[...]), axis=0)
    step = 512
    for s in range(0, width, step):
        part = dot_rt(dqkv_ref[:, :q_width], wq[s : s + step, :]) + dot(dqkv_ref[:, q_width:], joined[:, s : s + step])
        high_ref[:, s : s + step] = part[:half]
        low_ref[:, s : s + step] = part[half:].astype(BF)
        gain_one = jnp.sum(part * h1[:, s : s + step].astype(F32), axis=0, keepdims=True)
        for lane in range(0, step, 128):
            row = (s + lane) // 128
            gains[0, row : row + 1, :] = gain_one[:, lane : lane + 128]
            gains[0, width // 128 + row : width // 128 + row + 1, :] = gain_two[:, s + lane : s + lane + 128]
    gradient_body(place_xy, [((h1,), dqkv_ref, 0, q_width + 2 * HD), ((mid_a, mid_b, mid_c, mid_d), o_ref, 0, q_width)], outs)


def attention_back(place_docs, place_xy, mids, qkv, lse, h1, o, wq, wk, wv, wo, cos, sin, gain_two_part):
    half, width = mids[0].shape[0] + mids[1].shape[0], mids[0].shape[1]
    every = 2 * half
    q_width = wq.shape[1]
    got = pl.pallas_call(
        functools.partial(attention_back_kernel, place_docs.shape[0] - 1),
        out_shape=[
            jax.ShapeDtypeStruct((every, q_width + 2 * HD), BF),
            jax.ShapeDtypeStruct((half, width), F32),
            jax.ShapeDtypeStruct((half, width), BF),
            jax.ShapeDtypeStruct((1, width // 64, 128), F32),
        ]
        + gradient_shapes(2 * q_width + 2 * HD),
        in_specs=[smem()] * 2 + [vmem()] * 15,
        out_specs=[vmem()] * 12,
        scratch_shapes=[
            pltpu.VMEM((every, every), F32),
            pltpu.VMEM((every, q_width), BF),
        ],
        compiler_params=params(12),
        name="attention_back",
        cost_estimate=cost(19),
    )(place_docs, place_xy, *mids, qkv, lse, h1, o, wq, wk.T, wv.T, wo, cos, sin, gain_two_part)
    return (*got[1:4], got[4:])


def lay_out_kernel(plan, keep, got, *outs):
    for out, parts in zip(outs, plan):
        for start, blocks, first, width, to in parts:
            for half in range(2):
                for b in range(blocks):
                    low, high = max(128 * b, first), min(128 * (b + 1), first + width)
                    if low >= high:
                        continue
                    at = start + half * blocks + b
                    total = keep[at] + got[at].astype(F32)
                    out[32 * half : 32 * (half + 1), to + low - first : to + high - first] = total[:, low - 128 * b : high - 128 * b]


def lay_out(keep, got, plan):
    widths = [sum(part[3] for part in parts) for parts in plan]
    return pl.pallas_call(
        functools.partial(lay_out_kernel, plan),
        out_shape=[jax.ShapeDtypeStruct((64, width), F32) for width in widths],
        in_specs=[vmem()] * 2,
        out_specs=[vmem()] * len(plan),
        compiler_params=params(12),
        name="lay_out",
        cost_estimate=cost(1),
    )(keep, got)


def rotary_tables(offset):
    half_size = HD // 2
    freqs = THETA ** (-(jnp.arange(half_size, dtype=F32) * 2.0 / HD))
    angles = offset.astype(F32)[:, None] * freqs[None, :]
    cosine, sine = jnp.cos(angles), jnp.sin(angles)
    return jnp.concatenate((cosine,) * 4, axis=1), jnp.concatenate((-sine, sine) * 2, axis=1)


def over_core(values):
    return lax.ppermute(values, "tensor", [(t, t ^ 1) for t in range(4)])


def over_z(values):
    return lax.ppermute(values, "tensor", [(t, t ^ 2) for t in range(4)])


def over_diagonal(values):
    return lax.ppermute(values, "tensor", [(t, t ^ 3) for t in range(4)])


def over_x(values, xor):
    return lax.ppermute(values, "dp", [(d, d ^ (xor * 8)) for d in range(32)])


def over_y(values, xor):
    return lax.ppermute(values, "dp", [(d, d ^ (xor * 2)) for d in range(32)])


def over_z_hi(values):
    return lax.ppermute(values, "dp", [(d, d ^ 1) for d in range(32)])


def after(value, *others):
    return lax.optimization_barrier((value, *others))[0] if others else value


def add(*terms):
    total = terms[0].astype(F32)
    for term in terms[1:]:
        total = total + term.astype(F32)
    return total


def norm(values):
    inverse = lax.rsqrt(jnp.mean(values * values, axis=-1, keepdims=True) + EPSILON)
    return values * inverse, inverse


def norm_back(normed, inverse, gain, grads):
    scaled = grads * gain
    return inverse * (scaled - normed * jnp.mean(scaled * normed, axis=-1, keepdims=True))


LINKS = ((over_x, 1), (over_x, 3), (over_y, 1), (over_y, 3))
ROUTES = ((0, 1, 2, 3), (1, 0, 3, 2), (2, 3, 0, 1), (3, 2, 1, 0))


class Reduction:
    def __init__(self, arrays, joined=False):
        self.joined = joined
        self.blocks = arrays[0].shape[2]
        self.sends = [arrays[2 * part].reshape(-1, 32, 128) for part in range(4)]
        self.kept = [[(arrays[2 * part + 1].reshape(-1, 32, 128), self.starts(0, 8))] for part in range(4)]
        self.near, self.far, self.last = {}, {}, {}

    def starts(self, at, rows):
        return {row: at + row * self.blocks for row in range(rows)}

    def route(self, part, step):
        return ROUTES[part - part % 2 if self.joined and step >= 2 else part][step]

    def order(self, part):
        return ((1, 3), (3, 1))[0 if self.joined else part % 2]

    def row(self, part, row, rows=1):
        return [(array, starts[row], rows * self.blocks) for array, starts in self.kept[part]]

    def sum(self, part, step):
        first, second = self.order(part)
        if step == 0:
            return [(self.sends[part], 0, 8 * self.blocks)]
        if step == 1:
            return self.row(part, 4, 4)
        if step == 2:
            return self.row(part, min(first, 2), 2)
        if step == 3:
            return self.row(part, second) + [self.far[part]]
        return self.row(part, 0) + self.near.get(part, []) + [self.last[part]]

    def take(self, part, step, got, at):
        n = self.blocks
        if step < 2:
            self.kept[part].append((got, self.starts(at, 8 - 4 * step)))
        elif step == 2:
            near, far = (0, 1) if self.order(part)[0] == 1 else (1, 0)
            self.near[part] = [(got, at + near * n, n)]
            self.far[part] = (got, at + far * n, n)
        else:
            self.last[part] = (got, at, n)


def fold(jobs, time=0.5):
    folded = []
    for part in range(4):
        sums, places = [], []
        at = 0
        for r, rows in jobs:
            rows = {"last": (0, r.order(part)[1]), "own": (0,)}.get(rows, rows)
            starts = {}
            for row in rows:
                terms = r.row(part, row)
                if row == 0:
                    terms = terms + r.near.get(part, [])
                sums.append(terms)
                starts[row] = at
                at += r.blocks
            r.near.pop(part, None)
            places.append((r, starts))
        array = combine(sums, time)
        folded.append(array)
        for r, starts in places:
            r.kept[part] = [(array, starts)]
    return folded


class Gains:
    def __init__(self, block):
        self.held = [(block, 0)]

    def terms(self):
        return [(array, start, 1) for array, start in self.held]

    def exchange(self, hop, before):
        sent = sum(array[start : start + 1].astype(F32) for array, start in self.held).astype(BF)
        self.held = [(sent, 0), (hop(after(sent, *before)), 0)]


def takers(jobs, link):
    return [(r, part, step) for r, step in jobs for part in range(4) if r.route(part, step) == link]


def prepare(jobs, gains=None, gains_link=None):
    operands = []
    for link in range(4):
        taken = takers(jobs, link)
        if not taken:
            operands.append(None)
            continue
        if len(taken) == 1 and taken[0][2] == 0:
            operands.append(taken[0][0].sends[taken[0][1]])
            continue
        sums = [r.sum(part, step) for r, part, step in taken]
        operands.append(combine(sums + ([gains.terms()] if link == gains_link else [])))
    return operands


def send(jobs, operands, before=None, anchor=(), gains=None, gains_link=None):
    arrived = []
    for link, (operand, (hop, xor)) in enumerate(zip(operands, LINKS)):
        if operand is None:
            arrived.append(before[link])
            continue
        got = hop(after(operand, *before[link]) if before else operand, xor)
        arrived.append((got,))
        got = after(got, *anchor)
        at = 0
        for r, part, step in takers(jobs, link):
            r.take(part, step, got, at)
            at += r.blocks * (8, 4, 2, 1)[step]
        if link == gains_link:
            gains.held = [(operand, at), (got, at)]
    return arrived


def stage(jobs, before=None, **more):
    return send(jobs, prepare(jobs, **more), before, **more)


def finish(reductions, place, gains=None):
    give, keep = ends(
        place,
        [[r.sum(part, 4) for part in range(4)] for r in reductions],
        gains.terms() if gains else (),
    )
    return keep, over_z_hi(give)


def per_device(
    tokens,
    attn_gain,
    query_weight,
    key_weight,
    value_weight,
    out_weight,
    mlp_gain,
    gate_weight,
    up_weight,
    down_weight,
    cotangent,
    doc_lengths,
):
    rows = tokens.shape[0]
    place_dp = lax.axis_index("dp")
    place_t = lax.axis_index("tensor")
    place_xy = jnp.stack((place_dp // 8, (place_dp // 2) % 4, place_dp % 2))
    q_width = query_weight.shape[1]
    gain_one, gain_two = attn_gain.astype(F32), mlp_gain.astype(F32)

    across = over_z(tokens)
    places = jnp.concatenate(
        [(place_t ^ j) * rows + jnp.arange(rows, dtype=jnp.int32) for j in (0, 2, 1, 3)]
    )
    opening, ending = jnp.zeros_like(places), jnp.int32(0)
    for number in range(doc_lengths.shape[0]):
        ending = ending + doc_lengths[number]
        opening = jnp.maximum(opening, jnp.where(places >= ending, ending, 0))
    cos, sin = rotary_tables(places - opening)
    place_docs = jnp.concatenate((place_t[None], doc_lengths))
    attn_row, mlp_row = attn_gain.reshape(1, -1), mlp_gain.reshape(1, -1)
    near = touch(query_weight, out_weight)
    across, cos, sin, place_docs, place_xy, attn_row, mlp_row, near = lax.optimization_barrier(
        (across, cos, sin, place_docs, place_xy, attn_row, mlp_row, near)
    )
    token_blocks = (tokens, across, over_core(tokens), over_core(across))

    cot_across = over_z(after(cotangent, across))
    h1, qkv, heads_out, lse, high, low = attention(
        place_docs, token_blocks, attn_row, query_weight, key_weight, value_weight, out_weight, cos, sin, near
    )
    cot_pair = pair(cotangent, cot_across, low)
    chip, low = chip_sums(high, after(over_core(low), cot_pair))
    z_sums = over_z(low)
    cot_halves = (cot_pair, over_core(after(cot_pair, chip)))
    near = touch(after(gate_weight, cot_halves[1]), up_weight, down_weight)
    mid, h2 = middle(tokens, across, chip, after(z_sums, near), mlp_row)
    h2 = (h2, over_core(h2))
    units = gate_weight.shape[1]
    split = units // 2 // 128 * 128 + 128
    hidden, grad_gate_val, grad_up_val, first = mlp(
        place_xy, h2, gate_weight, up_weight, down_weight, cot_halves, near, split
    )
    first_sum = Reduction(first)
    first_links = stage([(first_sum, 0)])
    high, low, gain_two_part, second = mlp_back(
        place_xy, after(grad_gate_val, first[0]), grad_up_val, gate_weight, up_weight, h2, split
    )
    chip, low = chip_sums(high, after(over_core(low), *[link[0] for link in first_links]))
    second_sum = Reduction(second)
    links = stage([(second_sum, 0)], first_links)
    z_sums = after(over_z(low), *fold([(first_sum, range(8))]))
    grad_own, *mid_low = middle_back(mid, cot_pair, chip, z_sums, mlp_row, rows + rows // 2)
    mid_low = (*mid_low, over_core(mid_low[0]), over_core(mid_low[1]))

    jobs = [(first_sum, 1), (second_sum, 1)]
    operands = prepare(jobs)
    high, low, gains, attn = attention_back(
        place_docs, place_xy, mid_low, after(qkv, *operands), lse, h1, heads_out,
        query_weight, key_weight, value_weight, out_weight, cos, sin, gain_two_part,
    )
    links = send(jobs, operands, links, (low,))
    attn_sum = Reduction(attn, joined=True)
    gains = Gains(gains)
    own, other = chip_sums(high, after(over_core(low), *[link[0] for link in links]), False)
    jobs = [(first_sum, 2), (second_sum, 2), (attn_sum, 0)]
    operands = prepare(jobs, gains, 0)
    folded = fold([(first_sum, "last"), (second_sum, "last")])
    other = over_z(other)
    out_high, out_low = output(after(hidden, other), down_weight)
    links = send(jobs, operands, links, (*folded, out_low), gains, 0)
    grad_h1 = own + other.astype(F32)
    result_got = over_core(after(out_low, grad_h1))
    result_chip = add(out_high, result_got)
    result_z = over_z(result_chip[rows:].astype(BF))
    result = (mid[:rows] + result_chip[:rows] + result_z.astype(F32)).astype(BF)
    jobs = [(first_sum, 3), (second_sum, 3), (attn_sum, 1)]
    operands = prepare(jobs, gains, 1)
    folded = fold([(first_sum, "own"), (second_sum, "own"), (attn_sum, range(4))])
    links = send(jobs, operands, links, folded, gains, 1)
    blocks, more = first_sum.blocks, second_sum.blocks
    plan = [
        [(0, blocks, 0, units, 0)],
        [(0, blocks, units, split, 0), (2 * blocks, more, 0, units - split, split)],
        [(2 * blocks, more, units - split, units, 0)],
    ]
    first_ends = finish([first_sum, second_sum], place_xy)
    links = stage([(attn_sum, 2)], links, gains=gains, gains_link=2)
    links = [(*link, result_z) for link in links]
    links = stage([(attn_sum, 3)], links, gains=gains, gains_link=3)
    keep, got = finish([attn_sum], place_xy, gains)
    out_down, out_gate, out_up = lay_out(first_ends[0], after(first_ends[1], keep), plan)
    got = after(got, out_up)
    cuts = ((0, q_width), (q_width, HD), (q_width + HD, HD), (q_width + 2 * HD, q_width))
    plan = [[(1, attn_sum.blocks, first, width, 0)] for first, width in cuts]
    out_query, out_key, out_value, out_out = lay_out(keep, got, plan)
    total = add(keep[0], got[0])
    grad_gains = (total + over_core(total)) + (over_z(total) + over_diagonal(total))
    grad_gains = grad_gains.reshape(2, -1)

    normed, inverse = norm(tokens.astype(F32))
    grad_tokens = grad_own + norm_back(normed, inverse, gain_one, grad_h1)
    return (
        result,
        grad_tokens.astype(BF),
        grad_gains[0] / gain_one,
        out_query,
        out_key,
        out_value,
        out_out.T,
        grad_gains[1] / gain_two,
        out_gate,
        out_up,
        out_down.T,
    )


def solution(mesh):
    in_specs = (
        P(("dp", "tensor"), None),
        P(),
        P(None, "tensor"),
        P(None, "tensor"),
        P(None, "tensor"),
        P("tensor", None),
        P(),
        P(None, "tensor"),
        P(None, "tensor"),
        P("tensor", None),
        P(("dp", "tensor"), None),
        P("dp"),
    )
    out_specs = (
        P(("dp", "tensor"), None),
        P(("dp", "tensor"), None),
        P(),
        P("dp", "tensor"),
        P("dp", "tensor"),
        P("dp", "tensor"),
        P("tensor", "dp"),
        P(),
        P("dp", "tensor"),
        P("dp", "tensor"),
        P("tensor", "dp"),
    )
    return jax.shard_map(
        per_device, mesh=mesh, in_specs=in_specs, out_specs=out_specs, check_vma=False
    )
```

```python
import functools
import math

import jax
import jax.numpy as jnp
from jax import lax
from jax.experimental import pallas as pl
from jax.experimental.pallas import tpu as pltpu
from jax.sharding import PartitionSpec as P

HD = 64
EPSILON = 1e-05
THETA = 10000.0
MASKED = -1000000000.0
BF = jnp.bfloat16
F32 = jnp.float32
MIB = 1024 * 1024


def cost(time):
    return pl.CostEstimate(flops=int(time * 1e9), bytes_accessed=1024, transcendentals=0)


def dot(left, right):
    return jnp.dot(left, right, preferred_element_type=F32)


def dot_t(left, right):
    return lax.dot_general(left, right, (((0,), (0,)), ((), ())), preferred_element_type=F32)


def dot_rt(left, right):
    return lax.dot_general(left, right, (((1,), (1,)), ((), ())), preferred_element_type=F32)


def vmem():
    return pl.BlockSpec(memory_space=pltpu.VMEM)


def smem():
    return pl.BlockSpec(memory_space=pltpu.SMEM)


def hbm():
    return pl.BlockSpec(memory_space=pl.ANY)


def params(size):
    return pltpu.CompilerParams(vmem_limit_bytes=size * MIB)


def swap_halves(values):
    width = values.shape[1]
    lane = lax.broadcasted_iota(jnp.int32, values.shape, 1)
    return jnp.where(
        lane % HD < HD // 2,
        pltpu.roll(values, width - HD // 2, 1),
        pltpu.roll(values, HD // 2, 1),
    )


def wide(table, width):
    return jnp.concatenate([table] * (width // table.shape[1]), axis=1) if width > table.shape[1] else table[:, :width]


def places_of(place_t, ends, rows, shape, axis):
    index = lax.broadcasted_iota(jnp.int32, shape, axis)
    block = index // rows
    order = jnp.where(block == 0, 0, jnp.where(block == 1, 2, jnp.where(block == 2, 1, 3)))
    places = (place_t ^ order) * rows + index % rows
    opening = jnp.zeros(shape, jnp.int32)
    for end in ends:
        opening = jnp.maximum(opening, jnp.where(places >= end, end, 0))
    return places, opening


def doc_ends(place_ref, count):
    ends, total = [], jnp.int32(0)
    for i in range(count):
        total = total + place_ref[1 + i]
        ends.append(total)
    return ends


def attention_kernel(
    docs, place_ref, own, zpart, cpart, diag, gain, wq, wk, wv, wo, cos, sin, near,
    h1_ref, qkv_ref, o_ref, lse_ref, high_ref, low_ref, bias_ref,
):
    rows = own.shape[0]
    every = 4 * rows
    half = 2 * rows
    q_width = wq.shape[1]
    heads = q_width // HD
    gain_row = gain[...].astype(F32)
    for number, block in enumerate((own, zpart, cpart, diag)):
        values = block[...].astype(F32)
        inverse = lax.rsqrt(jnp.mean(values * values, axis=-1, keepdims=True) + EPSILON)
        h1_ref[number * rows : (number + 1) * rows, :] = (values * inverse * gain_row).astype(BF)
    h1 = h1_ref[...]
    joined = jnp.concatenate((wk[...], wv[...]), axis=0)
    table_c, table_s = cos[...], sin[...]

    def rope(values):
        width = values.shape[1]
        return values * wide(table_c, width) + swap_halves(values) * wide(table_s, width)

    scale = 1.0 / math.sqrt(HD)
    kv = dot_rt(h1, joined)
    lane = lax.broadcasted_iota(jnp.int32, kv.shape, 1)
    qkv_ref[:, q_width:] = jnp.where(lane < HD, rope(kv), kv).astype(BF)
    qkv_ref[:, :q_width] = rope(dot(h1, wq[...])).astype(BF)

    ends = doc_ends(place_ref, docs)
    places_q, opening_q = places_of(place_ref[0], ends, rows, (every, 1), 0)
    places_k, _ = places_of(place_ref[0], ends, rows, (1, every), 1)
    bias_ref[...] = jnp.where((places_k <= places_q) & (places_k >= opening_q), 0.0, MASKED)

    keys = qkv_ref[:, q_width : q_width + HD]
    kv_low = qkv_ref[:, q_width:]
    lane = lax.broadcasted_iota(jnp.int32, kv_low.shape, 1)
    ones_vals = jnp.where(lane < HD, jnp.ones_like(kv_low), kv_low)
    lse_lane = lax.broadcasted_iota(jnp.int32, (every, 128), 1)
    lse = jnp.zeros((every, 128), F32)
    for head in range(heads):
        query = qkv_ref[:, head * HD : (head + 1) * HD]
        scores = dot_rt(query, keys) * scale + bias_ref[...]
        highest = jnp.max(scores, axis=-1, keepdims=True)
        raised = jnp.exp(scores - highest)
        mixed = dot(raised.astype(BF), ones_vals)
        totals = mixed[:, :1]
        o_ref[:, head * HD : (head + 1) * HD] = (mixed[:, HD:] / totals).astype(BF)
        lse = jnp.where(lse_lane == head, highest + jnp.log(totals), lse)
    lse_ref[...] = lse.T[:heads, :]
    high_ref[...] = dot(o_ref[:half, :], wo[...])
    low_ref[...] = dot(o_ref[half:, :], wo[...]).astype(BF)


def attention(place_docs, blocks, gain, wq, wk, wv, wo, cos, sin, near):
    rows, width = blocks[0].shape
    every = rows * 4
    q_width = wq.shape[1]
    heads = q_width // HD
    shapes = (
        jax.ShapeDtypeStruct((every, width), BF),
        jax.ShapeDtypeStruct((every, q_width + 2 * HD), BF),
        jax.ShapeDtypeStruct((every, q_width), BF),
        jax.ShapeDtypeStruct((heads, every), F32),
        jax.ShapeDtypeStruct((2 * rows, width), F32),
        jax.ShapeDtypeStruct((2 * rows, width), BF),
    )
    return pl.pallas_call(
        functools.partial(attention_kernel, place_docs.shape[0] - 1),
        out_shape=shapes,
        in_specs=[smem()] + [vmem()] * 12,
        out_specs=[vmem()] * 6,
        scratch_shapes=[pltpu.VMEM((every, every), F32)],
        compiler_params=params(12),
        name="attention",
        cost_estimate=cost(11),
    )(place_docs, *blocks, gain, wq, wk.T, wv.T, wo, cos, sin, near)


SEND = ((1, 2), (3, 2))
KEEP = ((0, 3), (0, 1))


def gradient_body(place_ref, groups, outs, tile=512):
    place_x, place_y = place_ref[0], place_ref[1]
    at = 0
    for lefts, right, begin, width in groups:
        for jx in range(4):
            columns = []
            for jy in range(4):
                start = pl.multiple_of(((place_x ^ jx) * 4 + (place_y ^ jy)) * 128, 128)
                columns.append(jnp.concatenate([left[:, pl.ds(start, 128)] for left in lefts], axis=0))
            left = jnp.concatenate(columns, axis=1)
            for s in range(0, width, tile):
                n = min(tile, width - s)
                cube = dot_t(left, right[:, begin + s : begin + s + n]).astype(BF).reshape(4, 4, 32, n)
                for b in range(n // 128):
                    block = at + s // 128 + b
                    piece = cube[:, :, :, b * 128 : (b + 1) * 128]
                    for part in range(2):
                        for number, slots in enumerate((SEND[part], KEEP[part])):
                            if jx in slots:
                                outs[2 * part + number][slots.index(jx), :, block] = piece[:, part]
                            for slot in range(2):
                                outs[4 + 2 * part + number][slot, jx, block] = piece[slots[slot], 2 + part]
        at += width // 128


def gradient_shapes(width):
    return [jax.ShapeDtypeStruct((2, 4, width // 128, 32, 128), BF)] * 8


def mlp_kernel(tile, split, place_ref, h2_a, h2_b, wg, wu, wd, cot_a, cot_b, near, hid_ref, dgate_ref, dup_ref, *outs):
    units = wg.shape[1]
    h2 = jnp.concatenate((h2_a[...], h2_b[...]), axis=0)
    cot = jnp.concatenate((cot_a[...], cot_b[...]), axis=0)
    for s in range(0, units, tile):
        cut = slice(s, min(s + tile, units))
        gate = dot(h2, wg[:, cut])
        up = dot(h2, wu[:, cut])
        dh = dot_rt(cot, wd[cut, :])
        sig = jax.nn.sigmoid(gate)
        active = gate * sig
        hid_ref[:, cut] = (active * up).astype(BF)
        dgate_ref[:, cut] = (dh * up * (sig + active * (1.0 - sig))).astype(BF)
        dup_ref[:, cut] = (dh * active).astype(BF)
    gradient_body(place_ref, [((cot_a, cot_b), hid_ref, 0, units), ((h2_a, h2_b), dgate_ref, 0, split)], outs)


def mlp(place_xy, h2_halves, wg, wu, wd, cot_halves, near, split, tile=512):
    half, width = h2_halves[0].shape
    every = 2 * half
    units = wg.shape[1]
    got = pl.pallas_call(
        functools.partial(mlp_kernel, tile, split),
        out_shape=[jax.ShapeDtypeStruct((every, units), BF)] * 3 + gradient_shapes(units + split),
        in_specs=[smem()] + [vmem()] * 8,
        out_specs=[vmem()] * 11,
        compiler_params=params(14),
        name="mlp",
        cost_estimate=cost(18),
    )(place_xy, *h2_halves, wg, wu, wd, *cot_halves, near)
    return (*got[:3], got[3:])


def mlp_back_kernel(step, split, place_ref, dgate, dup, wg, wu, h2_a, h2_b, high_ref, low_ref, gain_ref, *outs):
    half, width = h2_a.shape
    for s in range(0, width, step):
        cut = slice(s, s + step)
        part = dot_rt(dgate[...], wg[cut, :]) + dot_rt(dup[...], wu[cut, :])
        high_ref[:, cut] = part[:half]
        low_ref[:, cut] = part[half:].astype(BF)
        gain_ref[:, cut] = jnp.sum(part[:half] * h2_a[:, cut].astype(F32), axis=0, keepdims=True) + jnp.sum(
            part[half:] * h2_b[:, cut].astype(F32), axis=0, keepdims=True
        )
    units = dup.shape[1]
    lefts = (h2_a, h2_b)
    gradient_body(place_ref, [(lefts, dgate, split, units - split), (lefts, dup, 0, units)], outs)


def mlp_back(place_xy, dgate, dup, wg, wu, h2_halves, split, step=512):
    half, width = h2_halves[0].shape
    got = pl.pallas_call(
        functools.partial(mlp_back_kernel, step, split),
        out_shape=[
            jax.ShapeDtypeStruct((half, width), F32),
            jax.ShapeDtypeStruct((half, width), BF),
            jax.ShapeDtypeStruct((1, width), F32),
        ]
        + gradient_shapes(2 * wg.shape[1] - split),
        in_specs=[smem()] + [vmem()] * 6,
        out_specs=[vmem()] * 11,
        compiler_params=params(12),
        name="mlp_back",
        cost_estimate=cost(14),
    )(place_xy, dgate, dup, wg, wu, *h2_halves)
    return (*got[:3], got[3:])


def touch_kernel(*refs):
    *sources, target = refs
    total = jnp.zeros(target.shape, F32)
    for source in sources:
        total = total + source[:16, :128].astype(F32)
    target[...] = total


def touch(*arrays):
    return pl.pallas_call(
        touch_kernel,
        out_shape=jax.ShapeDtypeStruct((16, 128), F32),
        in_specs=[vmem()] * len(arrays),
        out_specs=vmem(),
        compiler_params=params(12),
        name="touch",
        cost_estimate=cost(2),
    )(*arrays)


def pair_kernel(above, below, later, target):
    rows = above.shape[0]
    target[:rows] = above[...]
    target[rows:] = below[...]


def pair(above, below, later):
    rows, width = above.shape
    return pl.pallas_call(
        pair_kernel,
        out_shape=jax.ShapeDtypeStruct((2 * rows, width), above.dtype),
        in_specs=[vmem()] * 2 + [pl.BlockSpec(memory_space=pl.ANY)],
        out_specs=vmem(),
        compiler_params=params(4),
        name="pair",
        cost_estimate=cost(8),
    )(above, below, later)


def chip_kernel(high, got, *refs):
    total = high[...] + got[...].astype(F32)
    rows = total.shape[0] // 2
    chip, send = refs
    chip[...] = total[: chip.shape[0]]
    send[:rows] = total[rows:].astype(BF)
    if send.shape[0] > rows:
        send[rows:] = total[:rows].astype(BF)


def chip_sums(high, got, both=True):
    rows, width = high.shape[0] // 2, high.shape[1]
    count = 2 * rows if both else rows
    return pl.pallas_call(
        chip_kernel,
        out_shape=(jax.ShapeDtypeStruct((count, width), F32), jax.ShapeDtypeStruct((count, width), BF)),
        in_specs=[vmem()] * 2,
        out_specs=[vmem()] * 2,
        compiler_params=params(6),
        name="chip_sums",
        cost_estimate=cost(1),
    )(high, got)


def middle_kernel(own, across, chip, got, gain, mid_ref, h2_ref):
    mid = jnp.concatenate((own[...], across[...]), axis=0).astype(F32) + chip[...] + got[...].astype(F32)
    inverse = lax.rsqrt(jnp.mean(mid * mid, axis=-1, keepdims=True) + EPSILON)
    mid_ref[...] = mid
    h2_ref[...] = (mid * inverse * gain[...].astype(F32)).astype(BF)


def middle(own, across, chip, got, gain):
    return pl.pallas_call(
        middle_kernel,
        out_shape=(jax.ShapeDtypeStruct(chip.shape, F32), jax.ShapeDtypeStruct(chip.shape, BF)),
        in_specs=[vmem()] * 5,
        out_specs=[vmem()] * 2,
        compiler_params=params(8),
        name="middle",
        cost_estimate=cost(2),
    )(own, across, chip, got, gain)


def middle_back_kernel(mid_ref, cot, chip, got, gain, own, top, rest):
    mid = mid_ref[...]
    inverse = lax.rsqrt(jnp.mean(mid * mid, axis=-1, keepdims=True) + EPSILON)
    normed = mid * inverse
    scaled = (chip[...] + got[...].astype(F32)) * gain[...].astype(F32)
    grad = cot[...].astype(F32) + inverse * (scaled - normed * jnp.mean(scaled * normed, axis=-1, keepdims=True))
    own[...] = grad[: own.shape[0]]
    top[...] = grad[: top.shape[0]].astype(BF)
    rest[...] = grad[top.shape[0] :].astype(BF)


def middle_back(mid, cot, chip, got, gain, cut):
    half, width = mid.shape
    return pl.pallas_call(
        middle_back_kernel,
        out_shape=(
            jax.ShapeDtypeStruct((half // 2, width), F32),
            jax.ShapeDtypeStruct((cut, width), BF),
            jax.ShapeDtypeStruct((half - cut, width), BF),
        ),
        in_specs=[vmem()] * 5,
        out_specs=[vmem()] * 3,
        compiler_params=params(8),
        name="middle_back",
        cost_estimate=cost(2),
    )(mid, cot, chip, got, gain)


def output_kernel(step, hid, wd, high_ref, low_ref):
    half = high_ref.shape[0]
    for s in range(0, wd.shape[1], step):
        cut = slice(s, s + step)
        part = dot(hid[...], wd[:, cut])
        high_ref[:, cut] = part[:half].astype(BF)
        low_ref[:, cut] = part[half:].astype(BF)


def output(hid, wd, step=512):
    shape = jax.ShapeDtypeStruct((hid.shape[0] // 2, wd.shape[1]), BF)
    return pl.pallas_call(
        functools.partial(output_kernel, step),
        out_shape=[shape] * 2,
        in_specs=[vmem()] * 2,
        out_specs=[vmem()] * 2,
        compiler_params=params(8),
        name="output",
        cost_estimate=cost(4),
    )(hid, wd)


def combine_kernel(sums, *refs):
    out = refs[-1]
    at = 0
    for count, terms in sums:
        total = None
        for number, start in terms:
            term = refs[number][start : start + count].astype(F32)
            total = term if total is None else total + term
        out[at : at + count] = total.astype(out.dtype)
        at += count


def combine(sums, time=0.5):
    arrays, plan = [], []
    for terms in sums:
        listed = []
        for array, start, count in terms:
            known = [i for i, a in enumerate(arrays) if a is array]
            if not known:
                arrays.append(array)
            listed.append((known[0] if known else len(arrays) - 1, start))
        plan.append((terms[0][2], listed))
    total = sum(count for count, _ in plan)
    return pl.pallas_call(
        functools.partial(combine_kernel, plan),
        out_shape=jax.ShapeDtypeStruct((total, 32, 128), BF),
        in_specs=[vmem()] * len(arrays),
        out_specs=vmem(),
        compiler_params=params(8),
        name="combine",
        cost_estimate=cost(time),
    )(*arrays)


def ends_kernel(sums, extra, place_ref, *refs):
    give, keep = refs[-2:]
    at = 0
    if extra:
        total = None
        for number, start in extra:
            term = refs[number][start : start + 1].astype(F32)
            total = term if total is None else total + term
        give[0:1] = total.astype(BF)
        keep[0:1] = total.astype(BF).astype(F32)
        at = 1
    for parts in sums:
        count = parts[0][0]
        totals = []
        for _, terms in parts:
            total = None
            for number, start in terms:
                term = refs[number][start : start + count].astype(F32)
                total = term if total is None else total + term
            totals.append(total)
        for half in range(2):
            cut = slice(at, at + count)
            give[cut] = jnp.where(place_ref[2] == 0, totals[2 + half], totals[half]).astype(BF)
            keep[cut] = jnp.where(place_ref[2] == 0, totals[half], totals[2 + half])
            at += count


def ends(place, sums, extra=()):
    arrays, plan = [], []
    for parts in sums:
        planned = []
        for terms in parts:
            listed = []
            for array, start, count in terms:
                known = [i for i, a in enumerate(arrays) if a is array]
                if not known:
                    arrays.append(array)
                listed.append((known[0] if known else len(arrays) - 1, start))
            planned.append((terms[0][2], listed))
        plan.append(planned)
    arrays += [array for array, _, _ in extra]
    more = [(len(arrays) - len(extra) + i, start) for i, (_, start, _) in enumerate(extra)]
    total = sum(2 * parts[0][0] for parts in plan) + bool(extra)
    return pl.pallas_call(
        functools.partial(ends_kernel, plan, more),
        out_shape=(jax.ShapeDtypeStruct((total, 32, 128), BF), jax.ShapeDtypeStruct((total, 32, 128), F32)),
        in_specs=[smem()] + [vmem()] * len(arrays),
        out_specs=[vmem()] * 2,
        compiler_params=params(16),
        name="ends",
        cost_estimate=cost(1),
    )(place, *arrays)


def attention_back_kernel(
    docs, place_ref, place_xy, mid_a, mid_b, mid_c, mid_d, qkv, lse_ref, h1, o_ref, wq, wk, wv, wo, cos, sin, gain_two, *refs
):
    dqkv_ref, high_ref, low_ref, gains, *outs, bias_ref, do_ref = refs
    half = mid_a.shape[0] + mid_b.shape[0]
    rows, every = half // 2, 2 * half
    q_width = wq.shape[1]
    heads = q_width // HD
    width = wq.shape[0]
    scale = 1.0 / math.sqrt(HD)
    mid = jnp.concatenate((mid_a[...], mid_b[...], mid_c[...], mid_d[...]), axis=0)
    do_ref[...] = dot_rt(mid, wo[...]).astype(BF)
    ends = doc_ends(place_ref, docs)
    places_q, opening_q = places_of(place_ref[0], ends, rows, (1, every), 1)
    places_k, _ = places_of(place_ref[0], ends, rows, (every, 1), 0)
    bias_ref[...] = jnp.where((places_k <= places_q) & (places_k >= opening_q), 0.0, MASKED)
    keys = qkv[:, q_width : q_width + HD]
    vals = qkv[:, q_width + HD : q_width + 2 * HD]
    dk = jnp.zeros((every, HD), F32)
    dv = jnp.zeros((every, HD), F32)
    table_c, table_s = cos[...], sin[...]

    def unrope(values):
        wide_now = values.shape[1]
        return values * wide(table_c, wide_now) - swap_halves(values) * wide(table_s, wide_now)

    for pair in range(heads // 2):
        dqs = []
        for head in (2 * pair, 2 * pair + 1):
            cut = slice(head * HD, (head + 1) * HD)
            query = qkv[:, cut]
            grad_o = do_ref[:, cut]
            scores = dot_rt(keys, query) * scale + bias_ref[...]
            chances = jnp.exp(scores - lse_ref[head : head + 1, :])
            grad_chances = dot_rt(vals, grad_o)
            centre = jnp.sum(chances * grad_chances, axis=0, keepdims=True)
            grad_scores = (chances * (grad_chances - centre)).astype(BF)
            dv = dv + dot(chances.astype(BF), grad_o)
            dk = dk + dot(grad_scores, query)
            dqs.append(dot_t(grad_scores, keys))
        dq = jnp.concatenate(dqs, axis=1) * scale
        dqkv_ref[:, pair * 2 * HD : (pair + 1) * 2 * HD] = unrope(dq).astype(BF)
    both = jnp.concatenate((dk * scale, dv), axis=1)
    lane = lax.broadcasted_iota(jnp.int32, both.shape, 1)
    dqkv_ref[:, q_width:] = jnp.where(lane < HD, unrope(both), both).astype(BF)
    joined = jnp.concatenate((wk[...], wv[...]), axis=0)
    step = 512
    for s in range(0, width, step):
        part = dot_rt(dqkv_ref[:, :q_width], wq[s : s + step, :]) + dot(dqkv_ref[:, q_width:], joined[:, s : s + step])
        high_ref[:, s : s + step] = part[:half]
        low_ref[:, s : s + step] = part[half:].astype(BF)
        gain_one = jnp.sum(part * h1[:, s : s + step].astype(F32), axis=0, keepdims=True)
        for lane in range(0, step, 128):
            row = (s + lane) // 128
            gains[0, row : row + 1, :] = gain_one[:, lane : lane + 128]
            gains[0, width // 128 + row : width // 128 + row + 1, :] = gain_two[:, s + lane : s + lane + 128]
    gradient_body(place_xy, [((h1,), dqkv_ref, 0, q_width + 2 * HD), ((mid_a, mid_b, mid_c, mid_d), o_ref, 0, q_width)], outs)


def attention_back(place_docs, place_xy, mids, qkv, lse, h1, o, wq, wk, wv, wo, cos, sin, gain_two_part):
    half, width = mids[0].shape[0] + mids[1].shape[0], mids[0].shape[1]
    every = 2 * half
    q_width = wq.shape[1]
    got = pl.pallas_call(
        functools.partial(attention_back_kernel, place_docs.shape[0] - 1),
        out_shape=[
            jax.ShapeDtypeStruct((every, q_width + 2 * HD), BF),
            jax.ShapeDtypeStruct((half, width), F32),
            jax.ShapeDtypeStruct((half, width), BF),
            jax.ShapeDtypeStruct((1, width // 64, 128), F32),
        ]
        + gradient_shapes(2 * q_width + 2 * HD),
        in_specs=[smem()] * 2 + [vmem()] * 15,
        out_specs=[vmem()] * 12,
        scratch_shapes=[
            pltpu.VMEM((every, every), F32),
            pltpu.VMEM((every, q_width), BF),
        ],
        compiler_params=params(12),
        name="attention_back",
        cost_estimate=cost(19),
    )(place_docs, place_xy, *mids, qkv, lse, h1, o, wq, wk.T, wv.T, wo, cos, sin, gain_two_part)
    return (*got[1:4], got[4:])


def lay_out_kernel(plan, keep, got, *outs):
    for out, parts in zip(outs, plan):
        for start, blocks, first, width, to in parts:
            for half in range(2):
                for b in range(blocks):
                    low, high = max(128 * b, first), min(128 * (b + 1), first + width)
                    if low >= high:
                        continue
                    at = start + half * blocks + b
                    total = keep[at] + got[at].astype(F32)
                    out[32 * half : 32 * (half + 1), to + low - first : to + high - first] = total[:, low - 128 * b : high - 128 * b]


def lay_out(keep, got, plan):
    widths = [sum(part[3] for part in parts) for parts in plan]
    return pl.pallas_call(
        functools.partial(lay_out_kernel, plan),
        out_shape=[jax.ShapeDtypeStruct((64, width), F32) for width in widths],
        in_specs=[vmem()] * 2,
        out_specs=[vmem()] * len(plan),
        compiler_params=params(12),
        name="lay_out",
        cost_estimate=cost(1),
    )(keep, got)


def rotary_tables(offset):
    half_size = HD // 2
    freqs = THETA ** (-(jnp.arange(half_size, dtype=F32) * 2.0 / HD))
    angles = offset.astype(F32)[:, None] * freqs[None, :]
    cosine, sine = jnp.cos(angles), jnp.sin(angles)
    return jnp.concatenate((cosine,) * 4, axis=1), jnp.concatenate((-sine, sine) * 2, axis=1)


def over_core(values):
    return lax.ppermute(values, "tensor", [(t, t ^ 1) for t in range(4)])


def over_z(values):
    return lax.ppermute(values, "tensor", [(t, t ^ 2) for t in range(4)])


def over_diagonal(values):
    return lax.ppermute(values, "tensor", [(t, t ^ 3) for t in range(4)])


def over_x(values, xor):
    return lax.ppermute(values, "dp", [(d, d ^ (xor * 8)) for d in range(32)])


def over_y(values, xor):
    return lax.ppermute(values, "dp", [(d, d ^ (xor * 2)) for d in range(32)])


def over_z_hi(values):
    return lax.ppermute(values, "dp", [(d, d ^ 1) for d in range(32)])


def after(value, *others):
    return lax.optimization_barrier((value, *others))[0] if others else value


def add(*terms):
    total = terms[0].astype(F32)
    for term in terms[1:]:
        total = total + term.astype(F32)
    return total


def norm(values):
    inverse = lax.rsqrt(jnp.mean(values * values, axis=-1, keepdims=True) + EPSILON)
    return values * inverse, inverse


def norm_back(normed, inverse, gain, grads):
    scaled = grads * gain
    return inverse * (scaled - normed * jnp.mean(scaled * normed, axis=-1, keepdims=True))


LINKS = ((over_x, 1), (over_x, 3), (over_y, 1), (over_y, 3))
ROUTES = ((0, 1, 2, 3), (1, 0, 3, 2), (2, 3, 0, 1), (3, 2, 1, 0))


class Reduction:
    def __init__(self, arrays, joined=False):
        self.joined = joined
        self.blocks = arrays[0].shape[2]
        self.sends = [arrays[2 * part].reshape(-1, 32, 128) for part in range(4)]
        self.kept = [[(arrays[2 * part + 1].reshape(-1, 32, 128), self.starts(0, 8))] for part in range(4)]
        self.near, self.far, self.last = {}, {}, {}

    def starts(self, at, rows):
        return {row: at + row * self.blocks for row in range(rows)}

    def route(self, part, step):
        return ROUTES[part - part % 2 if self.joined and step >= 2 else part][step]

    def order(self, part):
        return ((1, 3), (3, 1))[0 if self.joined else part % 2]

    def row(self, part, row, rows=1):
        return [(array, starts[row], rows * self.blocks) for array, starts in self.kept[part]]

    def sum(self, part, step):
        first, second = self.order(part)
        if step == 0:
            return [(self.sends[part], 0, 8 * self.blocks)]
        if step == 1:
            return self.row(part, 4, 4)
        if step == 2:
            return self.row(part, min(first, 2), 2)
        if step == 3:
            return self.row(part, second) + [self.far[part]]
        return self.row(part, 0) + self.near.get(part, []) + [self.last[part]]

    def take(self, part, step, got, at):
        n = self.blocks
        if step < 2:
            self.kept[part].append((got, self.starts(at, 8 - 4 * step)))
        elif step == 2:
            near, far = (0, 1) if self.order(part)[0] == 1 else (1, 0)
            self.near[part] = [(got, at + near * n, n)]
            self.far[part] = (got, at + far * n, n)
        else:
            self.last[part] = (got, at, n)


def fold(jobs, time=0.5):
    folded = []
    for part in range(4):
        sums, places = [], []
        at = 0
        for r, rows in jobs:
            rows = {"last": (0, r.order(part)[1]), "own": (0,)}.get(rows, rows)
            starts = {}
            for row in rows:
                terms = r.row(part, row)
                if row == 0:
                    terms = terms + r.near.get(part, [])
                sums.append(terms)
                starts[row] = at
                at += r.blocks
            r.near.pop(part, None)
            places.append((r, starts))
        array = combine(sums, time)
        folded.append(array)
        for r, starts in places:
            r.kept[part] = [(array, starts)]
    return folded


class Gains:
    def __init__(self, block):
        self.held = [(block, 0)]

    def terms(self):
        return [(array, start, 1) for array, start in self.held]

    def exchange(self, hop, before):
        sent = sum(array[start : start + 1].astype(F32) for array, start in self.held).astype(BF)
        self.held = [(sent, 0), (hop(after(sent, *before)), 0)]


def takers(jobs, link):
    return [(r, part, step) for r, step in jobs for part in range(4) if r.route(part, step) == link]


def prepare(jobs, gains=None, gains_link=None):
    operands = []
    for link in range(4):
        taken = takers(jobs, link)
        if not taken:
            operands.append(None)
            continue
        if len(taken) == 1 and taken[0][2] == 0:
            operands.append(taken[0][0].sends[taken[0][1]])
            continue
        sums = [r.sum(part, step) for r, part, step in taken]
        operands.append(combine(sums + ([gains.terms()] if link == gains_link else [])))
    return operands


def send(jobs, operands, before=None, anchor=(), gains=None, gains_link=None):
    arrived = []
    for link, (operand, (hop, xor)) in enumerate(zip(operands, LINKS)):
        if operand is None:
            arrived.append(before[link])
            continue
        got = hop(after(operand, *before[link]) if before else operand, xor)
        arrived.append((got,))
        got = after(got, *anchor)
        at = 0
        for r, part, step in takers(jobs, link):
            r.take(part, step, got, at)
            at += r.blocks * (8, 4, 2, 1)[step]
        if link == gains_link:
            gains.held = [(operand, at), (got, at)]
    return arrived


def stage(jobs, before=None, **more):
    return send(jobs, prepare(jobs, **more), before, **more)


def finish(reductions, place, plan, before=(), gains=None, anchor=None):
    keep, give = None, None
    give, keep = ends(
        place,
        [[r.sum(part, 4) for part in range(4)] for r in reductions],
        gains.terms() if gains else (),
    )
    got = over_z_hi(after(give, *before))
    if anchor is not None:
        got = after(got, anchor)
    outs = lay_out(keep, got, plan)
    if gains:
        total = add(keep[0], got[0])
        outs = (*outs, (total + over_core(total)) + (over_z(total) + over_diagonal(total)))
    return outs


def per_device(
    tokens,
    attn_gain,
    query_weight,
    key_weight,
    value_weight,
    out_weight,
    mlp_gain,
    gate_weight,
    up_weight,
    down_weight,
    cotangent,
    doc_lengths,
):
    rows = tokens.shape[0]
    place_dp = lax.axis_index("dp")
    place_t = lax.axis_index("tensor")
    place_xy = jnp.stack((place_dp // 8, (place_dp // 2) % 4, place_dp % 2))
    q_width = query_weight.shape[1]
    gain_one, gain_two = attn_gain.astype(F32), mlp_gain.astype(F32)

    across = over_z(tokens)
    places = jnp.concatenate(
        [(place_t ^ j) * rows + jnp.arange(rows, dtype=jnp.int32) for j in (0, 2, 1, 3)]
    )
    opening, ending = jnp.zeros_like(places), jnp.int32(0)
    for number in range(doc_lengths.shape[0]):
        ending = ending + doc_lengths[number]
        opening = jnp.maximum(opening, jnp.where(places >= ending, ending, 0))
    cos, sin = rotary_tables(places - opening)
    place_docs = jnp.concatenate((place_t[None], doc_lengths))
    attn_row, mlp_row = attn_gain.reshape(1, -1), mlp_gain.reshape(1, -1)
    near = touch(query_weight, out_weight)
    across, cos, sin, place_docs, place_xy, attn_row, mlp_row, near = lax.optimization_barrier(
        (across, cos, sin, place_docs, place_xy, attn_row, mlp_row, near)
    )
    token_blocks = (tokens, across, over_core(tokens), over_core(across))

    cot_across = over_z(after(cotangent, across))
    h1, qkv, heads_out, lse, high, low = attention(
        place_docs, token_blocks, attn_row, query_weight, key_weight, value_weight, out_weight, cos, sin, near
    )
    cot_pair = pair(cotangent, cot_across, low)
    chip, low = chip_sums(high, after(over_core(low), cot_pair))
    z_sums = over_z(low)
    cot_halves = (cot_pair, over_core(after(cot_pair, chip)))
    near = touch(after(gate_weight, cot_halves[1]), up_weight, down_weight)
    mid, h2 = middle(tokens, across, chip, after(z_sums, near), mlp_row)
    h2 = (h2, over_core(h2))
    units = gate_weight.shape[1]
    split = units // 2 // 128 * 128 + 128
    hidden, grad_gate_val, grad_up_val, first = mlp(
        place_xy, h2, gate_weight, up_weight, down_weight, cot_halves, near, split
    )
    first_sum = Reduction(first)
    first_links = stage([(first_sum, 0)])
    high, low, gain_two_part, second = mlp_back(
        place_xy, after(grad_gate_val, first[0]), grad_up_val, gate_weight, up_weight, h2, split
    )
    chip, low = chip_sums(high, after(over_core(low), *[link[0] for link in first_links]))
    second_sum = Reduction(second)
    links = stage([(second_sum, 0)], first_links)
    z_sums = after(over_z(low), *fold([(first_sum, range(8))]))
    grad_own, *mid_low = middle_back(mid, cot_pair, chip, z_sums, mlp_row, rows + rows // 2)
    mid_low = (*mid_low, over_core(mid_low[0]), over_core(mid_low[1]))

    jobs = [(first_sum, 1), (second_sum, 1)]
    operands = prepare(jobs)
    high, low, gains, attn = attention_back(
        place_docs, place_xy, mid_low, after(qkv, *operands), lse, h1, heads_out,
        query_weight, key_weight, value_weight, out_weight, cos, sin, gain_two_part,
    )
    links = send(jobs, operands, links, (low,))
    attn_sum = Reduction(attn, joined=True)
    gains = Gains(gains)
    own, other = chip_sums(high, after(over_core(low), *[link[0] for link in links]), False)
    jobs = [(first_sum, 2), (second_sum, 2), (attn_sum, 0)]
    operands = prepare(jobs, gains, 0)
    folded = fold([(first_sum, "last"), (second_sum, "last")])
    other = over_z(other)
    out_high, out_low = output(after(hidden, other), down_weight)
    links = send(jobs, operands, links, (*folded, out_low), gains, 0)
    grad_h1 = own + other.astype(F32)
    result_got = over_core(after(out_low, grad_h1))
    result_chip = add(out_high, result_got)
    result_z = over_z(result_chip[rows:].astype(BF))
    result = (mid[:rows] + result_chip[:rows] + result_z.astype(F32)).astype(BF)
    jobs = [(first_sum, 3), (second_sum, 3), (attn_sum, 1)]
    operands = prepare(jobs, gains, 1)
    folded = fold([(first_sum, "own"), (second_sum, "own"), (attn_sum, range(4))])
    links = send(jobs, operands, links, folded, gains, 1)
    blocks, more = first_sum.blocks, second_sum.blocks
    plan = [
        [(0, blocks, 0, units, 0)],
        [(0, blocks, units, split, 0), (2 * blocks, more, 0, units - split, split)],
        [(2 * blocks, more, units - split, units, 0)],
    ]
    out_down, out_gate, out_up = finish([first_sum, second_sum], place_xy, plan)
    links = stage([(attn_sum, 2)], links, gains=gains, gains_link=2)
    links = [(*link, result_z) for link in links]
    links = stage([(attn_sum, 3)], links, gains=gains, gains_link=3)
    cuts = ((0, q_width), (q_width, HD), (q_width + HD, HD), (q_width + 2 * HD, q_width))
    plan = [[(1, attn_sum.blocks, first, width, 0)] for first, width in cuts]
    out_query, out_key, out_value, out_out, grad_gains = finish([attn_sum], place_xy, plan, [], gains, out_up)
    grad_gains = grad_gains.reshape(2, -1)

    normed, inverse = norm(tokens.astype(F32))
    grad_tokens = grad_own + norm_back(normed, inverse, gain_one, grad_h1)
    return (
        result,
        grad_tokens.astype(BF),
        grad_gains[0] / gain_one,
        out_query,
        out_key,
        out_value,
        out_out.T,
        grad_gains[1] / gain_two,
        out_gate,
        out_up,
        out_down.T,
    )


def solution(mesh):
    in_specs = (
        P(("dp", "tensor"), None),
        P(),
        P(None, "tensor"),
        P(None, "tensor"),
        P(None, "tensor"),
        P("tensor", None),
        P(),
        P(None, "tensor"),
        P(None, "tensor"),
        P("tensor", None),
        P(("dp", "tensor"), None),
        P("dp"),
    )
    out_specs = (
        P(("dp", "tensor"), None),
        P(("dp", "tensor"), None),
        P(),
        P("dp", "tensor"),
        P("dp", "tensor"),
        P("dp", "tensor"),
        P("tensor", "dp"),
        P(),
        P("dp", "tensor"),
        P("dp", "tensor"),
        P("tensor", "dp"),
    )
    return jax.shard_map(
        per_device, mesh=mesh, in_specs=in_specs, out_specs=out_specs, check_vma=False
    )
```

```python
import functools
import math

import jax
import jax.numpy as jnp
from jax import lax
from jax.experimental import pallas as pl
from jax.experimental.pallas import tpu as pltpu
from jax.sharding import PartitionSpec as P

HD = 64
EPSILON = 1e-05
THETA = 10000.0
MASKED = -1000000000.0
BF = jnp.bfloat16
F32 = jnp.float32
MIB = 1024 * 1024


def cost(time):
    return pl.CostEstimate(flops=int(time * 1e9), bytes_accessed=1024, transcendentals=0)


def dot(left, right):
    return jnp.dot(left, right, preferred_element_type=F32)


def dot_t(left, right):
    return lax.dot_general(left, right, (((0,), (0,)), ((), ())), preferred_element_type=F32)


def dot_rt(left, right):
    return lax.dot_general(left, right, (((1,), (1,)), ((), ())), preferred_element_type=F32)


def vmem():
    return pl.BlockSpec(memory_space=pltpu.VMEM)


def smem():
    return pl.BlockSpec(memory_space=pltpu.SMEM)


def hbm():
    return pl.BlockSpec(memory_space=pl.ANY)


def params(size):
    return pltpu.CompilerParams(vmem_limit_bytes=size * MIB)


def swap_halves(values):
    width = values.shape[1]
    lane = lax.broadcasted_iota(jnp.int32, values.shape, 1)
    return jnp.where(
        lane % HD < HD // 2,
        pltpu.roll(values, width - HD // 2, 1),
        pltpu.roll(values, HD // 2, 1),
    )


def wide(table, width):
    return jnp.concatenate([table] * (width // table.shape[1]), axis=1) if width > table.shape[1] else table[:, :width]


def places_of(place_t, ends, rows, shape, axis):
    index = lax.broadcasted_iota(jnp.int32, shape, axis)
    block = index // rows
    order = jnp.where(block == 0, 0, jnp.where(block == 1, 2, jnp.where(block == 2, 1, 3)))
    places = (place_t ^ order) * rows + index % rows
    opening = jnp.zeros(shape, jnp.int32)
    for end in ends:
        opening = jnp.maximum(opening, jnp.where(places >= end, end, 0))
    return places, opening


def doc_ends(place_ref, count):
    ends, total = [], jnp.int32(0)
    for i in range(count):
        total = total + place_ref[1 + i]
        ends.append(total)
    return ends


def attention_kernel(
    docs, place_ref, own, zpart, cpart, diag, gain, wq, wk, wv, wo, cos, sin, near,
    h1_ref, qkv_ref, o_ref, lse_ref, high_ref, low_ref, bias_ref,
):
    rows = own.shape[0]
    every = 4 * rows
    half = 2 * rows
    q_width = wq.shape[1]
    heads = q_width // HD
    gain_row = gain[...].astype(F32)
    for number, block in enumerate((own, zpart, cpart, diag)):
        values = block[...].astype(F32)
        inverse = lax.rsqrt(jnp.mean(values * values, axis=-1, keepdims=True) + EPSILON)
        h1_ref[number * rows : (number + 1) * rows, :] = (values * inverse * gain_row).astype(BF)
    h1 = h1_ref[...]
    joined = jnp.concatenate((wk[...], wv[...]), axis=0)
    table_c, table_s = cos[...], sin[...]

    def rope(values):
        width = values.shape[1]
        return values * wide(table_c, width) + swap_halves(values) * wide(table_s, width)

    scale = 1.0 / math.sqrt(HD)
    kv = dot_rt(h1, joined)
    lane = lax.broadcasted_iota(jnp.int32, kv.shape, 1)
    qkv_ref[:, q_width:] = jnp.where(lane < HD, rope(kv), kv).astype(BF)
    qkv_ref[:, :q_width] = rope(dot(h1, wq[...])).astype(BF)

    ends = doc_ends(place_ref, docs)
    places_q, opening_q = places_of(place_ref[0], ends, rows, (every, 1), 0)
    places_k, _ = places_of(place_ref[0], ends, rows, (1, every), 1)
    bias_ref[...] = jnp.where((places_k <= places_q) & (places_k >= opening_q), 0.0, MASKED)

    keys = qkv_ref[:, q_width : q_width + HD]
    kv_low = qkv_ref[:, q_width:]
    lane = lax.broadcasted_iota(jnp.int32, kv_low.shape, 1)
    ones_vals = jnp.where(lane < HD, jnp.ones_like(kv_low), kv_low)
    lse_lane = lax.broadcasted_iota(jnp.int32, (every, 128), 1)
    lse = jnp.zeros((every, 128), F32)
    for head in range(heads):
        query = qkv_ref[:, head * HD : (head + 1) * HD]
        scores = dot_rt(query, keys) * scale + bias_ref[...]
        highest = jnp.max(scores, axis=-1, keepdims=True)
        raised = jnp.exp(scores - highest)
        mixed = dot(raised.astype(BF), ones_vals)
        totals = mixed[:, :1]
        o_ref[:, head * HD : (head + 1) * HD] = (mixed[:, HD:] / totals).astype(BF)
        lse = jnp.where(lse_lane == head, highest + jnp.log(totals), lse)
    lse_ref[...] = lse.T[:heads, :]
    high_ref[...] = dot(o_ref[:half, :], wo[...])
    low_ref[...] = dot(o_ref[half:, :], wo[...]).astype(BF)


def attention(place_docs, blocks, gain, wq, wk, wv, wo, cos, sin, near):
    rows, width = blocks[0].shape
    every = rows * 4
    q_width = wq.shape[1]
    heads = q_width // HD
    shapes = (
        jax.ShapeDtypeStruct((every, width), BF),
        jax.ShapeDtypeStruct((every, q_width + 2 * HD), BF),
        jax.ShapeDtypeStruct((every, q_width), BF),
        jax.ShapeDtypeStruct((heads, every), F32),
        jax.ShapeDtypeStruct((2 * rows, width), F32),
        jax.ShapeDtypeStruct((2 * rows, width), BF),
    )
    return pl.pallas_call(
        functools.partial(attention_kernel, place_docs.shape[0] - 1),
        out_shape=shapes,
        in_specs=[smem()] + [vmem()] * 12,
        out_specs=[vmem()] * 6,
        scratch_shapes=[pltpu.VMEM((every, every), F32)],
        compiler_params=params(7),
        name="attention",
        cost_estimate=cost(11),
    )(place_docs, *blocks, gain, wq, wk.T, wv.T, wo, cos, sin, near)


SEND = ((1, 2), (3, 2))
KEEP = ((0, 3), (0, 1))


def gradient_body(place_ref, groups, outs, tile=512):
    place_x, place_y = place_ref[0], place_ref[1]
    at = 0
    for lefts, right, begin, width in groups:
        for jx in range(4):
            columns = []
            for jy in range(4):
                start = pl.multiple_of(((place_x ^ jx) * 4 + (place_y ^ jy)) * 128, 128)
                columns.append(jnp.concatenate([left[:, pl.ds(start, 128)] for left in lefts], axis=0))
            left = jnp.concatenate(columns, axis=1)
            for s in range(0, width, tile):
                n = min(tile, width - s)
                cube = dot_t(left, right[:, begin + s : begin + s + n]).astype(BF).reshape(4, 4, 32, n)
                for b in range(n // 128):
                    block = at + s // 128 + b
                    piece = cube[:, :, :, b * 128 : (b + 1) * 128]
                    for part in range(2):
                        for number, slots in enumerate((SEND[part], KEEP[part])):
                            if jx in slots:
                                outs[2 * part + number][slots.index(jx), :, block] = piece[:, part]
                            for slot in range(2):
                                outs[4 + 2 * part + number][slot, jx, block] = piece[slots[slot], 2 + part]
        at += width // 128


def gradient_shapes(width):
    return [jax.ShapeDtypeStruct((2, 4, width // 128, 32, 128), BF)] * 8


def mlp_kernel(tile, split, place_ref, h2_a, h2_b, wg, wu, wd, cot_a, cot_b, near, hid_ref, dgate_ref, dup_ref, *outs):
    units = wg.shape[1]
    h2 = jnp.concatenate((h2_a[...], h2_b[...]), axis=0)
    cot = jnp.concatenate((cot_a[...], cot_b[...]), axis=0)
    for s in range(0, units, tile):
        cut = slice(s, min(s + tile, units))
        gate = dot(h2, wg[:, cut])
        up = dot(h2, wu[:, cut])
        dh = dot_rt(cot, wd[cut, :])
        sig = jax.nn.sigmoid(gate)
        active = gate * sig
        hid_ref[:, cut] = (active * up).astype(BF)
        dgate_ref[:, cut] = (dh * up * (sig + active * (1.0 - sig))).astype(BF)
        dup_ref[:, cut] = (dh * active).astype(BF)
    gradient_body(place_ref, [((cot_a, cot_b), hid_ref, 0, units), ((h2_a, h2_b), dgate_ref, 0, split)], outs)


def mlp(place_xy, h2_halves, wg, wu, wd, cot_halves, near, split, tile=512):
    half, width = h2_halves[0].shape
    every = 2 * half
    units = wg.shape[1]
    got = pl.pallas_call(
        functools.partial(mlp_kernel, tile, split),
        out_shape=[jax.ShapeDtypeStruct((every, units), BF)] * 3 + gradient_shapes(units + split),
        in_specs=[smem()] + [vmem()] * 8,
        out_specs=[vmem()] * 11,
        compiler_params=params(13),
        name="mlp",
        cost_estimate=cost(18),
    )(place_xy, *h2_halves, wg, wu, wd, *cot_halves, near)
    return (*got[:3], got[3:])


def mlp_back_kernel(step, split, place_ref, dgate, dup, wg, wu, h2_a, h2_b, high_ref, low_ref, gain_ref, *outs):
    half, width = h2_a.shape
    for s in range(0, width, step):
        cut = slice(s, s + step)
        part = dot_rt(dgate[...], wg[cut, :]) + dot_rt(dup[...], wu[cut, :])
        high_ref[:, cut] = part[:half]
        low_ref[:, cut] = part[half:].astype(BF)
        gain_ref[:, cut] = jnp.sum(part[:half] * h2_a[:, cut].astype(F32), axis=0, keepdims=True) + jnp.sum(
            part[half:] * h2_b[:, cut].astype(F32), axis=0, keepdims=True
        )
    units = dup.shape[1]
    lefts = (h2_a, h2_b)
    gradient_body(place_ref, [(lefts, dgate, split, units - split), (lefts, dup, 0, units)], outs)


def mlp_back(place_xy, dgate, dup, wg, wu, h2_halves, split, step=512):
    half, width = h2_halves[0].shape
    got = pl.pallas_call(
        functools.partial(mlp_back_kernel, step, split),
        out_shape=[
            jax.ShapeDtypeStruct((half, width), F32),
            jax.ShapeDtypeStruct((half, width), BF),
            jax.ShapeDtypeStruct((1, width), F32),
        ]
        + gradient_shapes(2 * wg.shape[1] - split),
        in_specs=[smem()] + [vmem()] * 6,
        out_specs=[vmem()] * 11,
        compiler_params=params(6),
        name="mlp_back",
        cost_estimate=cost(14),
    )(place_xy, dgate, dup, wg, wu, *h2_halves)
    return (*got[:3], got[3:])


def touch_kernel(*refs):
    *sources, target = refs
    total = jnp.zeros(target.shape, F32)
    for source in sources:
        total = total + source[:16, :128].astype(F32)
    target[...] = total


def touch(*arrays):
    return pl.pallas_call(
        touch_kernel,
        out_shape=jax.ShapeDtypeStruct((16, 128), F32),
        in_specs=[vmem()] * len(arrays),
        out_specs=vmem(),
        compiler_params=params(12),
        name="touch",
        cost_estimate=cost(2),
    )(*arrays)


def pair_kernel(above, below, later, target):
    rows = above.shape[0]
    target[:rows] = above[...]
    target[rows:] = below[...]


def pair(above, below, later):
    rows, width = above.shape
    return pl.pallas_call(
        pair_kernel,
        out_shape=jax.ShapeDtypeStruct((2 * rows, width), above.dtype),
        in_specs=[vmem()] * 2 + [pl.BlockSpec(memory_space=pl.ANY)],
        out_specs=vmem(),
        compiler_params=params(4),
        name="pair",
        cost_estimate=cost(8),
    )(above, below, later)


def chip_kernel(high, got, *refs):
    total = high[...] + got[...].astype(F32)
    rows = total.shape[0] // 2
    chip, send = refs
    chip[...] = total[: chip.shape[0]]
    send[:rows] = total[rows:].astype(BF)
    if send.shape[0] > rows:
        send[rows:] = total[:rows].astype(BF)


def chip_sums(high, got, both=True):
    rows, width = high.shape[0] // 2, high.shape[1]
    count = 2 * rows if both else rows
    return pl.pallas_call(
        chip_kernel,
        out_shape=(jax.ShapeDtypeStruct((count, width), F32), jax.ShapeDtypeStruct((count, width), BF)),
        in_specs=[vmem()] * 2,
        out_specs=[vmem()] * 2,
        compiler_params=params(6),
        name="chip_sums",
        cost_estimate=cost(1),
    )(high, got)


def middle_kernel(own, across, chip, got, gain, mid_ref, h2_ref):
    mid = jnp.concatenate((own[...], across[...]), axis=0).astype(F32) + chip[...] + got[...].astype(F32)
    inverse = lax.rsqrt(jnp.mean(mid * mid, axis=-1, keepdims=True) + EPSILON)
    mid_ref[...] = mid
    h2_ref[...] = (mid * inverse * gain[...].astype(F32)).astype(BF)


def middle(own, across, chip, got, gain):
    return pl.pallas_call(
        middle_kernel,
        out_shape=(jax.ShapeDtypeStruct(chip.shape, F32), jax.ShapeDtypeStruct(chip.shape, BF)),
        in_specs=[vmem()] * 5,
        out_specs=[vmem()] * 2,
        compiler_params=params(8),
        name="middle",
        cost_estimate=cost(2),
    )(own, across, chip, got, gain)


def middle_back_kernel(mid_ref, cot, chip, got, gain, own, top, rest):
    mid = mid_ref[...]
    inverse = lax.rsqrt(jnp.mean(mid * mid, axis=-1, keepdims=True) + EPSILON)
    normed = mid * inverse
    scaled = (chip[...] + got[...].astype(F32)) * gain[...].astype(F32)
    grad = cot[...].astype(F32) + inverse * (scaled - normed * jnp.mean(scaled * normed, axis=-1, keepdims=True))
    own[...] = grad[: own.shape[0]]
    top[...] = grad[: top.shape[0]].astype(BF)
    rest[...] = grad[top.shape[0] :].astype(BF)


def middle_back(mid, cot, chip, got, gain, cut):
    half, width = mid.shape
    return pl.pallas_call(
        middle_back_kernel,
        out_shape=(
            jax.ShapeDtypeStruct((half // 2, width), F32),
            jax.ShapeDtypeStruct((cut, width), BF),
            jax.ShapeDtypeStruct((half - cut, width), BF),
        ),
        in_specs=[vmem()] * 5,
        out_specs=[vmem()] * 3,
        compiler_params=params(8),
        name="middle_back",
        cost_estimate=cost(2),
    )(mid, cot, chip, got, gain)


def output_kernel(step, hid, wd, high_ref, low_ref):
    half = high_ref.shape[0]
    for s in range(0, wd.shape[1], step):
        cut = slice(s, s + step)
        part = dot(hid[...], wd[:, cut])
        high_ref[:, cut] = part[:half].astype(BF)
        low_ref[:, cut] = part[half:].astype(BF)


def output(hid, wd, step=512):
    shape = jax.ShapeDtypeStruct((hid.shape[0] // 2, wd.shape[1]), BF)
    return pl.pallas_call(
        functools.partial(output_kernel, step),
        out_shape=[shape] * 2,
        in_specs=[vmem()] * 2,
        out_specs=[vmem()] * 2,
        compiler_params=params(8),
        name="output",
        cost_estimate=cost(4),
    )(hid, wd)


def combine_kernel(sums, *refs):
    out = refs[-1]
    at = 0
    for count, terms in sums:
        total = None
        for number, start in terms:
            term = refs[number][start : start + count].astype(F32)
            total = term if total is None else total + term
        out[at : at + count] = total.astype(out.dtype)
        at += count


def combine(sums, time=0.5):
    arrays, plan = [], []
    for terms in sums:
        listed = []
        for array, start, count in terms:
            known = [i for i, a in enumerate(arrays) if a is array]
            if not known:
                arrays.append(array)
            listed.append((known[0] if known else len(arrays) - 1, start))
        plan.append((terms[0][2], listed))
    total = sum(count for count, _ in plan)
    return pl.pallas_call(
        functools.partial(combine_kernel, plan),
        out_shape=jax.ShapeDtypeStruct((total, 32, 128), BF),
        in_specs=[vmem()] * len(arrays),
        out_specs=vmem(),
        compiler_params=params(8),
        name="combine",
        cost_estimate=cost(time),
    )(*arrays)


def ends_kernel(sums, extra, place_ref, *refs):
    give, keep = refs[-2:]
    at = 0
    if extra:
        total = None
        for number, start in extra:
            term = refs[number][start : start + 1].astype(F32)
            total = term if total is None else total + term
        give[0:1] = total.astype(BF)
        keep[0:1] = total.astype(BF).astype(F32)
        at = 1
    for parts in sums:
        count = parts[0][0]
        totals = []
        for _, terms in parts:
            total = None
            for number, start in terms:
                term = refs[number][start : start + count].astype(F32)
                total = term if total is None else total + term
            totals.append(total)
        for half in range(2):
            cut = slice(at, at + count)
            give[cut] = jnp.where(place_ref[2] == 0, totals[2 + half], totals[half]).astype(BF)
            keep[cut] = jnp.where(place_ref[2] == 0, totals[half], totals[2 + half])
            at += count


def ends(place, sums, extra=()):
    arrays, plan = [], []
    for parts in sums:
        planned = []
        for terms in parts:
            listed = []
            for array, start, count in terms:
                known = [i for i, a in enumerate(arrays) if a is array]
                if not known:
                    arrays.append(array)
                listed.append((known[0] if known else len(arrays) - 1, start))
            planned.append((terms[0][2], listed))
        plan.append(planned)
    arrays += [array for array, _, _ in extra]
    more = [(len(arrays) - len(extra) + i, start) for i, (_, start, _) in enumerate(extra)]
    total = sum(2 * parts[0][0] for parts in plan) + bool(extra)
    return pl.pallas_call(
        functools.partial(ends_kernel, plan, more),
        out_shape=(jax.ShapeDtypeStruct((total, 32, 128), BF), jax.ShapeDtypeStruct((total, 32, 128), F32)),
        in_specs=[smem()] + [vmem()] * len(arrays),
        out_specs=[vmem()] * 2,
        compiler_params=params(16),
        name="ends",
        cost_estimate=cost(1),
    )(place, *arrays)


def attention_back_kernel(
    docs, place_ref, place_xy, mid_a, mid_b, mid_c, mid_d, qkv, lse_ref, h1, o_ref, wq, wk, wv, wo, cos, sin, gain_two, *refs
):
    dqkv_ref, high_ref, low_ref, gains, *outs, bias_ref, do_ref = refs
    half = mid_a.shape[0] + mid_b.shape[0]
    rows, every = half // 2, 2 * half
    q_width = wq.shape[1]
    heads = q_width // HD
    width = wq.shape[0]
    scale = 1.0 / math.sqrt(HD)
    mid = jnp.concatenate((mid_a[...], mid_b[...], mid_c[...], mid_d[...]), axis=0)
    do_ref[...] = dot_rt(mid, wo[...]).astype(BF)
    ends = doc_ends(place_ref, docs)
    places_q, opening_q = places_of(place_ref[0], ends, rows, (1, every), 1)
    places_k, _ = places_of(place_ref[0], ends, rows, (every, 1), 0)
    bias_ref[...] = jnp.where((places_k <= places_q) & (places_k >= opening_q), 0.0, MASKED)
    keys = qkv[:, q_width : q_width + HD]
    vals = qkv[:, q_width + HD : q_width + 2 * HD]
    dk = jnp.zeros((every, HD), F32)
    dv = jnp.zeros((every, HD), F32)
    table_c, table_s = cos[...], sin[...]

    def unrope(values):
        wide_now = values.shape[1]
        return values * wide(table_c, wide_now) - swap_halves(values) * wide(table_s, wide_now)

    for pair in range(heads // 2):
        dqs = []
        for head in (2 * pair, 2 * pair + 1):
            cut = slice(head * HD, (head + 1) * HD)
            query = qkv[:, cut]
            grad_o = do_ref[:, cut]
            scores = dot_rt(keys, query) * scale + bias_ref[...]
            chances = jnp.exp(scores - lse_ref[head : head + 1, :])
            grad_chances = dot_rt(vals, grad_o)
            centre = jnp.sum(chances * grad_chances, axis=0, keepdims=True)
            grad_scores = (chances * (grad_chances - centre)).astype(BF)
            dv = dv + dot(chances.astype(BF), grad_o)
            dk = dk + dot(grad_scores, query)
            dqs.append(dot_t(grad_scores, keys))
        dq = jnp.concatenate(dqs, axis=1) * scale
        dqkv_ref[:, pair * 2 * HD : (pair + 1) * 2 * HD] = unrope(dq).astype(BF)
    both = jnp.concatenate((dk * scale, dv), axis=1)
    lane = lax.broadcasted_iota(jnp.int32, both.shape, 1)
    dqkv_ref[:, q_width:] = jnp.where(lane < HD, unrope(both), both).astype(BF)
    joined = jnp.concatenate((wk[...], wv[...]), axis=0)
    step = 512
    for s in range(0, width, step):
        part = dot_rt(dqkv_ref[:, :q_width], wq[s : s + step, :]) + dot(dqkv_ref[:, q_width:], joined[:, s : s + step])
        high_ref[:, s : s + step] = part[:half]
        low_ref[:, s : s + step] = part[half:].astype(BF)
        gain_one = jnp.sum(part * h1[:, s : s + step].astype(F32), axis=0, keepdims=True)
        for lane in range(0, step, 128):
            row = (s + lane) // 128
            gains[0, row : row + 1, :] = gain_one[:, lane : lane + 128]
            gains[0, width // 128 + row : width // 128 + row + 1, :] = gain_two[:, s + lane : s + lane + 128]
    gradient_body(place_xy, [((h1,), dqkv_ref, 0, q_width + 2 * HD), ((mid_a, mid_b, mid_c, mid_d), o_ref, 0, q_width)], outs)


def attention_back(place_docs, place_xy, mids, qkv, lse, h1, o, wq, wk, wv, wo, cos, sin, gain_two_part):
    half, width = mids[0].shape[0] + mids[1].shape[0], mids[0].shape[1]
    every = 2 * half
    q_width = wq.shape[1]
    got = pl.pallas_call(
        functools.partial(attention_back_kernel, place_docs.shape[0] - 1),
        out_shape=[
            jax.ShapeDtypeStruct((every, q_width + 2 * HD), BF),
            jax.ShapeDtypeStruct((half, width), F32),
            jax.ShapeDtypeStruct((half, width), BF),
            jax.ShapeDtypeStruct((1, width // 64, 128), F32),
        ]
        + gradient_shapes(2 * q_width + 2 * HD),
        in_specs=[smem()] * 2 + [vmem()] * 15,
        out_specs=[vmem()] * 12,
        scratch_shapes=[
            pltpu.VMEM((every, every), F32),
            pltpu.VMEM((every, q_width), BF),
        ],
        compiler_params=params(12),
        name="attention_back",
        cost_estimate=cost(19),
    )(place_docs, place_xy, *mids, qkv, lse, h1, o, wq, wk.T, wv.T, wo, cos, sin, gain_two_part)
    return (*got[1:4], got[4:])


def lay_out_kernel(plan, keep, got, *outs):
    for out, parts in zip(outs, plan):
        for start, blocks, first, width, to in parts:
            for half in range(2):
                for b in range(blocks):
                    low, high = max(128 * b, first), min(128 * (b + 1), first + width)
                    if low >= high:
                        continue
                    at = start + half * blocks + b
                    total = keep[at] + got[at].astype(F32)
                    out[32 * half : 32 * (half + 1), to + low - first : to + high - first] = total[:, low - 128 * b : high - 128 * b]


def lay_out(keep, got, plan):
    widths = [sum(part[3] for part in parts) for parts in plan]
    return pl.pallas_call(
        functools.partial(lay_out_kernel, plan),
        out_shape=[jax.ShapeDtypeStruct((64, width), F32) for width in widths],
        in_specs=[vmem()] * 2,
        out_specs=[vmem()] * len(plan),
        compiler_params=params(12),
        name="lay_out",
        cost_estimate=cost(1),
    )(keep, got)


def rotary_tables(offset):
    half_size = HD // 2
    freqs = THETA ** (-(jnp.arange(half_size, dtype=F32) * 2.0 / HD))
    angles = offset.astype(F32)[:, None] * freqs[None, :]
    cosine, sine = jnp.cos(angles), jnp.sin(angles)
    return jnp.concatenate((cosine,) * 4, axis=1), jnp.concatenate((-sine, sine) * 2, axis=1)


def over_core(values):
    return lax.ppermute(values, "tensor", [(t, t ^ 1) for t in range(4)])


def over_z(values):
    return lax.ppermute(values, "tensor", [(t, t ^ 2) for t in range(4)])


def over_diagonal(values):
    return lax.ppermute(values, "tensor", [(t, t ^ 3) for t in range(4)])


def over_x(values, xor):
    return lax.ppermute(values, "dp", [(d, d ^ (xor * 8)) for d in range(32)])


def over_y(values, xor):
    return lax.ppermute(values, "dp", [(d, d ^ (xor * 2)) for d in range(32)])


def over_z_hi(values):
    return lax.ppermute(values, "dp", [(d, d ^ 1) for d in range(32)])


def after(value, *others):
    return lax.optimization_barrier((value, *others))[0] if others else value


def add(*terms):
    total = terms[0].astype(F32)
    for term in terms[1:]:
        total = total + term.astype(F32)
    return total


def norm(values):
    inverse = lax.rsqrt(jnp.mean(values * values, axis=-1, keepdims=True) + EPSILON)
    return values * inverse, inverse


def norm_back(normed, inverse, gain, grads):
    scaled = grads * gain
    return inverse * (scaled - normed * jnp.mean(scaled * normed, axis=-1, keepdims=True))


LINKS = ((over_x, 1), (over_x, 3), (over_y, 1), (over_y, 3))
ROUTES = ((0, 1, 2, 3), (1, 0, 3, 2), (2, 3, 0, 1), (3, 2, 1, 0))


class Reduction:
    def __init__(self, arrays, joined=False):
        self.joined = joined
        self.blocks = arrays[0].shape[2]
        self.sends = [arrays[2 * part].reshape(-1, 32, 128) for part in range(4)]
        self.kept = [[(arrays[2 * part + 1].reshape(-1, 32, 128), self.starts(0, 8))] for part in range(4)]
        self.near, self.far, self.last = {}, {}, {}

    def starts(self, at, rows):
        return {row: at + row * self.blocks for row in range(rows)}

    def route(self, part, step):
        return ROUTES[part - part % 2 if self.joined and step >= 2 else part][step]

    def order(self, part):
        return ((1, 3), (3, 1))[0 if self.joined else part % 2]

    def row(self, part, row, rows=1):
        return [(array, starts[row], rows * self.blocks) for array, starts in self.kept[part]]

    def sum(self, part, step):
        first, second = self.order(part)
        if step == 0:
            return [(self.sends[part], 0, 8 * self.blocks)]
        if step == 1:
            return self.row(part, 4, 4)
        if step == 2:
            return self.row(part, min(first, 2), 2)
        if step == 3:
            return self.row(part, second) + [self.far[part]]
        return self.row(part, 0) + self.near.get(part, []) + [self.last[part]]

    def take(self, part, step, got, at):
        n = self.blocks
        if step < 2:
            self.kept[part].append((got, self.starts(at, 8 - 4 * step)))
        elif step == 2:
            near, far = (0, 1) if self.order(part)[0] == 1 else (1, 0)
            self.near[part] = [(got, at + near * n, n)]
            self.far[part] = (got, at + far * n, n)
        else:
            self.last[part] = (got, at, n)


def fold(jobs, time=0.5):
    folded = []
    for part in range(4):
        sums, places = [], []
        at = 0
        for r, rows in jobs:
            rows = {"last": (0, r.order(part)[1]), "own": (0,)}.get(rows, rows)
            starts = {}
            for row in rows:
                terms = r.row(part, row)
                if row == 0:
                    terms = terms + r.near.get(part, [])
                sums.append(terms)
                starts[row] = at
                at += r.blocks
            r.near.pop(part, None)
            places.append((r, starts))
        array = combine(sums, time)
        folded.append(array)
        for r, starts in places:
            r.kept[part] = [(array, starts)]
    return folded


class Gains:
    def __init__(self, block):
        self.held = [(block, 0)]

    def terms(self):
        return [(array, start, 1) for array, start in self.held]

    def exchange(self, hop, before):
        sent = sum(array[start : start + 1].astype(F32) for array, start in self.held).astype(BF)
        self.held = [(sent, 0), (hop(after(sent, *before)), 0)]


def takers(jobs, link):
    return [(r, part, step) for r, step in jobs for part in range(4) if r.route(part, step) == link]


def prepare(jobs, gains=None, gains_link=None):
    operands = []
    for link in range(4):
        taken = takers(jobs, link)
        if not taken:
            operands.append(None)
            continue
        if len(taken) == 1 and taken[0][2] == 0:
            operands.append(taken[0][0].sends[taken[0][1]])
            continue
        sums = [r.sum(part, step) for r, part, step in taken]
        operands.append(combine(sums + ([gains.terms()] if link == gains_link else [])))
    return operands


def send(jobs, operands, before=None, anchor=(), gains=None, gains_link=None):
    arrived = []
    for link, (operand, (hop, xor)) in enumerate(zip(operands, LINKS)):
        if operand is None:
            arrived.append(before[link])
            continue
        got = hop(after(operand, *before[link]) if before else operand, xor)
        arrived.append((got,))
        got = after(got, *anchor)
        at = 0
        for r, part, step in takers(jobs, link):
            r.take(part, step, got, at)
            at += r.blocks * (8, 4, 2, 1)[step]
        if link == gains_link:
            gains.held = [(operand, at), (got, at)]
    return arrived


def stage(jobs, before=None, **more):
    return send(jobs, prepare(jobs, **more), before, **more)


def finish(reductions, place, plan, before=(), gains=None, anchor=None):
    keep, give = None, None
    give, keep = ends(
        place,
        [[r.sum(part, 4) for part in range(4)] for r in reductions],
        gains.terms() if gains else (),
    )
    got = over_z_hi(after(give, *before))
    if anchor is not None:
        got = after(got, anchor)
    outs = lay_out(keep, got, plan)
    if gains:
        total = add(keep[0], got[0])
        outs = (*outs, (total + over_core(total)) + (over_z(total) + over_diagonal(total)))
    return outs


def per_device(
    tokens,
    attn_gain,
    query_weight,
    key_weight,
    value_weight,
    out_weight,
    mlp_gain,
    gate_weight,
    up_weight,
    down_weight,
    cotangent,
    doc_lengths,
):
    rows = tokens.shape[0]
    place_dp = lax.axis_index("dp")
    place_t = lax.axis_index("tensor")
    place_xy = jnp.stack((place_dp // 8, (place_dp // 2) % 4, place_dp % 2))
    q_width = query_weight.shape[1]
    gain_one, gain_two = attn_gain.astype(F32), mlp_gain.astype(F32)

    across = over_z(tokens)
    places = jnp.concatenate(
        [(place_t ^ j) * rows + jnp.arange(rows, dtype=jnp.int32) for j in (0, 2, 1, 3)]
    )
    opening, ending = jnp.zeros_like(places), jnp.int32(0)
    for number in range(doc_lengths.shape[0]):
        ending = ending + doc_lengths[number]
        opening = jnp.maximum(opening, jnp.where(places >= ending, ending, 0))
    cos, sin = rotary_tables(places - opening)
    place_docs = jnp.concatenate((place_t[None], doc_lengths))
    attn_row, mlp_row = attn_gain.reshape(1, -1), mlp_gain.reshape(1, -1)
    near = touch(query_weight, out_weight)
    across, cos, sin, place_docs, place_xy, attn_row, mlp_row, near = lax.optimization_barrier(
        (across, cos, sin, place_docs, place_xy, attn_row, mlp_row, near)
    )
    token_blocks = (tokens, across, over_core(tokens), over_core(across))

    cot_across = over_z(after(cotangent, across))
    h1, qkv, heads_out, lse, high, low = attention(
        place_docs, token_blocks, attn_row, query_weight, key_weight, value_weight, out_weight, cos, sin, near
    )
    cot_pair = pair(cotangent, cot_across, low)
    chip, low = chip_sums(high, after(over_core(low), cot_pair))
    z_sums = over_z(low)
    cot_halves = (cot_pair, over_core(after(cot_pair, chip)))
    near = touch(after(gate_weight, cot_halves[1]), up_weight, down_weight)
    mid, h2 = middle(tokens, across, chip, after(z_sums, near), mlp_row)
    h2 = (h2, over_core(h2))
    units = gate_weight.shape[1]
    split = units // 2 // 128 * 128 + 128
    hidden, grad_gate_val, grad_up_val, first = mlp(
        place_xy, h2, gate_weight, up_weight, down_weight, cot_halves, near, split
    )
    first_sum = Reduction(first)
    first_links = stage([(first_sum, 0)])
    high, low, gain_two_part, second = mlp_back(
        place_xy, after(grad_gate_val, first[0]), grad_up_val, gate_weight, up_weight, h2, split
    )
    chip, low = chip_sums(high, after(over_core(low), *[link[0] for link in first_links]))
    second_sum = Reduction(second)
    links = stage([(second_sum, 0)], first_links)
    z_sums = after(over_z(low), *fold([(first_sum, range(8))]))
    grad_own, *mid_low = middle_back(mid, cot_pair, chip, z_sums, mlp_row, rows + rows // 2)
    mid_low = (*mid_low, over_core(mid_low[0]), over_core(mid_low[1]))

    jobs = [(first_sum, 1), (second_sum, 1)]
    operands = prepare(jobs)
    high, low, gains, attn = attention_back(
        place_docs, place_xy, mid_low, after(qkv, *operands), lse, h1, heads_out,
        query_weight, key_weight, value_weight, out_weight, cos, sin, gain_two_part,
    )
    links = send(jobs, operands, links, (low,))
    attn_sum = Reduction(attn, joined=True)
    gains = Gains(gains)
    own, other = chip_sums(high, after(over_core(low), *[link[0] for link in links]), False)
    jobs = [(first_sum, 2), (second_sum, 2), (attn_sum, 0)]
    operands = prepare(jobs, gains, 0)
    folded = fold([(first_sum, "last"), (second_sum, "last")])
    other = over_z(other)
    out_high, out_low = output(after(hidden, other), down_weight)
    links = send(jobs, operands, links, (*folded, out_low), gains, 0)
    grad_h1 = own + other.astype(F32)
    result_got = over_core(after(out_low, grad_h1))
    result_chip = add(out_high, result_got)
    result_z = over_z(result_chip[rows:].astype(BF))
    result = (mid[:rows] + result_chip[:rows] + result_z.astype(F32)).astype(BF)
    jobs = [(first_sum, 3), (second_sum, 3), (attn_sum, 1)]
    operands = prepare(jobs, gains, 1)
    folded = fold([(first_sum, "own"), (second_sum, "own"), (attn_sum, range(4))])
    links = send(jobs, operands, links, folded, gains, 1)
    blocks, more = first_sum.blocks, second_sum.blocks
    plan = [
        [(0, blocks, 0, units, 0)],
        [(0, blocks, units, split, 0), (2 * blocks, more, 0, units - split, split)],
        [(2 * blocks, more, units - split, units, 0)],
    ]
    out_down, out_gate, out_up = finish([first_sum, second_sum], place_xy, plan)
    links = stage([(attn_sum, 2)], links, gains=gains, gains_link=2)
    links = [(*link, result_z) for link in links]
    links = stage([(attn_sum, 3)], links, gains=gains, gains_link=3)
    cuts = ((0, q_width), (q_width, HD), (q_width + HD, HD), (q_width + 2 * HD, q_width))
    plan = [[(1, attn_sum.blocks, first, width, 0)] for first, width in cuts]
    out_query, out_key, out_value, out_out, grad_gains = finish([attn_sum], place_xy, plan, [], gains, out_up)
    grad_gains = grad_gains.reshape(2, -1)

    normed, inverse = norm(tokens.astype(F32))
    grad_tokens = grad_own + norm_back(normed, inverse, gain_one, grad_h1)
    return (
        result,
        grad_tokens.astype(BF),
        grad_gains[0] / gain_one,
        out_query,
        out_key,
        out_value,
        out_out.T,
        grad_gains[1] / gain_two,
        out_gate,
        out_up,
        out_down.T,
    )


def solution(mesh):
    in_specs = (
        P(("dp", "tensor"), None),
        P(),
        P(None, "tensor"),
        P(None, "tensor"),
        P(None, "tensor"),
        P("tensor", None),
        P(),
        P(None, "tensor"),
        P(None, "tensor"),
        P("tensor", None),
        P(("dp", "tensor"), None),
        P("dp"),
    )
    out_specs = (
        P(("dp", "tensor"), None),
        P(("dp", "tensor"), None),
        P(),
        P("dp", "tensor"),
        P("dp", "tensor"),
        P("dp", "tensor"),
        P("tensor", "dp"),
        P(),
        P("dp", "tensor"),
        P("dp", "tensor"),
        P("tensor", "dp"),
    )
    return jax.shard_map(
        per_device, mesh=mesh, in_specs=in_specs, out_specs=out_specs, check_vma=False
    )
```
